256 devices in a mesh: slab: 64 (over y_lo, z, x), freq: 4 (over y_hi, core).
Axes of the slice: x: 4, y: 4 (y_hi: 2, y_lo: 2; y = y_hi * 2 + y_lo), z: 8, core: 2. Of those that a mesh axis runs over, the one named last changes fastest.
Arguments:
- source_field: bfloat16 [2, 8, 2048, 16, 256], P(None, 'freq', 'slab'), may hold values from -6 to 6
- receiver_field: bfloat16 [2, 8, 2048, 16, 256], P(None, 'freq', 'slab'), may hold values from -6 to 6
Outputs:
- extended: float32 [16, 65, 2048, 256], P('freq', None, 'slab')
The draws below stay inside these ranges and needn't reach their ends.
All inputs are finite; a program needn't handle non-finite values.
Results may differ from the reference program's by a relative error of at most 0.0003.
Values may be sent and summed in bfloat16 or wider, within the bound.
No kernel may reach another device: no remote copies, remote signals or barrier semaphores. Data moves between devices by JAX's collectives and lax.ppermute only.
A program may use at most 128 MiB of HBM per device.

```python
import jax
import jax.numpy as jnp
from jax import lax

NF = 8
HMAX = 32
NY = 16
NZ = 256
H2 = 65
NX = 2048


def block_scale(rng, dims, pieces, smallest, high):
    gain, own = 1.0, jax.random.fold_in(rng, 6)
    for dim, parts in pieces:
        steps = jnp.exp(jax.random.uniform(jax.random.fold_in(own, dim), (parts,), jnp.float32, smallest / len(pieces), high / len(pieces)))
        gain = gain * jnp.repeat(steps, dims[dim] // parts).reshape([-1 if axis == dim else 1 for axis in range(len(dims))])
    return gain


def scatter_about(own_key, extent, width, limit, cuts=(), kind=jnp.bfloat16):
    result = jax.random.normal(own_key, extent, jnp.float32) * width
    if len(cuts) > 0:
        result = block_scale(own_key, extent, cuts, -0.22, 0.18) * result
    return jnp.clip(result, min=-limit, max=limit).astype(kind)


def setup_inputs(seed: int = 0) -> dict:
    key_of = jax.random.split(jax.random.key(seed), 3)
    source_field = scatter_about(key_of[0], (2, NF, NX, NY, NZ), 1.0, 6.0, ((1, 4), (2, 64)))
    receiver_field = scatter_about(key_of[1], (2, NF, NX, NY, NZ), 1.0, 6.0, ((1, 4), (2, 64)))
    return dict(source_field=source_field, receiver_field=receiver_field)


def reference(source_field, receiver_field):
    widths = ((0, 0), (0, 0), (HMAX, HMAX), (0, 0), (0, 0))
    source_padded = jnp.pad(source_field, widths)
    receiver_padded = jnp.pad(receiver_field, widths)

    def one_offset(offset_index):
        source_window = lax.dynamic_slice_in_dim(source_padded, (2 * HMAX - offset_index).astype(jnp.int32), NX, 2)
        receiver_window = lax.dynamic_slice_in_dim(receiver_padded, offset_index.astype(jnp.int32), NX, 2)
        return 0.25 * jnp.einsum("cfxyz,cfxyz->yxz", source_window.astype(jnp.float32), receiver_window.astype(jnp.float32))

    stacked = lax.map(one_offset, jnp.arange(H2, dtype=jnp.int32))
    return jnp.transpose(stacked, (1, 0, 2, 3))
```

```python
import functools

import jax
import jax.numpy as jnp
from jax import lax
from jax.experimental import pallas as pl
from jax.experimental.pallas import tpu as pltpu
from jax.sharding import PartitionSpec as P

HMAX = 32
GROUPS = 4
ROWS = 16
LANES = 128


def regroup_kernel(group_ref, source_ref, receiver_ref, *out_refs):
    freqs, cells = source_ref.shape[1], source_ref.shape[2]

    def regroup(order):
        for field, ref in enumerate((source_ref, receiver_ref)):
            for f in range(freqs):

                def one_cell(x, _):
                    halves = [
                        [ref[c, f, x, :, zh * LANES : (zh + 1) * LANES].astype(jnp.float32) for zh in range(2)]
                        for c in range(2)
                    ]
                    for d in range(GROUPS):
                        q = order ^ d
                        rows = [halves[c][zh][4 * q : 4 * q + 4] for c in range(2) for zh in range(2)]
                        out_refs[d][field, f, x] = jnp.concatenate(rows, axis=0).astype(jnp.bfloat16)
                    return 0

                lax.fori_loop(0, cells, one_cell, 0, unroll=4)

    for order in range(GROUPS):
        pl.when(group_ref[0] == order)(functools.partial(regroup, order))


def regrouped(group, source_field, receiver_field):
    two, freqs, cells, _, _ = source_field.shape
    steps = 4
    spec_in = pl.BlockSpec((2, freqs, cells // steps, 16, 256), lambda i: (0, 0, i, 0, 0))
    spec_out = pl.BlockSpec((2, freqs, cells // steps, ROWS, LANES), lambda i: (0, 0, i, 0, 0))
    return pl.pallas_call(
        regroup_kernel,
        grid=(steps,),
        in_specs=[pl.BlockSpec(memory_space=pltpu.SMEM), spec_in, spec_in],
        out_specs=[spec_out] * GROUPS,
        out_shape=[jax.ShapeDtypeStruct((2, freqs, cells, ROWS, LANES), jnp.bfloat16)] * GROUPS,
        cost_estimate=pl.CostEstimate(flops=0, bytes_accessed=4 << 20, transcendentals=0),
    )(group, source_field, receiver_field)


TX = 8
TH = 5


def image_kernel(edge_ref, *refs):
    blocks = refs[: 3 * GROUPS]
    out_ref = refs[3 * GROUPS]
    raw, fields, turn, stage, in_sems, out_sems = refs[3 * GROUPS + 1 :]
    cells = blocks[0].shape[2]
    freqs = blocks[0].shape[1]
    copies = []
    for d in range(GROUPS):
        for k in range(3):
            copies.append(
                pltpu.make_async_copy(
                    blocks[3 * d + k],
                    raw.at[:, pl.ds(freqs * d, freqs), pl.ds(cells * k, cells)],
                    in_sems.at[3 * d + k],
                )
            )
    for copy in copies:
        copy.start()
    for copy in copies:
        copy.wait()

    for side in range(2):

        @pl.when(edge_ref[side] == 0)
        def _():
            raw[:, :, pl.ds(2 * cells * side, cells)] = jnp.zeros(
                (2, freqs * GROUPS, cells, ROWS, LANES), jnp.bfloat16
            )

    def widen(p, _):
        for field in range(2):
            for f in range(freqs * GROUPS):
                fields[field, p, f] = raw[field, f, p].astype(jnp.float32)
        return 0

    lax.fori_loop(0, 3 * cells, widen, 0)

    def first_offset(step):
        return jnp.minimum(TH * step, 2 * HMAX + 1 - TH)

    steps = -(-(2 * HMAX + 1) // TH)

    def out_copy(step, slot):
        return pltpu.make_async_copy(stage.at[slot], out_ref.at[:, pl.ds(first_offset(step), TH)], out_sems.at[slot])

    def h_step(step, _):
        slot = lax.rem(step, 2)
        k0 = first_offset(step)

        @pl.when(step >= 2)
        def _():
            out_copy(step - 2, slot).wait()

        def x_step(xt, _):
            x0 = xt * TX
            s0 = x0 + 2 * HMAX - k0 - (TH - 1)
            r0 = x0 + k0
            total = [[None] * TX for _ in range(TH)]
            for f in range(freqs * GROUPS):
                for c in range(2):
                    s = [fields[0, s0 + i, f, 8 * c : 8 * c + 8] for i in range(TX + TH - 1)]
                    r = [fields[1, r0 + i, f, 8 * c : 8 * c + 8] for i in range(TX + TH - 1)]
                    for j in range(TH):
                        for i in range(TX):
                            product = s[i + TH - 1 - j] * r[i + j]
                            total[j][i] = product if total[j][i] is None else total[j][i] + product
            for j in range(TH):
                for i in range(TX):
                    turn[j, pl.ds(i, 8, stride=TX)] = 0.25 * total[j][i]
                for zh in range(2):
                    for y in range(4):
                        row = zh * 4 + y
                        stage[slot, y, j, pl.ds(pl.multiple_of(x0, TX), TX), zh * LANES : (zh + 1) * LANES] = turn[
                            j, row * TX : (row + 1) * TX
                        ]
            return 0

        lax.fori_loop(0, cells // TX, x_step, 0)
        out_copy(step, slot).start()
        return 0

    lax.fori_loop(0, steps, h_step, 0)
    for step in (steps - 2, steps - 1):
        out_copy(step, step % 2).wait()


def image(edge, blocks):
    two, freqs, cells, _, _ = blocks[0].shape
    total_freqs = freqs * GROUPS
    return pl.pallas_call(
        image_kernel,
        in_specs=[pl.BlockSpec(memory_space=pltpu.SMEM)] + [pl.BlockSpec(memory_space=pl.ANY)] * (3 * GROUPS),
        out_specs=pl.BlockSpec(memory_space=pl.ANY),
        out_shape=jax.ShapeDtypeStruct((4, 2 * HMAX + 1, cells, 256), jnp.float32),
        scratch_shapes=[
            pltpu.VMEM((2, total_freqs, 3 * cells, ROWS, LANES), jnp.bfloat16),
            pltpu.VMEM((2, 3 * cells, total_freqs, ROWS, LANES), jnp.float32),
            pltpu.VMEM((TH, 8 * TX, LANES), jnp.float32),
            pltpu.VMEM((2, 4, TH, cells, 256), jnp.float32),
            pltpu.SemaphoreType.DMA((3 * GROUPS,)),
            pltpu.SemaphoreType.DMA((2,)),
        ],
        compiler_params=pltpu.CompilerParams(vmem_limit_bytes=40 << 20),
        cost_estimate=pl.CostEstimate(flops=70_000_000, bytes_accessed=15 << 20, transcendentals=0),
    )(edge, *blocks)


def body(source_field, receiver_field):
    slabs = lax.axis_size("slab")
    forward = [(i, (i + 1) % slabs) for i in range(slabs)]
    backward = [(target, source) for source, target in forward]
    group = lax.axis_index("freq").astype(jnp.int32)
    slab = lax.axis_index("slab")
    edge = jnp.stack([slab > 0, slab < slabs - 1]).astype(jnp.int32)
    parts = regrouped(group[None], source_field, receiver_field)
    blocks = []
    for d in range(GROUPS):
        own = parts[d]
        if d:
            own = lax.ppermute(own, "freq", [(g, g ^ d) for g in range(GROUPS)])
        blocks += [lax.ppermute(own, "slab", forward), own, lax.ppermute(own, "slab", backward)]
    return image(edge, blocks)


def solution(mesh):
    in_specs = (P(None, "freq", "slab", None, None), P(None, "freq", "slab", None, None))
    out_specs = P("freq", None, "slab", None)
    return jax.shard_map(body, mesh=mesh, in_specs=in_specs, out_specs=out_specs, check_vma=False)
```

```python
import functools

import jax
import jax.numpy as jnp
from jax import lax
from jax.experimental import pallas as pl
from jax.experimental.pallas import tpu as pltpu
from jax.sharding import PartitionSpec as P

HMAX = 32
OFFSETS = 2 * HMAX + 1
GROUPS = 4
ROWS = 16
LANES = 128
TX = 8
TH = 5


def regroup_kernel(group_ref, source_ref, receiver_ref, *out_refs):
    freqs, cells = source_ref.shape[1], source_ref.shape[2]

    def regroup(order):
        for field, ref in enumerate((source_ref, receiver_ref)):
            for f in range(freqs):

                def one_cell(x, _):
                    low = lax.broadcasted_iota(jnp.int32, (8, LANES), 0) < 4
                    parts = [[None, None] for _ in range(GROUPS)]
                    for c in range(2):
                        near = ref[c, f, x, :, :LANES].astype(jnp.float32)
                        far = ref[c, f, x, :, LANES:].astype(jnp.float32)
                        for pair in range(2):
                            a = near[8 * pair : 8 * pair + 8]
                            b = far[8 * pair : 8 * pair + 8]
                            parts[2 * pair][c] = jnp.where(low, a, pltpu.roll(b, 4, 0))
                            parts[2 * pair + 1][c] = jnp.where(low, pltpu.roll(a, 4, 0), b)
                    for d in range(GROUPS):
                        out_refs[d][field, f, x] = jnp.concatenate(parts[order ^ d], axis=0).astype(jnp.bfloat16)
                    return 0

                lax.fori_loop(0, cells, one_cell, 0, unroll=4)

    for order in range(GROUPS):
        pl.when(group_ref[0] == order)(functools.partial(regroup, order))


def regrouped(group, source_field, receiver_field):
    two, freqs, cells, _, _ = source_field.shape
    steps = 4
    spec_in = pl.BlockSpec((2, freqs, cells // steps, 16, 256), lambda i: (0, 0, i, 0, 0))
    spec_out = pl.BlockSpec((2, freqs, cells // steps, ROWS, LANES), lambda i: (0, 0, i, 0, 0))
    return pl.pallas_call(
        regroup_kernel,
        grid=(steps,),
        in_specs=[pl.BlockSpec(memory_space=pltpu.SMEM), spec_in, spec_in],
        out_specs=[spec_out] * GROUPS,
        out_shape=[jax.ShapeDtypeStruct((2, freqs, cells, ROWS, LANES), jnp.bfloat16)] * GROUPS,
        cost_estimate=pl.CostEstimate(flops=0, bytes_accessed=4 << 20, transcendentals=0),
    )(group, source_field, receiver_field)


def image_kernel(first, last, groups, *refs):
    blocks = refs[: 3 * groups]
    refs = refs[3 * groups :]
    if not first:
        partial_ref, refs = refs[0], refs[1:]
    out_ref, refs = refs[0], refs[1:]
    raw, fields, stage, in_sems, out_sems = refs[:5]
    refs = refs[5:]
    if last:
        turn, refs = refs[0], refs[1:]
    if not first:
        before, before_sems = refs
    freqs, cells = blocks[0].shape[1], blocks[0].shape[2]
    total_freqs = freqs * groups
    steps = OFFSETS // TH

    def before_copy(step, slot):
        return pltpu.make_async_copy(partial_ref.at[pl.ds(TH * step, TH)], before.at[slot], before_sems.at[slot])

    def out_copy(step, slot):
        if last:
            return pltpu.make_async_copy(stage.at[slot], out_ref.at[:, pl.ds(TH * step, TH)], out_sems.at[slot])
        return pltpu.make_async_copy(stage.at[slot], out_ref.at[pl.ds(TH * step, TH)], out_sems.at[slot])

    copies = []
    for d in range(groups):
        for k in range(3):
            copies.append(
                pltpu.make_async_copy(
                    blocks[3 * d + k],
                    raw.at[:, pl.ds(freqs * d, freqs), pl.ds(cells * k, cells)],
                    in_sems.at[3 * d + k],
                )
            )
    for copy in copies:
        copy.start()
    if not first:
        before_copy(0, 0).start()
    for copy in copies:
        copy.wait()

    def widen(p, _):
        for field in range(2):
            for f in range(total_freqs):
                fields[field, p, f] = raw[field, f, p].astype(jnp.float32)
        return 0

    lax.fori_loop(0, 3 * cells, widen, 0)

    def h_step(step, _):
        slot = lax.rem(step, 2)
        k0 = TH * step

        if not first:

            @pl.when(step + 1 < steps)
            def _():
                before_copy(step + 1, 1 - slot).start()

            before_copy(step, slot).wait()

        @pl.when(step >= 2)
        def _():
            out_copy(step - 2, slot).wait()

        def x_step(xt, _):
            x0 = xt * TX
            s0 = x0 + 2 * HMAX - k0 - (TH - 1)
            r0 = x0 + k0
            total = [[None] * TX for _ in range(TH)]
            if not first:
                total = [[before[slot, j, x0 + i] for i in range(TX)] for j in range(TH)]
            for f in range(total_freqs):
                for c in range(2):
                    s = [fields[0, s0 + i, f, 8 * c : 8 * c + 8] for i in range(TX + TH - 1)]
                    r = [fields[1, r0 + i, f, 8 * c : 8 * c + 8] for i in range(TX + TH - 1)]
                    for j in range(TH):
                        for i in range(TX):
                            product = s[i + TH - 1 - j] * r[i + j]
                            total[j][i] = product if total[j][i] is None else total[j][i] + product
            for j in range(TH):
                if not last:
                    for i in range(TX):
                        stage[slot, j, x0 + i] = total[j][i]
                    continue
                for i in range(TX):
                    turn[j, pl.ds(i, 8, stride=TX)] = 0.25 * total[j][i]
                for zh in range(2):
                    for y in range(4):
                        row = zh * 4 + y
                        stage[slot, y, j, pl.ds(pl.multiple_of(x0, TX), TX), zh * LANES : (zh + 1) * LANES] = turn[
                            j, row * TX : (row + 1) * TX
                        ]
            return 0

        lax.fori_loop(0, cells // TX, x_step, 0)
        out_copy(step, slot).start()
        return 0

    lax.fori_loop(0, steps, h_step, 0)
    for step in (steps - 2, steps - 1):
        out_copy(step, step % 2).wait()


def image(blocks, before, last):
    two, freqs, cells, _, _ = blocks[0].shape
    groups = len(blocks) // 3
    total_freqs = freqs * groups
    first = before is None
    stage_shape = (2, 4, TH, cells, 2 * LANES) if last else (2, TH, cells, 8, LANES)
    out_shape = (4, OFFSETS, cells, 2 * LANES) if last else (OFFSETS, cells, 8, LANES)
    scratch = [
        pltpu.VMEM((2, total_freqs, 3 * cells, ROWS, LANES), jnp.bfloat16),
        pltpu.VMEM((2, 3 * cells, total_freqs, ROWS, LANES), jnp.float32),
        pltpu.VMEM(stage_shape, jnp.float32),
        pltpu.SemaphoreType.DMA((3 * groups,)),
        pltpu.SemaphoreType.DMA((2,)),
    ]
    if last:
        scratch.append(pltpu.VMEM((TH, 8 * TX, LANES), jnp.float32))
    if not first:
        scratch += [pltpu.VMEM((2, TH, cells, 8, LANES), jnp.float32), pltpu.SemaphoreType.DMA((2,))]
    operands = list(blocks) + ([] if first else [before])
    return pl.pallas_call(
        functools.partial(image_kernel, first, last, groups),
        in_specs=[pl.BlockSpec(memory_space=pl.ANY)] * len(operands),
        out_specs=pl.BlockSpec(memory_space=pl.ANY),
        out_shape=jax.ShapeDtypeStruct(out_shape, jnp.float32),
        scratch_shapes=scratch,
        compiler_params=pltpu.CompilerParams(vmem_limit_bytes=60 << 20),
        cost_estimate=pl.CostEstimate(flops=17_000_000 * groups, bytes_accessed=15 << 20, transcendentals=0),
    )(*operands)


def body(source_field, receiver_field):
    slabs = lax.axis_size("slab")
    middle = slabs // 2
    group = lax.axis_index("freq").astype(jnp.int32)
    slab = lax.axis_index("slab")
    parts = list(regrouped(group[None], source_field, receiver_field))
    owned = [parts[0]] + [
        lax.ppermute(parts[d], "freq", [(g, g ^ d) for g in range(GROUPS)]) for d in range(1, GROUPS)
    ]

    def rim(d, step):
        sender = middle - 1 if step > 0 else middle
        direct = d >= 2
        pairs = []
        for s in range(slabs):
            if 0 <= s + step < slabs:
                for g in range(GROUPS):
                    to = g ^ d if direct and s == sender else g
                    pairs.append((s * GROUPS + g, (s + step) * GROUPS + to))
        value = jnp.where(slab == sender, parts[d], owned[d]) if direct else owned[d]
        return lax.ppermute(value, ("slab", "freq"), pairs)

    blocks = []
    for d in range(GROUPS):
        if d >= 2:
            ahead = blocks[d - 2]
            owned[d], parts[d], ahead[0], ahead[2] = lax.optimization_barrier(
                (owned[d], parts[d], ahead[0], ahead[2])
            )
        blocks.append([rim(d, 1), owned[d], rim(d, -1)])
    total = image(blocks[0] + blocks[1], None, False)
    total = image(blocks[2], total, False)
    return image(blocks[3], total, True)


def solution(mesh):
    in_specs = (P(None, "freq", "slab", None, None), P(None, "freq", "slab", None, None))
    out_specs = P("freq", None, "slab", None)
    return jax.shard_map(body, mesh=mesh, in_specs=in_specs, out_specs=out_specs, check_vma=False)
```

```python
import functools

import jax
import jax.numpy as jnp
from jax import lax
from jax.experimental import pallas as pl
from jax.experimental.pallas import tpu as pltpu
from jax.sharding import PartitionSpec as P

HMAX = 32
OFFSETS = 2 * HMAX + 1
GROUPS = 4
ROWS = 16
LANES = 128
TX = 8
TH = 4
SLOTS = 4
CHUNKS = 4
RLIM, SLIM, LLIM = 62, 40, 40


def regroup_kernel(group_ref, source_ref, receiver_ref, *refs):
    out_refs, (held, sems) = refs[:GROUPS], refs[GROUPS:]
    freqs, cells = source_ref.shape[1], source_ref.shape[2]
    share = cells // CHUNKS

    def fetch(field, chunk):
        ref = (source_ref, receiver_ref)[field]
        part = pl.ds(chunk * share, share)
        return pltpu.make_async_copy(ref.at[:, :, part], held.at[field, :, :, part], sems.at[field, chunk])

    for chunk in range(CHUNKS):
        for field in range(2):
            fetch(field, chunk).start()

    def regroup(order):
        low = lax.broadcasted_iota(jnp.int32, (8, LANES), 0) < 4
        for chunk in range(CHUNKS):
            for field in range(2):
                fetch(field, chunk).wait()

                def one_cell(x, _):
                    for f in range(freqs):
                        parts = [[None, None] for _ in range(GROUPS)]
                        for c in range(2):
                            near = held[field, c, f, x, :, :LANES].astype(jnp.float32)
                            far = held[field, c, f, x, :, LANES:].astype(jnp.float32)
                            for pair in range(2):
                                a = near[8 * pair : 8 * pair + 8]
                                b = far[8 * pair : 8 * pair + 8]
                                parts[2 * pair][c] = jnp.where(low, a, pltpu.roll(b, 4, 0))
                                parts[2 * pair + 1][c] = jnp.where(low, pltpu.roll(a, 4, 0), b)
                        for d in range(GROUPS):
                            out_refs[d][field, f, x] = jnp.concatenate(parts[order ^ d], axis=0).astype(jnp.bfloat16)
                    return 0

                lax.fori_loop(chunk * share, (chunk + 1) * share, one_cell, 0, unroll=2)

    for order in range(GROUPS):
        pl.when(group_ref[0] == order)(functools.partial(regroup, order))


def regrouped(group, source_field, receiver_field):
    two, freqs, cells, _, _ = source_field.shape
    return pl.pallas_call(
        regroup_kernel,
        in_specs=[pl.BlockSpec(memory_space=pltpu.SMEM)] + [pl.BlockSpec(memory_space=pltpu.HBM)] * 2,
        out_specs=[pl.BlockSpec(memory_space=pltpu.VMEM)] * GROUPS,
        out_shape=[jax.ShapeDtypeStruct((2, freqs, cells, ROWS, LANES), jnp.bfloat16)] * GROUPS,
        scratch_shapes=[pltpu.VMEM((2, 2, freqs, cells, 16, 2 * LANES), jnp.bfloat16), pltpu.SemaphoreType.DMA((2, CHUNKS))],
        compiler_params=pltpu.CompilerParams(vmem_limit_bytes=RLIM << 20),
        cost_estimate=pl.CostEstimate(flops=0, bytes_accessed=4 << 20, transcendentals=0),
        name="regroup",
    )(group, source_field, receiver_field)


def image_kernel(first, last, counts, side_ref, *refs):
    groups = len(counts)
    blocks = refs[: sum(counts)]
    refs = refs[sum(counts) :]
    if not first:
        before, refs = refs[0], refs[1:]
    out_ref, fields, raw, raw_sems = refs[:4]
    if last:
        turn, stage, sems = refs[4:]
    freqs, cells = blocks[0].shape[1], blocks[0].shape[2]
    total_freqs = freqs * groups

    def fetch(index):
        return pltpu.make_async_copy(blocks[index], raw.at[index], raw_sems.at[index])

    for index in range(sum(counts)):
        fetch(index).start()

    def widen(index, group, part):
        def one_cell(x, _):
            for field in range(2):
                for f in range(freqs):
                    fields[field, cells * part + x, freqs * group + f] = raw[index, field, f, x].astype(jnp.float32)
            return 0

        lax.fori_loop(0, cells, one_cell, 0, unroll=4)

    at = 0
    for group, count in enumerate(counts):
        for index in range(at, at + count):
            fetch(index).wait()
        left, own, right = at, at + 1, at + 2
        widen(own, group, 1)
        if count == 4:
            across = at + 3
            pl.when(side_ref[0] == 1)(functools.partial(widen, across, group, 0))
            pl.when(side_ref[0] == 0)(functools.partial(widen, left, group, 0))
            pl.when(side_ref[1] == 1)(functools.partial(widen, across, group, 2))
            pl.when(side_ref[1] == 0)(functools.partial(widen, right, group, 2))
        else:
            widen(left, group, 0)
            widen(right, group, 2)
        at += count

    def out_copy(k0, rows, slot):
        return pltpu.make_async_copy(stage.at[slot, :, pl.ds(0, rows)], out_ref.at[:, pl.ds(k0, rows)], sems.at[slot])

    def tile(k0, rows, x0, slot):
        s0 = x0 + 2 * HMAX - k0 - (rows - 1)
        r0 = x0 + k0
        if first:
            total = [[None] * TX for _ in range(rows)]
        else:
            total = [[before[k0 + j, x0 + i] for i in range(TX)] for j in range(rows)]
        for f in range(total_freqs):
            for c in range(2):
                s = [fields[0, s0 + i, f, 8 * c : 8 * c + 8] for i in range(TX + rows - 1)]
                r = [fields[1, r0 + i, f, 8 * c : 8 * c + 8] for i in range(TX + rows - 1)]
                for j in range(rows):
                    for i in range(TX):
                        product = s[i + rows - 1 - j] * r[i + j]
                        total[j][i] = product if total[j][i] is None else total[j][i] + product
        for j in range(rows):
            if not last:
                for i in range(TX):
                    out_ref[k0 + j, x0 + i] = total[j][i]
                continue
            for i in range(TX):
                turn[j, pl.ds(i, 8, stride=TX)] = 0.25 * total[j][i]
            for zh in range(2):
                for y in range(4):
                    row = zh * 4 + y
                    stage[slot, y, j, pl.ds(pl.multiple_of(x0, TX), TX), zh * LANES : (zh + 1) * LANES] = turn[
                        j, row * TX : (row + 1) * TX
                    ]

    def band(k0, rows, slot):
        def x_step(xt, _):
            tile(k0, rows, xt * TX, slot)
            return 0

        lax.fori_loop(0, cells // TX, x_step, 0)

    steps = OFFSETS // TH

    def h_step(step, _):
        slot = lax.rem(step, SLOTS)
        if last:

            @pl.when(step >= SLOTS)
            def _():
                out_copy(TH * (step - SLOTS), TH, slot).wait()

        band(TH * step, TH, slot)
        if last:
            out_copy(TH * step, TH, slot).start()
        return 0

    lax.fori_loop(0, steps, h_step, 0)
    rest = OFFSETS - TH * steps
    if last:
        out_copy(TH * (steps - SLOTS), TH, steps % SLOTS).wait()
    band(TH * steps, rest, steps % SLOTS)
    if last:
        out_copy(TH * steps, rest, steps % SLOTS).start()
        for step in range(steps - SLOTS + 1, steps):
            out_copy(TH * step, TH, step % SLOTS).wait()
        out_copy(TH * steps, rest, steps % SLOTS).wait()


def image(side, blocks, before, last):
    two, freqs, cells, _, _ = blocks[0][0].shape
    counts = tuple(len(group) for group in blocks)
    first = before is None
    out_shape = (4, OFFSETS, cells, 2 * LANES) if last else (OFFSETS, cells, 8, LANES)
    scratch = [
        pltpu.VMEM((2, 3 * cells, freqs * len(blocks), ROWS, LANES), jnp.float32),
        pltpu.VMEM((sum(counts), 2, freqs, cells, ROWS, LANES), jnp.bfloat16),
        pltpu.SemaphoreType.DMA((sum(counts),)),
    ]
    if last:
        scratch += [
            pltpu.VMEM((TH, 8 * TX, LANES), jnp.float32),
            pltpu.VMEM((SLOTS, 4, TH, cells, 2 * LANES), jnp.float32),
            pltpu.SemaphoreType.DMA((SLOTS,)),
        ]
    operands = [block for group in blocks for block in group] + ([] if first else [before])
    vmem = pl.BlockSpec(memory_space=pltpu.VMEM)
    hbm = pl.BlockSpec(memory_space=pltpu.HBM)
    return pl.pallas_call(
        functools.partial(image_kernel, first, last, counts),
        in_specs=[pl.BlockSpec(memory_space=pltpu.SMEM)] + [hbm] * sum(counts) + ([] if first else [vmem]),
        out_specs=hbm if last else vmem,
        out_shape=jax.ShapeDtypeStruct(out_shape, jnp.float32),
        scratch_shapes=scratch,
        input_output_aliases={} if first or last else {len(operands): 0},
        compiler_params=pltpu.CompilerParams(vmem_limit_bytes=(LLIM if last else SLIM) << 20),
        cost_estimate=pl.CostEstimate(flops=17_000_000 * len(blocks), bytes_accessed=9 << 20, transcendentals=0),
        name="image_last" if last else "image_sum",
    )(side, *operands)


def body(source_field, receiver_field):
    slabs = lax.axis_size("slab")
    middle = slabs // 2
    group = lax.axis_index("freq").astype(jnp.int32)
    slab = lax.axis_index("slab")
    side = jnp.stack([slab == middle, slab == middle - 1]).astype(jnp.int32)
    parts = list(regrouped(group[None], source_field, receiver_field))
    owned = [parts[0]] + [
        lax.ppermute(parts[d], "freq", [(g, g ^ d) for g in range(GROUPS)]) for d in range(1, GROUPS)
    ]

    def rim(d, step):
        cut = middle - 1 if step > 0 else middle
        pairs = [(s, s + step) for s in range(slabs) if 0 <= s + step < slabs and (d == 0 or s != cut)]
        return lax.ppermute(owned[d], "slab", pairs)

    def across(d):
        value, turn = (parts[d], d) if d >= 2 else (owned[d], 0)
        pairs = []
        for g in range(GROUPS):
            pairs.append(((middle - 1) * GROUPS + g, middle * GROUPS + (g ^ turn)))
            pairs.append((middle * GROUPS + g, (middle - 1) * GROUPS + (g ^ turn)))
        return lax.ppermute(value, ("slab", "freq"), pairs)

    blocks = []
    for d in range(GROUPS):
        if d >= 2:
            ahead = blocks[d - 2]
            owned[d], ahead[0], ahead[2] = lax.optimization_barrier((owned[d], ahead[0], ahead[2]))
        blocks.append([rim(d, 1), owned[d], rim(d, -1)])
        if d:
            blocks[d].append(across(d))
    total = image(side, blocks[:3], None, False)
    return image(side, blocks[3:], total, True)


def solution(mesh):
    in_specs = (P(None, "freq", "slab", None, None), P(None, "freq", "slab", None, None))
    out_specs = P("freq", None, "slab", None)
    return jax.shard_map(body, mesh=mesh, in_specs=in_specs, out_specs=out_specs, check_vma=False)
```

```python
import functools

import jax
import jax.numpy as jnp
from jax import lax
from jax.experimental import pallas as pl
from jax.experimental.pallas import tpu as pltpu
from jax.sharding import PartitionSpec as P

HMAX = 32
OFFSETS = 2 * HMAX + 1
GROUPS = 4
ROWS = 16
LANES = 128
TX = 8
TH = 4
SLOTS = 4
CHUNKS = 4
NEAR = HMAX // 2


def regroup_kernel(group_ref, source_ref, receiver_ref, *refs):
    out_refs, (held, sems) = refs[:GROUPS], refs[GROUPS:]
    freqs, cells = source_ref.shape[1], source_ref.shape[2]
    share = cells // CHUNKS

    def fetch(field, chunk):
        ref = (source_ref, receiver_ref)[field]
        part = pl.ds(chunk * share, share)
        return pltpu.make_async_copy(ref.at[:, :, part], held.at[field, :, :, part], sems.at[field, chunk])

    for chunk in range(CHUNKS):
        for field in range(2):
            fetch(field, chunk).start()

    def regroup(order):
        low = lax.broadcasted_iota(jnp.int32, (8, LANES), 0) < 4
        for chunk in range(CHUNKS):
            for field in range(2):
                fetch(field, chunk).wait()

                def one_cell(x, _):
                    for f in range(freqs):
                        parts = [[None, None] for _ in range(GROUPS)]
                        for c in range(2):
                            near = held[field, c, f, x, :, :LANES].astype(jnp.float32)
                            far = held[field, c, f, x, :, LANES:].astype(jnp.float32)
                            for pair in range(2):
                                a = near[8 * pair : 8 * pair + 8]
                                b = far[8 * pair : 8 * pair + 8]
                                parts[2 * pair][c] = jnp.where(low, a, pltpu.roll(b, 4, 0))
                                parts[2 * pair + 1][c] = jnp.where(low, pltpu.roll(a, 4, 0), b)
                        for d in range(GROUPS):
                            out_refs[d][field, f, x] = jnp.concatenate(parts[order ^ d], axis=0).astype(jnp.bfloat16)
                    return 0

                lax.fori_loop(chunk * share, (chunk + 1) * share, one_cell, 0, unroll=2)

    for order in range(GROUPS):
        pl.when(group_ref[0] == order)(functools.partial(regroup, order))


def regrouped(group, source_field, receiver_field):
    two, freqs, cells, _, _ = source_field.shape
    return pl.pallas_call(
        regroup_kernel,
        in_specs=[pl.BlockSpec(memory_space=pltpu.SMEM)] + [pl.BlockSpec(memory_space=pl.ANY)] * 2,
        out_specs=[pl.BlockSpec(memory_space=pltpu.VMEM)] * GROUPS,
        out_shape=[pltpu.VMEM((2, freqs, cells, ROWS, LANES), jnp.bfloat16)] * GROUPS,
        scratch_shapes=[pltpu.VMEM((2, 2, freqs, cells, 16, 2 * LANES), jnp.bfloat16), pltpu.SemaphoreType.DMA((2, CHUNKS))],
        compiler_params=pltpu.CompilerParams(vmem_limit_bytes=12 << 20),
        cost_estimate=pl.CostEstimate(flops=0, bytes_accessed=4 << 20, transcendentals=0),
        name="regroup",
    )(group, *(pltpu.with_memory_space_constraint(x, pltpu.HBM) for x in (source_field, receiver_field)))


def pack_kernel(copies, refs_in, *refs):
    flags_ref, ins, outs = refs[0], refs[1 : 1 + refs_in], refs[1 + refs_in :]
    for flag, value, source, part, half, out, slot in copies:

        def copy(source=source, part=part, half=half, out=out, slot=slot):
            cells = outs[out].shape[3]

            def one_cell(x, _):
                for field in range(2):
                    for f in range(outs[out].shape[2]):
                        at = (field, f, half * cells + x) if part is None else (part, field, f, half * cells + x)
                        outs[out][slot, field, f, x] = ins[source][at]
                return 0

            lax.fori_loop(0, cells, one_cell, 0, unroll=4)

        if flag is None:
            copy()
        else:
            pl.when(flags_ref[flag] == value)(copy)


def pack(flags, arrays, copies, shapes):
    vmem = pl.BlockSpec(memory_space=pltpu.VMEM)
    return pl.pallas_call(
        functools.partial(pack_kernel, copies, len(arrays)),
        in_specs=[pl.BlockSpec(memory_space=pltpu.SMEM)] + [vmem] * len(arrays),
        out_specs=[vmem] * len(shapes),
        out_shape=[jax.ShapeDtypeStruct(shape, jnp.bfloat16) for shape in shapes],
        compiler_params=pltpu.CompilerParams(vmem_limit_bytes=12 << 20),
        cost_estimate=pl.CostEstimate(flops=0, bytes_accessed=2 << 20, transcendentals=0),
        name="pack",
    )(flags, *arrays)


def sum_kernel(plan, bands, first, last, flags_ref, *refs):
    count = 1 + max(entry[0] for entry in plan)
    blocks, refs = refs[:count], refs[count:]
    befores = ()
    if not first:
        befores, refs = refs[: len(bands)], refs[len(bands) :]
    if last == 2:
        refs = refs[1:]
    outs = refs[: 1 if last else len(bands)]
    fields = refs[len(outs)]
    if last:
        turn, stage, sems = refs[len(outs) + 1 :]
        out_ref = outs[0]
    cells = stage.shape[4 - 1] if last else outs[0].shape[1]
    total_freqs = fields.shape[2]

    def fill(index, part, at, length, to, group):
        def one_cell(x, _):
            for field in range(2):
                for f in range(2):
                    if index is None:
                        value = jnp.zeros((ROWS, LANES), jnp.float32)
                    elif part is None:
                        value = blocks[index][field, f, at + x].astype(jnp.float32)
                    else:
                        value = blocks[index][part, field, f, at + x].astype(jnp.float32)
                    fields[field, to + x, 2 * group + f] = value
            return 0

        lax.fori_loop(0, length, one_cell, 0, unroll=4)

    for index, part, length, to, group, flag, value in plan:
        place = functools.partial(fill, index, part, 0, length, to, group)
        if flag is None:
            place()
        else:
            pl.when(flags_ref[flag] == value)(place)
    for length, to, flag, value in sorted({(e[2], e[3], e[5], 2) for e in plan if e[5] is not None}):
        for group in range(total_freqs // 2):
            pl.when(flags_ref[flag] == value)(functools.partial(fill, None, None, 0, length, to, group))

    def tile(before, out, k0, row0, rows, x0, slot):
        s0 = x0 + 2 * HMAX - k0 - (rows - 1)
        r0 = x0 + k0
        if first:
            total = [[None] * TX for _ in range(rows)]
        else:
            total = [[before[row0 + j, x0 + i] for i in range(TX)] for j in range(rows)]
        for f in range(total_freqs):
            for c in range(2):
                s = [fields[0, s0 + i, f, 8 * c : 8 * c + 8] for i in range(TX + rows - 1)]
                r = [fields[1, r0 + i, f, 8 * c : 8 * c + 8] for i in range(TX + rows - 1)]
                for j in range(rows):
                    for i in range(TX):
                        product = s[i + rows - 1 - j] * r[i + j]
                        total[j][i] = product if total[j][i] is None else total[j][i] + product
        for j in range(rows):
            if not last:
                for i in range(TX):
                    out[row0 + j, x0 + i] = total[j][i]
                continue
            for i in range(TX):
                turn[j, pl.ds(i, 8, stride=TX)] = 0.25 * total[j][i]
            for zh in range(2):
                for y in range(4):
                    row = zh * 4 + y
                    stage[slot, y, j, pl.ds(pl.multiple_of(x0, TX), TX), zh * LANES : (zh + 1) * LANES] = turn[
                        j, row * TX : (row + 1) * TX
                    ]

    def out_copy(k0, rows, slot):
        return pltpu.make_async_copy(stage.at[slot, :, pl.ds(0, rows)], out_ref.at[:, pl.ds(k0, rows)], sems.at[slot])

    for band, (k_first, steps, jump_at, jump, rest) in enumerate(bands):
        before = befores[band] if befores else None
        out = None if last else outs[band]

        def first_row(step):
            k0 = k_first + TH * step
            return k0 if not jump else k0 + jnp.where(step >= jump_at, jump, 0)

        def rows_of(k0, row0, rows, slot):
            def x_step(xt, _):
                tile(before, out, k0, row0, rows, xt * TX, slot)
                return 0

            lax.fori_loop(0, cells // TX, x_step, 0)

        def h_step(step, _):
            slot = lax.rem(step, SLOTS)
            if last:

                @pl.when(step >= SLOTS)
                def _():
                    out_copy(first_row(step - SLOTS), TH, slot).wait()

            rows_of(first_row(step), TH * step, TH, slot)
            if last:
                out_copy(first_row(step), TH, slot).start()
            return 0

        lax.fori_loop(0, steps, h_step, 0)
        if rest:
            slot = steps % SLOTS
            k0 = k_first + TH * steps
            if last:
                out_copy(first_row(steps - SLOTS), TH, slot).wait()
            rows_of(k0, TH * steps, rest, slot)
            if last:
                out_copy(k0, rest, slot).start()
        if last:
            for step in range(steps - SLOTS + (1 if rest else 0), steps):
                out_copy(first_row(step), TH, step % SLOTS).wait()
            if rest:
                out_copy(k_first + TH * steps, rest, steps % SLOTS).wait()


NEAR_BAND = (HMAX - NEAR, 2 * NEAR // TH, 0, 0, 1)
FAR_BAND = (0, 2 * NEAR // TH, NEAR // TH, 2 * NEAR + 1, 0)


def summed(flags, blocks, plan, bands, befores, cells, groups, last, image=None):
    first = befores is None
    heights = [TH * band[1] + band[4] for band in bands]
    scratch = [pltpu.VMEM((2, 3 * cells, 2 * groups, ROWS, LANES), jnp.float32)]
    vmem = pl.BlockSpec(memory_space=pltpu.VMEM)
    hbm = pl.BlockSpec(memory_space=pl.ANY)
    operands = list(blocks) + ([] if first else list(befores))
    in_specs = [pl.BlockSpec(memory_space=pltpu.SMEM)] + [vmem] * len(operands)
    aliases = {}
    if last:
        scratch += [
            pltpu.VMEM((TH, 8 * TX, LANES), jnp.float32),
            pltpu.VMEM((SLOTS, 4, TH, cells, 2 * LANES), jnp.float32),
            pltpu.SemaphoreType.DMA((SLOTS,)),
        ]
        out_shape = jax.ShapeDtypeStruct((4, OFFSETS, cells, 2 * LANES), jnp.float32)
        out_specs = hbm
        if last == 2:
            operands.append(image)
            in_specs.append(hbm)
            aliases = {len(operands): 0}
    else:
        out_shape = [pltpu.VMEM((height, cells, 8, LANES), jnp.float32) for height in heights]
        out_specs = [vmem] * len(heights)
    return pl.pallas_call(
        functools.partial(sum_kernel, plan, bands, first, last),
        in_specs=in_specs,
        out_specs=out_specs,
        out_shape=out_shape,
        scratch_shapes=scratch,
        input_output_aliases=aliases,
        compiler_params=pltpu.CompilerParams(vmem_limit_bytes=24 << 20),
        cost_estimate=pl.CostEstimate(
            flops=260_000 * groups * sum(heights), bytes_accessed=130_000 * sum(heights), transcendentals=0
        ),
        name="image" if last else "partial",
    )(flags, *operands)


def body(source_field, receiver_field):
    slabs = lax.axis_size("slab")
    middle = slabs // 2
    cells, freqs = source_field.shape[2], source_field.shape[1]
    group = lax.axis_index("freq").astype(jnp.int32)
    slab = lax.axis_index("slab")
    left_flag = jnp.where(slab == 0, 2, jnp.where(slab == middle, 1, 0))
    right_flag = jnp.where(slab == slabs - 1, 2, jnp.where(slab == middle - 1, 1, 0))
    flags = jnp.stack([left_flag, right_flag]).astype(jnp.int32)
    edges = jnp.where(flags == 1, 0, flags)
    parts = regrouped(group[None], source_field, receiver_field)

    def swap(part, d):
        return lax.ppermute(part, "freq", [(g, g ^ d) for g in range(GROUPS)])

    two, three, one, other = swap(parts[2], 2), swap(parts[3], 3), swap(parts[1], 1), swap(parts[3], 1)

    whole = (2, 2, freqs, cells, ROWS, LANES)
    (own,) = pack(flags, (parts[0], one), ((None, 0, 0, None, 0, 0, 0), (None, 0, 1, None, 0, 0, 1)), (whole,))
    onward = [(s, s // middle * middle + (s + 1) % middle) for s in range(slabs)]
    left = lax.ppermute(own, "slab", onward)
    right = lax.ppermute(own, "slab", [(t, s) for s, t in onward])
    half = (2, 2, freqs, NEAR, ROWS, LANES)
    copies = []
    for out, flag, side in ((0, 1, 1), (1, 0, 0), (2, 1, 0), (3, 0, 1)):
        for slot in range(2):
            copies += [(flag, value, source, None, side, out, slot) for value, source in ((0, slot), (2, slot), (1, 2 + slot))]
    for slot in range(2):
        copies += [(0, value, source, slot, 0, 4, slot) for value, source in ((0, 5), (1, 5), (2, 4))]
    on_near, back_near, on_far, back_far, across = pack(
        flags, (two, three, parts[2], other, left, right), copies, (half,) * 4 + (whole,)
    )
    across = lax.ppermute(across, "slab", [(0, middle), (slabs - 1, middle - 1)])

    def around(value, step):
        cut = middle - 1 if step > 0 else middle
        pairs = []
        for s in range(slabs):
            for g in range(GROUPS):
                pairs.append((s * GROUPS + g, (s + step) % slabs * GROUPS + (g ^ 2 if s == cut else g)))
        return lax.ppermute(value, ("slab", "freq"), pairs)

    left_near, right_near = around(on_near, 1), around(back_near, -1)
    left_far, right_far = around(on_far, 1), around(back_far, -1)
    plan = []
    for g in range(2):
        plan += [(0, g, cells, cells, g, None, 0)]
        plan += [(1, g, cells, 0, g, 0, 0), (3, g, cells, 0, g, 0, 1)]
        plan += [(2, g, cells, 2 * cells, g, 1, 0), (3, g, cells, 2 * cells, g, 1, 1)]
    blocks = (own, left, right, across)
    befores = summed(flags, blocks, plan, (NEAR_BAND, FAR_BAND), None, cells, 2, 0)
    plan = [(0, None, cells, cells, 0, None, 0), (1, None, cells, cells, 1, None, 0)]
    for g in range(2):
        plan += [(2, g, NEAR, cells - NEAR, g, 0, 0), (3, g, NEAR, 2 * cells, g, 1, 0)]
    image = summed(edges, (two, three, left_near, right_near), plan, (NEAR_BAND,), befores[:1], cells, 2, 1)
    for g in range(2):
        plan += [(4, g, NEAR, cells - 2 * NEAR, g, 0, 0), (5, g, NEAR, 2 * cells + NEAR, g, 1, 0)]
    blocks = (two, three, left_near, right_near, left_far, right_far)
    return summed(edges, blocks, plan, (FAR_BAND,), befores[1:], cells, 2, 2, image)


def solution(mesh):
    in_specs = (P(None, "freq", "slab", None, None), P(None, "freq", "slab", None, None))
    out_specs = P("freq", None, "slab", None)
    return jax.shard_map(body, mesh=mesh, in_specs=in_specs, out_specs=out_specs, check_vma=False)
```

```python
import functools

import jax
import jax.numpy as jnp
from jax import lax
from jax.experimental import pallas as pl
from jax.experimental.pallas import tpu as pltpu
from jax.sharding import PartitionSpec as P

HMAX = 32
OFFSETS = 2 * HMAX + 1
GROUPS = 4
ROWS = 16
LANES = 128
TX = 8
TH = 4
SLOTS = 4
CHUNKS = 4
NEAR = HMAX // 2


def regroup_kernel(group_ref, source_ref, receiver_ref, *refs):
    out_refs, (held, sems) = refs[:GROUPS], refs[GROUPS:]
    freqs, cells = source_ref.shape[1], source_ref.shape[2]
    share = cells // CHUNKS

    def fetch(field, chunk):
        ref = (source_ref, receiver_ref)[field]
        part = pl.ds(chunk * share, share)
        return pltpu.make_async_copy(ref.at[:, :, part], held.at[field, :, :, part], sems.at[field, chunk])

    for chunk in range(CHUNKS):
        for field in range(2):
            fetch(field, chunk).start()

    def regroup(order):
        low = lax.broadcasted_iota(jnp.int32, (8, LANES), 0) < 4
        for chunk in range(CHUNKS):
            for field in range(2):
                fetch(field, chunk).wait()

                def one_cell(x, _):
                    for f in range(freqs):
                        parts = [[None, None] for _ in range(GROUPS)]
                        for c in range(2):
                            near = held[field, c, f, x, :, :LANES].astype(jnp.float32)
                            far = held[field, c, f, x, :, LANES:].astype(jnp.float32)
                            for pair in range(2):
                                a = near[8 * pair : 8 * pair + 8]
                                b = far[8 * pair : 8 * pair + 8]
                                parts[2 * pair][c] = jnp.where(low, a, pltpu.roll(b, 4, 0))
                                parts[2 * pair + 1][c] = jnp.where(low, pltpu.roll(a, 4, 0), b)
                        for d in range(GROUPS):
                            out_refs[d][field, f, x] = jnp.concatenate(parts[order ^ d], axis=0).astype(jnp.bfloat16)
                    return 0

                lax.fori_loop(chunk * share, (chunk + 1) * share, one_cell, 0, unroll=2)

    for order in range(GROUPS):
        pl.when(group_ref[0] == order)(functools.partial(regroup, order))


def regrouped(group, source_field, receiver_field):
    two, freqs, cells, _, _ = source_field.shape
    return pl.pallas_call(
        regroup_kernel,
        in_specs=[pl.BlockSpec(memory_space=pltpu.SMEM)] + [pl.BlockSpec(memory_space=pl.ANY)] * 2,
        out_specs=[pl.BlockSpec(memory_space=pltpu.VMEM)] * GROUPS,
        out_shape=[pltpu.VMEM((2, freqs, cells, ROWS, LANES), jnp.bfloat16)] * GROUPS,
        scratch_shapes=[pltpu.VMEM((2, 2, freqs, cells, 16, 2 * LANES), jnp.bfloat16), pltpu.SemaphoreType.DMA((2, CHUNKS))],
        compiler_params=pltpu.CompilerParams(vmem_limit_bytes=12 << 20),
        cost_estimate=pl.CostEstimate(flops=0, bytes_accessed=4 << 20, transcendentals=0),
        name="regroup",
    )(group, *(pltpu.with_memory_space_constraint(x, pltpu.HBM) for x in (source_field, receiver_field)))


def by_parity(flags_ref, choice):
    if isinstance(choice, int):
        return choice
    return jnp.where(flags_ref[0] == 0, choice[0], choice[1])


def pack_kernel(copies, refs_in, *refs):
    flags_ref, ins, outs = refs[0], refs[1 : 1 + refs_in], refs[1 + refs_in :]
    for crosses, source, part, at, out, slot in copies:

        def copy(source=source, part=part, at=at, out=out, slot=slot):
            start = by_parity(flags_ref, at)

            def one_cell(x, _):
                for field in range(2):
                    for f in range(outs[out].shape[2]):
                        where = (field, f, start + x) if part is None else (part, field, f, start + x)
                        outs[out][slot, field, f, x] = ins[source][where]
                return 0

            lax.fori_loop(0, outs[out].shape[3], one_cell, 0, unroll=4)

        if crosses is None:
            copy()
        else:
            pl.when((flags_ref[1] == 1) == crosses)(copy)


def pack(flags, arrays, copies, shapes, weight=1):
    vmem = pl.BlockSpec(memory_space=pltpu.VMEM)
    return pl.pallas_call(
        functools.partial(pack_kernel, copies, len(arrays)),
        in_specs=[pl.BlockSpec(memory_space=pltpu.SMEM)] + [vmem] * len(arrays),
        out_specs=[vmem] * len(shapes),
        out_shape=[jax.ShapeDtypeStruct(shape, jnp.bfloat16) for shape in shapes],
        compiler_params=pltpu.CompilerParams(vmem_limit_bytes=12 << 20),
        cost_estimate=pl.CostEstimate(flops=0, bytes_accessed=weight * (2 << 20), transcendentals=0),
        name="pack",
    )(flags, *arrays)


def sum_kernel(plan, bands, first, last, flags_ref, *refs):
    count = 1 + max(entry[0] for entry in plan if entry[0] is not None)
    blocks, refs = refs[:count], refs[count:]
    befores = ()
    if not first:
        befores, refs = refs[: len(bands)], refs[len(bands) :]
    if last == 2:
        refs = refs[1:]
    outs = refs[: 1 if last else len(bands)]
    fields = refs[len(outs)]
    if last:
        turn, stage, sems = refs[len(outs) + 1 :]
        out_ref = outs[0]
    cells = stage.shape[4 - 1] if last else outs[0].shape[1]
    total_freqs = fields.shape[2]

    def fill(index, part, at, length, to, group):
        start, to = by_parity(flags_ref, at), by_parity(flags_ref, to)

        def one_cell(x, _):
            for field in range(2):
                for f in range(2):
                    if index is None:
                        value = jnp.zeros((ROWS, LANES), jnp.float32)
                    elif part is None:
                        value = blocks[index][field, f, start + x].astype(jnp.float32)
                    else:
                        value = blocks[index][part, field, f, start + x].astype(jnp.float32)
                    fields[field, to + x, 2 * group + f] = value
            return 0

        lax.fori_loop(0, length, one_cell, 0, unroll=4)

    for index, part, at, length, to, group, values in plan:
        place = functools.partial(fill, index, part, at, length, to, group)
        if values is None:
            place()
        else:
            pl.when(functools.reduce(jnp.logical_or, [flags_ref[1] == value for value in values]))(place)

    def tile(before, out, k0, row0, rows, x0, slot):
        s0 = x0 + 2 * HMAX - k0 - (rows - 1)
        r0 = x0 + k0
        if first:
            total = [[None] * TX for _ in range(rows)]
        else:
            total = [[before[row0 + j, x0 + i] for i in range(TX)] for j in range(rows)]
        for f in range(total_freqs):
            for c in range(2):
                s = [fields[0, s0 + i, f, 8 * c : 8 * c + 8] for i in range(TX + rows - 1)]
                r = [fields[1, r0 + i, f, 8 * c : 8 * c + 8] for i in range(TX + rows - 1)]
                for j in range(rows):
                    for i in range(TX):
                        product = s[i + rows - 1 - j] * r[i + j]
                        total[j][i] = product if total[j][i] is None else total[j][i] + product
        for j in range(rows):
            if not last:
                for i in range(TX):
                    out[row0 + j, x0 + i] = total[j][i]
                continue
            for i in range(TX):
                turn[j, pl.ds(i, 8, stride=TX)] = 0.25 * total[j][i]
            for zh in range(2):
                for y in range(4):
                    row = zh * 4 + y
                    stage[slot, y, j, pl.ds(pl.multiple_of(x0, TX), TX), zh * LANES : (zh + 1) * LANES] = turn[
                        j, row * TX : (row + 1) * TX
                    ]

    def out_copy(k0, rows, slot):
        return pltpu.make_async_copy(stage.at[slot, :, pl.ds(0, rows)], out_ref.at[:, pl.ds(k0, rows)], sems.at[slot])

    for band, (k_first, steps, jump_at, jump, rest) in enumerate(bands):
        before = befores[band] if befores else None
        out = None if last else outs[band]

        def first_row(step):
            k0 = k_first + TH * step
            return k0 if not jump else k0 + jnp.where(step >= jump_at, jump, 0)

        def rows_of(k0, row0, rows, slot):
            def x_step(xt, _):
                tile(before, out, k0, row0, rows, xt * TX, slot)
                return 0

            lax.fori_loop(0, cells // TX, x_step, 0)

        def h_step(step, _):
            slot = lax.rem(step, SLOTS)
            if last:

                @pl.when(step >= SLOTS)
                def _():
                    out_copy(first_row(step - SLOTS), TH, slot).wait()

            rows_of(first_row(step), TH * step, TH, slot)
            if last:
                out_copy(first_row(step), TH, slot).start()
            return 0

        lax.fori_loop(0, steps, h_step, 0)
        if rest:
            slot = steps % SLOTS
            k0 = k_first + TH * steps
            if last:
                out_copy(first_row(steps - SLOTS), TH, slot).wait()
            rows_of(k0, TH * steps, rest, slot)
            if last:
                out_copy(k0, rest, slot).start()
        if last:
            for step in range(steps - SLOTS + (1 if rest else 0), steps):
                out_copy(first_row(step), TH, step % SLOTS).wait()
            if rest:
                out_copy(k_first + TH * steps, rest, steps % SLOTS).wait()


NEAR_BAND = (HMAX - NEAR, 2 * NEAR // TH, 0, 0, 1)
FAR_BAND = (0, 2 * NEAR // TH, NEAR // TH, 2 * NEAR + 1, 0)


def summed(flags, blocks, plan, bands, befores, cells, groups, last, image=None):
    first = befores is None
    heights = [TH * band[1] + band[4] for band in bands]
    scratch = [pltpu.VMEM((2, 3 * cells, 2 * groups, ROWS, LANES), jnp.float32)]
    vmem = pl.BlockSpec(memory_space=pltpu.VMEM)
    hbm = pl.BlockSpec(memory_space=pl.ANY)
    operands = list(blocks) + ([] if first else list(befores))
    in_specs = [pl.BlockSpec(memory_space=pltpu.SMEM)] + [vmem] * len(operands)
    aliases = {}
    if last:
        scratch += [
            pltpu.VMEM((TH, 8 * TX, LANES), jnp.float32),
            pltpu.VMEM((SLOTS, 4, TH, cells, 2 * LANES), jnp.float32),
            pltpu.SemaphoreType.DMA((SLOTS,)),
        ]
        out_shape = jax.ShapeDtypeStruct((4, OFFSETS, cells, 2 * LANES), jnp.float32)
        out_specs = hbm
        if last == 2:
            operands.append(image)
            in_specs.append(hbm)
            aliases = {len(operands): 0}
    else:
        out_shape = [pltpu.VMEM((height, cells, 8, LANES), jnp.float32) for height in heights]
        out_specs = [vmem] * len(heights)
    return pl.pallas_call(
        functools.partial(sum_kernel, plan, bands, first, last),
        in_specs=in_specs,
        out_specs=out_specs,
        out_shape=out_shape,
        scratch_shapes=scratch,
        input_output_aliases=aliases,
        compiler_params=pltpu.CompilerParams(vmem_limit_bytes=24 << 20),
        cost_estimate=pl.CostEstimate(
            flops=260_000 * groups * sum(heights), bytes_accessed=130_000 * sum(heights), transcendentals=0
        ),
        name="image" if last else "partial",
    )(flags, *operands)


def body(source_field, receiver_field):
    slabs = lax.axis_size("slab")
    middle = slabs // 2
    cells, freqs = source_field.shape[2], source_field.shape[1]
    group = lax.axis_index("freq").astype(jnp.int32)
    slab = lax.axis_index("slab")
    beyond = jnp.where((slab == 0) | (slab == slabs - 1), 2, 0)
    beyond = jnp.where((slab == middle) | (slab == middle - 1), 1, beyond)
    flags = jnp.stack([slab % 2, beyond]).astype(jnp.int32)
    parts = regrouped(group[None], source_field, receiver_field)

    def swap(part, d):
        return lax.ppermute(part, "freq", [(g, g ^ d) for g in range(GROUPS)])

    def trade(value, partner, turned=()):
        pairs = []
        for s in range(slabs):
            for g in range(GROUPS):
                pairs.append((s * GROUPS + g, partner(s) * GROUPS + (g ^ 2 if s in turned else g)))
        return lax.ppermute(value, ("slab", "freq"), pairs)

    def side_a(s):
        return s ^ 1

    def side_b(s):
        return min(max(s + 1 if s % 2 else s - 1, 0), slabs - 1)

    def side_b_of_half(s):
        return s // middle * middle + (s + 1 if s % 2 else s - 1) % middle

    def over_middle(s):
        return {0: middle, middle: 0, middle - 1: slabs - 1, slabs - 1: middle - 1}.get(s, s)

    two, three, one, other = swap(parts[2], 2), swap(parts[3], 3), swap(parts[1], 1), swap(parts[3], 1)

    whole, half = [(2, 2, freqs, length, ROWS, LANES) for length in (cells, NEAR)]
    (own,) = pack(flags, (parts[0], one), ((None, 0, None, 0, 0, 0), (None, 1, None, 0, 0, 1)), (whole,))
    whole_a, whole_b = trade(own, side_a), trade(own, side_b_of_half)

    rest = cells - NEAR
    copies = []
    for slot in range(2):
        for out, at in ((0, (rest, 0)), (2, (0, rest))):
            copies.append((None, slot, None, at, out, slot))
        for out, at in ((1, (0, rest)), (3, (rest, 0))):
            copies += [(False, slot, None, at, out, slot), (True, 2 + slot, None, at, out, slot)]
    near_a, near_b, far_a, far_b = pack(flags, (two, three, parts[2], other), copies, (half,) * 4, 1)
    turned = (middle - 1, middle)
    near_a, near_b = trade(near_a, side_a), trade(near_b, side_b, turned)
    whole_a, whole_b, far_a, far_b = lax.optimization_barrier((whole_a, whole_b, far_a, far_b))
    copies = [(None, 0, slot, at, out, slot) for slot in range(2) for out, at in ((0, (rest, 0)), (1, (0, rest)))]
    near_over, far_over = pack(flags, (whole_b,), copies, (half,) * 2)
    near_over = trade(near_over, over_middle)
    far_a, far_b = trade(far_a, side_a), trade(far_b, side_b, turned)
    far_over, near_over = lax.optimization_barrier((far_over, near_over))
    far_over = trade(far_over, over_middle)

    near_at_a, near_at_b = (2 * cells, rest), (rest, 2 * cells)
    far_at_a, far_at_b = (2 * cells + NEAR, 0), (0, 2 * cells + NEAR)
    plan, far_plan = [], []
    for g in range(2):
        plan += [(0, g, 0, cells, cells, g, None), (1, g, (0, rest), NEAR, near_at_a, g, None)]
        plan += [(2, g, (rest, 0), NEAR, near_at_b, g, (0,)), (3, g, 0, NEAR, near_at_b, g, (1,))]
        plan += [(None, g, 0, NEAR, near_at_b, g, (2,))]
        far_plan += [(1, g, (rest, 0), NEAR, far_at_a, g, None)]
        far_plan += [(2, g, (0, rest), NEAR, far_at_b, g, (0,)), (4, g, 0, NEAR, far_at_b, g, (1,))]
        far_plan += [(None, g, 0, NEAR, far_at_b, g, (2,))]
    blocks = (own, whole_a, whole_b, near_over)
    befores = summed(flags, blocks, plan, (NEAR_BAND,), None, cells, 2, 0)
    far_sums = (flags, plan + far_plan, blocks)
    plan = [(0, None, 0, cells, cells, 0, None), (1, None, 0, cells, cells, 1, None)]
    far_plan = []
    for g in range(2):
        plan += [(2, g, 0, NEAR, near_at_a, g, None)]
        plan += [(3, g, 0, NEAR, near_at_b, g, (0, 1)), (None, g, 0, NEAR, near_at_b, g, (2,))]
        far_plan += [(4, g, 0, NEAR, far_at_a, g, None)]
        far_plan += [(5, g, 0, NEAR, far_at_b, g, (0, 1)), (None, g, 0, NEAR, far_at_b, g, (2,))]
    image = summed(flags, (two, three, near_a, near_b), plan, (NEAR_BAND,), befores, cells, 2, 1)
    image, far_over = lax.optimization_barrier((image, far_over))
    befores = summed(flags, far_sums[2] + (far_over,), far_sums[1], (FAR_BAND,), None, cells, 2, 0)
    blocks = (two, three, near_a, near_b, far_a, far_b)
    return summed(flags, blocks, plan + far_plan, (FAR_BAND,), befores, cells, 2, 2, image)


def solution(mesh):
    in_specs = (P(None, "freq", "slab", None, None), P(None, "freq", "slab", None, None))
    out_specs = P("freq", None, "slab", None)
    return jax.shard_map(body, mesh=mesh, in_specs=in_specs, out_specs=out_specs, check_vma=False)
```

```python
import functools

import jax
import jax.numpy as jnp
from jax import lax
from jax.experimental import pallas as pl
from jax.experimental.pallas import tpu as pltpu
from jax.sharding import PartitionSpec as P

HMAX = 32
OFFSETS = 2 * HMAX + 1
GROUPS = 4
ROWS = 16
LANES = 128
TX = 8
TH = 4
SLOTS = 4
CHUNKS = 4
NEAR = HMAX // 2


def regroup_kernel(group_ref, source_ref, receiver_ref, *refs):
    out_refs, (held, sems) = refs[:GROUPS], refs[GROUPS:]
    freqs, cells = source_ref.shape[1], source_ref.shape[2]
    share = cells // CHUNKS

    def fetch(field, chunk):
        ref = (source_ref, receiver_ref)[field]
        part = pl.ds(chunk * share, share)
        return pltpu.make_async_copy(ref.at[:, :, part], held.at[field, :, :, part], sems.at[field, chunk])

    for chunk in range(CHUNKS):
        for field in range(2):
            fetch(field, chunk).start()

    def regroup(order):
        low = lax.broadcasted_iota(jnp.int32, (8, LANES), 0) < 4
        for chunk in range(CHUNKS):
            for field in range(2):
                fetch(field, chunk).wait()

                def one_cell(x, _):
                    for f in range(freqs):
                        parts = [[None, None] for _ in range(GROUPS)]
                        for c in range(2):
                            near = held[field, c, f, x, :, :LANES].astype(jnp.float32)
                            far = held[field, c, f, x, :, LANES:].astype(jnp.float32)
                            for pair in range(2):
                                a = near[8 * pair : 8 * pair + 8]
                                b = far[8 * pair : 8 * pair + 8]
                                parts[2 * pair][c] = jnp.where(low, a, pltpu.roll(b, 4, 0))
                                parts[2 * pair + 1][c] = jnp.where(low, pltpu.roll(a, 4, 0), b)
                        for d in range(GROUPS):
                            out_refs[d][field, f, x] = jnp.concatenate(parts[order ^ d], axis=0).astype(jnp.bfloat16)
                    return 0

                lax.fori_loop(chunk * share, (chunk + 1) * share, one_cell, 0, unroll=2)

    for order in range(GROUPS):
        pl.when(group_ref[0] == order)(functools.partial(regroup, order))


def regrouped(group, source_field, receiver_field):
    two, freqs, cells, _, _ = source_field.shape
    return pl.pallas_call(
        regroup_kernel,
        in_specs=[pl.BlockSpec(memory_space=pltpu.SMEM)] + [pl.BlockSpec(memory_space=pl.ANY)] * 2,
        out_specs=[pl.BlockSpec(memory_space=pltpu.VMEM)] * GROUPS,
        out_shape=[pltpu.VMEM((2, freqs, cells, ROWS, LANES), jnp.bfloat16)] * GROUPS,
        scratch_shapes=[pltpu.VMEM((2, 2, freqs, cells, 16, 2 * LANES), jnp.bfloat16), pltpu.SemaphoreType.DMA((2, CHUNKS))],
        compiler_params=pltpu.CompilerParams(vmem_limit_bytes=12 << 20),
        cost_estimate=pl.CostEstimate(flops=0, bytes_accessed=4 << 20, transcendentals=0),
        name="regroup",
    )(group, *(pltpu.with_memory_space_constraint(x, pltpu.HBM) for x in (source_field, receiver_field)))


def by_parity(flags_ref, choice):
    if isinstance(choice, int):
        return choice
    return jnp.where(flags_ref[0] == 0, choice[0], choice[1])


def pack_kernel(copies, refs_in, *refs):
    flags_ref, ins, outs = refs[0], refs[1 : 1 + refs_in], refs[1 + refs_in :]
    for crosses, source, part, at, out, slot in copies:

        def copy(source=source, part=part, at=at, out=out, slot=slot):
            start = by_parity(flags_ref, at)

            def one_cell(x, _):
                for field in range(2):
                    for f in range(outs[out].shape[2]):
                        where = (field, f, start + x) if part is None else (part, field, f, start + x)
                        outs[out][slot, field, f, x] = ins[source][where]
                return 0

            lax.fori_loop(0, outs[out].shape[3], one_cell, 0, unroll=4)

        if crosses is None:
            copy()
        else:
            pl.when((flags_ref[1] == 1) == crosses)(copy)


def pack(flags, arrays, copies, shapes):
    vmem = pl.BlockSpec(memory_space=pltpu.VMEM)
    return pl.pallas_call(
        functools.partial(pack_kernel, copies, len(arrays)),
        in_specs=[pl.BlockSpec(memory_space=pltpu.SMEM)] + [vmem] * len(arrays),
        out_specs=[vmem] * len(shapes),
        out_shape=[jax.ShapeDtypeStruct(shape, jnp.bfloat16) for shape in shapes],
        compiler_params=pltpu.CompilerParams(vmem_limit_bytes=12 << 20),
        cost_estimate=pl.CostEstimate(flops=0, bytes_accessed=2 << 20, transcendentals=0),
        name="pack",
    )(flags, *arrays)


def sum_kernel(plan, bands, first, last, flags_ref, *refs):
    count = 1 + max(entry[0] for entry in plan if entry[0] is not None)
    blocks, refs = refs[:count], refs[count:]
    befores = ()
    if not first:
        befores, refs = refs[: len(bands)], refs[len(bands) :]
    if last == 2:
        refs = refs[1:]
    outs = refs[: 1 if last else len(bands)]
    fields = refs[len(outs)]
    if last:
        turn, stage, sems = refs[len(outs) + 1 :]
        out_ref = outs[0]
    cells = stage.shape[4 - 1] if last else outs[0].shape[1]
    total_freqs = fields.shape[2]

    def fill(index, part, at, length, to, group):
        start, to = by_parity(flags_ref, at), by_parity(flags_ref, to)

        def one_cell(x, _):
            for field in range(2):
                for f in range(2):
                    if index is None:
                        value = jnp.zeros((ROWS, LANES), jnp.float32)
                    elif part is None:
                        value = blocks[index][field, f, start + x].astype(jnp.float32)
                    else:
                        value = blocks[index][part, field, f, start + x].astype(jnp.float32)
                    fields[field, to + x, 2 * group + f] = value
            return 0

        lax.fori_loop(0, length, one_cell, 0, unroll=4)

    for index, part, at, length, to, group, values in plan:
        place = functools.partial(fill, index, part, at, length, to, group)
        if values is None:
            place()
        else:
            pl.when(functools.reduce(jnp.logical_or, [flags_ref[1] == value for value in values]))(place)

    def tile(before, out, k0, row0, rows, x0, slot):
        s0 = x0 + 2 * HMAX - k0 - (rows - 1)
        r0 = x0 + k0
        if first:
            total = [[None] * TX for _ in range(rows)]
        else:
            total = [[before[row0 + j, x0 + i] for i in range(TX)] for j in range(rows)]
        for f in range(total_freqs):
            for c in range(2):
                s = [fields[0, s0 + i, f, 8 * c : 8 * c + 8] for i in range(TX + rows - 1)]
                r = [fields[1, r0 + i, f, 8 * c : 8 * c + 8] for i in range(TX + rows - 1)]
                for j in range(rows):
                    for i in range(TX):
                        product = s[i + rows - 1 - j] * r[i + j]
                        total[j][i] = product if total[j][i] is None else total[j][i] + product
        for j in range(rows):
            if not last:
                for i in range(TX):
                    out[row0 + j, x0 + i] = total[j][i]
                continue
            for i in range(TX):
                turn[j, pl.ds(i, 8, stride=TX)] = 0.25 * total[j][i]
            for zh in range(2):
                for y in range(4):
                    row = zh * 4 + y
                    stage[slot, y, j, pl.ds(pl.multiple_of(x0, TX), TX), zh * LANES : (zh + 1) * LANES] = turn[
                        j, row * TX : (row + 1) * TX
                    ]

    def out_copy(k0, rows, slot):
        return pltpu.make_async_copy(stage.at[slot, :, pl.ds(0, rows)], out_ref.at[:, pl.ds(k0, rows)], sems.at[slot])

    for band, (k_first, steps, jump_at, jump, rest) in enumerate(bands):
        before = befores[band] if befores else None
        out = None if last else outs[band]

        def first_row(step):
            k0 = k_first + TH * step
            return k0 if not jump else k0 + jnp.where(step >= jump_at, jump, 0)

        def rows_of(k0, row0, rows, slot):
            def x_step(xt, _):
                tile(before, out, k0, row0, rows, xt * TX, slot)
                return 0

            lax.fori_loop(0, cells // TX, x_step, 0)

        def h_step(step, _):
            slot = lax.rem(step, SLOTS)
            if last:

                @pl.when(step >= SLOTS)
                def _():
                    out_copy(first_row(step - SLOTS), TH, slot).wait()

            rows_of(first_row(step), TH * step, TH, slot)
            if last:
                out_copy(first_row(step), TH, slot).start()
            return 0

        lax.fori_loop(0, steps, h_step, 0)
        if rest:
            slot = steps % SLOTS
            k0 = k_first + TH * steps
            if last:
                out_copy(first_row(steps - SLOTS), TH, slot).wait()
            rows_of(k0, TH * steps, rest, slot)
            if last:
                out_copy(k0, rest, slot).start()
        if last:
            for step in range(steps - SLOTS + (1 if rest else 0), steps):
                out_copy(first_row(step), TH, step % SLOTS).wait()
            if rest:
                out_copy(k_first + TH * steps, rest, steps % SLOTS).wait()


NEAR_BAND = (HMAX - NEAR, 2 * NEAR // TH, 0, 0, 1)
FAR_BAND = (0, 2 * NEAR // TH, NEAR // TH, 2 * NEAR + 1, 0)


def summed(flags, blocks, plan, bands, befores, cells, groups, last, image=None):
    first = befores is None
    heights = [TH * band[1] + band[4] for band in bands]
    scratch = [pltpu.VMEM((2, 3 * cells, 2 * groups, ROWS, LANES), jnp.float32)]
    vmem = pl.BlockSpec(memory_space=pltpu.VMEM)
    hbm = pl.BlockSpec(memory_space=pl.ANY)
    operands = list(blocks) + ([] if first else list(befores))
    in_specs = [pl.BlockSpec(memory_space=pltpu.SMEM)] + [vmem] * len(operands)
    aliases = {}
    if last:
        scratch += [
            pltpu.VMEM((TH, 8 * TX, LANES), jnp.float32),
            pltpu.VMEM((SLOTS, 4, TH, cells, 2 * LANES), jnp.float32),
            pltpu.SemaphoreType.DMA((SLOTS,)),
        ]
        out_shape = jax.ShapeDtypeStruct((4, OFFSETS, cells, 2 * LANES), jnp.float32)
        out_specs = hbm
        if last == 2:
            operands.append(image)
            in_specs.append(hbm)
            aliases = {len(operands): 0}
    else:
        out_shape = [pltpu.VMEM((height, cells, 8, LANES), jnp.float32) for height in heights]
        out_specs = [vmem] * len(heights)
    return pl.pallas_call(
        functools.partial(sum_kernel, plan, bands, first, last),
        in_specs=in_specs,
        out_specs=out_specs,
        out_shape=out_shape,
        scratch_shapes=scratch,
        input_output_aliases=aliases,
        compiler_params=pltpu.CompilerParams(vmem_limit_bytes=24 << 20),
        cost_estimate=pl.CostEstimate(
            flops=260_000 * groups * sum(heights), bytes_accessed=130_000 * sum(heights), transcendentals=0
        ),
        name="image" if last else "partial",
    )(flags, *operands)


def body(source_field, receiver_field):
    slabs = lax.axis_size("slab")
    middle = slabs // 2
    cells, freqs = source_field.shape[2], source_field.shape[1]
    group = lax.axis_index("freq").astype(jnp.int32)
    slab = lax.axis_index("slab")
    beyond = jnp.where((slab == 0) | (slab == slabs - 1), 2, 0)
    beyond = jnp.where((slab == middle) | (slab == middle - 1), 1, beyond)
    flags = jnp.stack([slab % 2, beyond]).astype(jnp.int32)
    parts = regrouped(group[None], source_field, receiver_field)

    def swap(part, d):
        return lax.ppermute(part, "freq", [(g, g ^ d) for g in range(GROUPS)])

    def trade(value, partner, turned=()):
        pairs = []
        for s in range(slabs):
            for g in range(GROUPS):
                pairs.append((s * GROUPS + g, partner(s) * GROUPS + (g ^ 2 if s in turned else g)))
        return lax.ppermute(value, ("slab", "freq"), pairs)

    def side_a(s):
        return s ^ 1

    def side_b(s):
        return min(max(s + 1 if s % 2 else s - 1, 0), slabs - 1)

    def side_b_of_half(s):
        return s // middle * middle + (s + 1 if s % 2 else s - 1) % middle

    def over_middle(s):
        return {0: middle, middle: 0, middle - 1: slabs - 1, slabs - 1: middle - 1}.get(s, s)

    two, three, one, other = swap(parts[2], 2), swap(parts[3], 3), swap(parts[1], 1), swap(parts[3], 1)

    whole, half = [(2, 2, freqs, length, ROWS, LANES) for length in (cells, NEAR)]
    rest = cells - NEAR
    copies = []
    for slot in range(2):
        copies += [(None, slot, None, 0, 0, slot), (None, 2 + slot, None, 0, 1, slot)]
        copies += [(None, slot, None, (0, rest), 2, slot), (None, slot, None, (rest, 0), 3, slot)]
    own, turned_own, near_b, far_b = pack(flags, (parts[0], one, parts[2], other), copies, (whole,) * 2 + (half,) * 2)
    whole_a = trade(own, side_a)
    first_near_b, first_far_b = trade(near_b, side_b_of_half), trade(far_b, side_b_of_half)
    near_over, far_over = trade(first_near_b, over_middle), trade(first_far_b, over_middle)

    copies = []
    for slot in range(2):
        for out, at in ((0, (rest, 0)), (2, (0, rest))):
            copies.append((None, slot, None, at, out, slot))
        for out, at in ((1, (0, rest)), (3, (rest, 0))):
            copies += [(False, slot, None, at, out, slot), (True, 2, slot, at, out, slot)]
    near_a, near_b, far_a, far_b = pack(flags, (two, three, turned_own), copies, (half,) * 4)
    turned = (middle - 1, middle)
    near_a, near_b = trade(near_a, side_a), trade(near_b, side_b, turned)
    whole_a, first_near_b, first_far_b, far_a, far_b = lax.optimization_barrier(
        (whole_a, first_near_b, first_far_b, far_a, far_b)
    )
    far_a, far_b = trade(far_a, side_a), trade(far_b, side_b, turned)

    near_at_a, near_at_b = (2 * cells, rest), (rest, 2 * cells)
    far_at_a, far_at_b = (2 * cells + NEAR, 0), (0, 2 * cells + NEAR)
    plan, far_plan = [], []
    for g in range(2):
        plan += [(0, g, 0, cells, cells, g, None), (1, g, (0, rest), NEAR, near_at_a, g, None)]
        plan += [(2, g, 0, NEAR, near_at_b, g, (0,)), (3, g, 0, NEAR, near_at_b, g, (1,))]
        plan += [(None, g, 0, NEAR, near_at_b, g, (2,))]
        far_plan += [(1, g, (rest, 0), NEAR, far_at_a, g, None)]
        far_plan += [(4, g, 0, NEAR, far_at_b, g, (0,)), (5, g, 0, NEAR, far_at_b, g, (1,))]
        far_plan += [(None, g, 0, NEAR, far_at_b, g, (2,))]
    blocks = (own, whole_a, first_near_b, near_over)
    befores = summed(flags, blocks, plan, (NEAR_BAND,), None, cells, 2, 0)
    far_sums = (flags, plan + far_plan, blocks)
    plan = [(0, None, 0, cells, cells, 0, None), (1, None, 0, cells, cells, 1, None)]
    far_plan = []
    for g in range(2):
        plan += [(2, g, 0, NEAR, near_at_a, g, None)]
        plan += [(3, g, 0, NEAR, near_at_b, g, (0, 1)), (None, g, 0, NEAR, near_at_b, g, (2,))]
        far_plan += [(4, g, 0, NEAR, far_at_a, g, None)]
        far_plan += [(5, g, 0, NEAR, far_at_b, g, (0, 1)), (None, g, 0, NEAR, far_at_b, g, (2,))]
    image = summed(flags, (two, three, near_a, near_b), plan, (NEAR_BAND,), befores, cells, 2, 1)
    image, far_over = lax.optimization_barrier((image, far_over))
    befores = summed(flags, far_sums[2] + (first_far_b, far_over), far_sums[1], (FAR_BAND,), None, cells, 2, 0)
    blocks = (two, three, near_a, near_b, far_a, far_b)
    return summed(flags, blocks, plan + far_plan, (FAR_BAND,), befores, cells, 2, 2, image)


def solution(mesh):
    in_specs = (P(None, "freq", "slab", None, None), P(None, "freq", "slab", None, None))
    out_specs = P("freq", None, "slab", None)
    return jax.shard_map(body, mesh=mesh, in_specs=in_specs, out_specs=out_specs, check_vma=False)
```

```python
import functools

import jax
import jax.numpy as jnp
from jax import lax
from jax.experimental import pallas as pl
from jax.experimental.pallas import tpu as pltpu
from jax.sharding import PartitionSpec as P

HMAX = 32
OFFSETS = 2 * HMAX + 1
GROUPS = 4
ROWS = 16
LANES = 128
TX = 8
TH = 4
SLOTS = 4
CHUNKS = 4
NEAR = HMAX // 2


def regroup_kernel(group_ref, source_ref, receiver_ref, *refs):
    out_refs, (held, sems) = refs[:GROUPS], refs[GROUPS:]
    freqs, cells = source_ref.shape[1], source_ref.shape[2]
    share = cells // CHUNKS

    def fetch(field, chunk):
        ref = (source_ref, receiver_ref)[field]
        part = pl.ds(chunk * share, share)
        return pltpu.make_async_copy(ref.at[:, :, part], held.at[field, :, :, part], sems.at[field, chunk])

    for chunk in range(CHUNKS):
        for field in range(2):
            fetch(field, chunk).start()

    def regroup(order):
        low = lax.broadcasted_iota(jnp.int32, (8, LANES), 0) < 4
        for chunk in range(CHUNKS):
            for field in range(2):
                fetch(field, chunk).wait()

                def one_cell(x, _):
                    for f in range(freqs):
                        parts = [[None, None] for _ in range(GROUPS)]
                        for c in range(2):
                            near = held[field, c, f, x, :, :LANES].astype(jnp.float32)
                            far = held[field, c, f, x, :, LANES:].astype(jnp.float32)
                            for pair in range(2):
                                a = near[8 * pair : 8 * pair + 8]
                                b = far[8 * pair : 8 * pair + 8]
                                parts[2 * pair][c] = jnp.where(low, a, pltpu.roll(b, 4, 0))
                                parts[2 * pair + 1][c] = jnp.where(low, pltpu.roll(a, 4, 0), b)
                        for d in range(GROUPS):
                            out_refs[d][field, f, x] = jnp.concatenate(parts[order ^ d], axis=0).astype(jnp.bfloat16)
                    return 0

                lax.fori_loop(chunk * share, (chunk + 1) * share, one_cell, 0, unroll=2)

    for order in range(GROUPS):
        pl.when(group_ref[0] == order)(functools.partial(regroup, order))


def regrouped(group, source_field, receiver_field):
    two, freqs, cells, _, _ = source_field.shape
    return pl.pallas_call(
        regroup_kernel,
        in_specs=[pl.BlockSpec(memory_space=pltpu.SMEM)] + [pl.BlockSpec(memory_space=pl.ANY)] * 2,
        out_specs=[pl.BlockSpec(memory_space=pltpu.VMEM)] * GROUPS,
        out_shape=[pltpu.VMEM((2, freqs, cells, ROWS, LANES), jnp.bfloat16)] * GROUPS,
        scratch_shapes=[pltpu.VMEM((2, 2, freqs, cells, 16, 2 * LANES), jnp.bfloat16), pltpu.SemaphoreType.DMA((2, CHUNKS))],
        compiler_params=pltpu.CompilerParams(vmem_limit_bytes=12 << 20),
        cost_estimate=pl.CostEstimate(flops=0, bytes_accessed=4 << 20, transcendentals=0),
        name="regroup",
    )(group, *(pltpu.with_memory_space_constraint(x, pltpu.HBM) for x in (source_field, receiver_field)))


def by_parity(flags_ref, choice):
    if isinstance(choice, int):
        return choice
    return jnp.where(flags_ref[0] == 0, choice[0], choice[1])


def pack_kernel(copies, refs_in, *refs):
    flags_ref, ins, outs = refs[0], refs[1 : 1 + refs_in], refs[1 + refs_in :]
    for crosses, source, part, at, out, slot in copies:

        def copy(source=source, part=part, at=at, out=out, slot=slot):
            start = by_parity(flags_ref, at)

            def one_cell(x, _):
                for field in range(2):
                    for f in range(outs[out].shape[2]):
                        where = (field, f, start + x) if part is None else (part, field, f, start + x)
                        outs[out][slot, field, f, x] = ins[source][where]
                return 0

            lax.fori_loop(0, outs[out].shape[3], one_cell, 0, unroll=4)

        if crosses is None:
            copy()
        else:
            pl.when((flags_ref[1] == 1) == crosses)(copy)


def pack(flags, arrays, copies, shapes):
    vmem = pl.BlockSpec(memory_space=pltpu.VMEM)
    return pl.pallas_call(
        functools.partial(pack_kernel, copies, len(arrays)),
        in_specs=[pl.BlockSpec(memory_space=pltpu.SMEM)] + [vmem] * len(arrays),
        out_specs=[vmem] * len(shapes),
        out_shape=[jax.ShapeDtypeStruct(shape, jnp.bfloat16) for shape in shapes],
        compiler_params=pltpu.CompilerParams(vmem_limit_bytes=12 << 20),
        cost_estimate=pl.CostEstimate(flops=0, bytes_accessed=2 << 20, transcendentals=0),
        name="pack",
    )(flags, *arrays)


def sum_kernel(plan, bands, first, last, flags_ref, *refs):
    count = 1 + max(entry[0] for entry in plan if entry[0] is not None)
    blocks, refs = refs[:count], refs[count:]
    befores = ()
    if not first:
        befores, refs = refs[: len(bands)], refs[len(bands) :]
    if last == 2:
        refs = refs[1:]
    outs = refs[: 1 if last else len(bands)]
    fields = refs[len(outs)]
    if last:
        turn, stage, sems = refs[len(outs) + 1 :]
        out_ref = outs[0]
    cells = stage.shape[4 - 1] if last else outs[0].shape[1]
    total_freqs = fields.shape[2]

    def fill(index, part, at, length, to, group):
        start, to = by_parity(flags_ref, at), by_parity(flags_ref, to)

        def one_cell(x, _):
            for field in range(2):
                for f in range(2):
                    if index is None:
                        value = jnp.zeros((ROWS, LANES), jnp.float32)
                    elif part is None:
                        value = blocks[index][field, f, start + x].astype(jnp.float32)
                    else:
                        value = blocks[index][part, field, f, start + x].astype(jnp.float32)
                    fields[field, to + x, 2 * group + f] = value
            return 0

        lax.fori_loop(0, length, one_cell, 0, unroll=4)

    for index, part, at, length, to, group, values in plan:
        place = functools.partial(fill, index, part, at, length, to, group)
        if values is None:
            place()
        else:
            pl.when(functools.reduce(jnp.logical_or, [flags_ref[1] == value for value in values]))(place)

    def tile(before, out, k0, row0, rows, x0, slot):
        s0 = x0 + 2 * HMAX - k0 - (rows - 1)
        r0 = x0 + k0
        if first:
            total = [[None] * TX for _ in range(rows)]
        else:
            total = [[before[row0 + j, x0 + i] for i in range(TX)] for j in range(rows)]
        for f in range(total_freqs):
            for c in range(2):
                s = [fields[0, s0 + i, f, 8 * c : 8 * c + 8] for i in range(TX + rows - 1)]
                r = [fields[1, r0 + i, f, 8 * c : 8 * c + 8] for i in range(TX + rows - 1)]
                for j in range(rows):
                    for i in range(TX):
                        product = s[i + rows - 1 - j] * r[i + j]
                        total[j][i] = product if total[j][i] is None else total[j][i] + product
        for j in range(rows):
            if not last:
                for i in range(TX):
                    out[row0 + j, x0 + i] = total[j][i]
                continue
            for i in range(TX):
                turn[j, pl.ds(i, 8, stride=TX)] = 0.25 * total[j][i]
            for zh in range(2):
                for y in range(4):
                    row = zh * 4 + y
                    stage[slot, y, j, pl.ds(pl.multiple_of(x0, TX), TX), zh * LANES : (zh + 1) * LANES] = turn[
                        j, row * TX : (row + 1) * TX
                    ]

    def out_copy(k0, rows, slot):
        return pltpu.make_async_copy(stage.at[slot, :, pl.ds(0, rows)], out_ref.at[:, pl.ds(k0, rows)], sems.at[slot])

    for band, (k_first, steps, jump_at, jump, rest) in enumerate(bands):
        before = befores[band] if befores else None
        out = None if last else outs[band]

        def first_row(step):
            k0 = k_first + TH * step
            return k0 if not jump else k0 + jnp.where(step >= jump_at, jump, 0)

        def rows_of(k0, row0, rows, slot):
            def x_step(xt, _):
                tile(before, out, k0, row0, rows, xt * TX, slot)
                return 0

            lax.fori_loop(0, cells // TX, x_step, 0)

        def h_step(step, _):
            slot = lax.rem(step, SLOTS)
            if last:

                @pl.when(step >= SLOTS)
                def _():
                    out_copy(first_row(step - SLOTS), TH, slot).wait()

            rows_of(first_row(step), TH * step, TH, slot)
            if last:
                out_copy(first_row(step), TH, slot).start()
            return 0

        lax.fori_loop(0, steps, h_step, 0)
        if rest:
            slot = steps % SLOTS
            k0 = k_first + TH * steps
            if last:
                out_copy(first_row(steps - SLOTS), TH, slot).wait()
            rows_of(k0, TH * steps, rest, slot)
            if last:
                out_copy(k0, rest, slot).start()
        if last:
            for step in range(steps - SLOTS + (1 if rest else 0), steps):
                out_copy(first_row(step), TH, step % SLOTS).wait()
            if rest:
                out_copy(k_first + TH * steps, rest, steps % SLOTS).wait()


NEAR_BAND = (HMAX - NEAR, 2 * NEAR // TH, 0, 0, 1)
FAR_BAND = (0, 2 * NEAR // TH, NEAR // TH, 2 * NEAR + 1, 0)


def summed(flags, blocks, plan, bands, befores, cells, groups, last, image=None):
    first = befores is None
    heights = [TH * band[1] + band[4] for band in bands]
    scratch = [pltpu.VMEM((2, 3 * cells, 2 * groups, ROWS, LANES), jnp.float32)]
    vmem = pl.BlockSpec(memory_space=pltpu.VMEM)
    hbm = pl.BlockSpec(memory_space=pl.ANY)
    operands = list(blocks) + ([] if first else list(befores))
    in_specs = [pl.BlockSpec(memory_space=pltpu.SMEM)] + [vmem] * len(operands)
    aliases = {}
    if last:
        scratch += [
            pltpu.VMEM((TH, 8 * TX, LANES), jnp.float32),
            pltpu.VMEM((SLOTS, 4, TH, cells, 2 * LANES), jnp.float32),
            pltpu.SemaphoreType.DMA((SLOTS,)),
        ]
        out_shape = jax.ShapeDtypeStruct((4, OFFSETS, cells, 2 * LANES), jnp.float32)
        out_specs = hbm
        if last == 2:
            operands.append(image)
            in_specs.append(hbm)
            aliases = {len(operands): 0}
    else:
        out_shape = [pltpu.VMEM((height, cells, 8, LANES), jnp.float32) for height in heights]
        out_specs = [vmem] * len(heights)
    return pl.pallas_call(
        functools.partial(sum_kernel, plan, bands, first, last),
        in_specs=in_specs,
        out_specs=out_specs,
        out_shape=out_shape,
        scratch_shapes=scratch,
        input_output_aliases=aliases,
        compiler_params=pltpu.CompilerParams(vmem_limit_bytes=24 << 20),
        cost_estimate=pl.CostEstimate(
            flops=260_000 * groups * sum(heights), bytes_accessed=130_000 * sum(heights), transcendentals=0
        ),
        name="image" if last else "partial",
    )(flags, *operands)


def body(source_field, receiver_field):
    slabs = lax.axis_size("slab")
    middle = slabs // 2
    cells, freqs = source_field.shape[2], source_field.shape[1]
    group = lax.axis_index("freq").astype(jnp.int32)
    slab = lax.axis_index("slab")
    beyond = jnp.where((slab == 0) | (slab == slabs - 1), 2, 0)
    beyond = jnp.where((slab == middle) | (slab == middle - 1), 1, beyond)
    flags = jnp.stack([slab % 2, beyond]).astype(jnp.int32)
    parts = regrouped(group[None], source_field, receiver_field)

    def swap(part, d):
        return lax.ppermute(part, "freq", [(g, g ^ d) for g in range(GROUPS)])

    def trade(value, partner, turned=()):
        pairs = []
        for s in range(slabs):
            for g in range(GROUPS):
                pairs.append((s * GROUPS + g, partner(s) * GROUPS + (g ^ 2 if s in turned else g)))
        return lax.ppermute(value, ("slab", "freq"), pairs)

    def side_a(s):
        return s ^ 1

    def side_b(s):
        return min(max(s + 1 if s % 2 else s - 1, 0), slabs - 1)

    def side_b_of_half(s):
        return s // middle * middle + (s + 1 if s % 2 else s - 1) % middle

    one, other = swap(parts[1], 1), swap(parts[3], 1)

    whole, half = [(2, 2, freqs, length, ROWS, LANES) for length in (cells, NEAR)]
    rest = cells - NEAR
    copies = []
    for slot in range(2):
        copies += [(None, slot, None, 0, 0, slot), (None, 2 + slot, None, 0, 1, slot)]
        copies += [(None, slot, None, (0, rest), 2, slot), (None, slot, None, (rest, 0), 3, slot)]
    own, turned_own, near_b, far_b = pack(flags, (parts[0], one, parts[2], other), copies, (whole,) * 2 + (half,) * 2)
    far_own = swap(turned_own, 2)
    whole_a = trade(own, side_a)
    first_near_b, first_far_b = trade(near_b, side_b_of_half), trade(far_b, side_b_of_half)
    over_middle = [(0, middle), (slabs - 1, middle - 1)]
    near_over, far_over = [lax.ppermute(value, "slab", over_middle) for value in (first_near_b, first_far_b)]

    copies = []
    for slot in range(2):
        for out, at in ((0, (rest, 0)), (2, (0, rest))):
            copies.append((None, 0, slot, at, out, slot))
        for out, at in ((1, (0, rest)), (3, (rest, 0))):
            copies += [(False, 0, slot, at, out, slot), (True, 1, slot, at, out, slot)]
    near_a, near_b, far_a, far_b = pack(flags, (far_own, turned_own), copies, (half,) * 4)
    turned = (middle - 1, middle)
    near_a, near_b = trade(near_a, side_a), trade(near_b, side_b, turned)
    whole_a, first_near_b, first_far_b, far_a, far_b = lax.optimization_barrier(
        (whole_a, first_near_b, first_far_b, far_a, far_b)
    )
    far_a, far_b = trade(far_a, side_a), trade(far_b, side_b, turned)

    near_at_a, near_at_b = (2 * cells, rest), (rest, 2 * cells)
    far_at_a, far_at_b = (2 * cells + NEAR, 0), (0, 2 * cells + NEAR)
    plan, far_plan = [], []
    for g in range(2):
        plan += [(0, g, 0, cells, cells, g, None), (1, g, (0, rest), NEAR, near_at_a, g, None)]
        plan += [(2, g, 0, NEAR, near_at_b, g, (0,)), (3, g, 0, NEAR, near_at_b, g, (1,))]
        plan += [(None, g, 0, NEAR, near_at_b, g, (2,))]
        far_plan += [(1, g, (rest, 0), NEAR, far_at_a, g, None)]
        far_plan += [(4, g, 0, NEAR, far_at_b, g, (0,)), (5, g, 0, NEAR, far_at_b, g, (1,))]
        far_plan += [(None, g, 0, NEAR, far_at_b, g, (2,))]
    blocks = (own, whole_a, first_near_b, near_over)
    befores = summed(flags, blocks, plan, (NEAR_BAND,), None, cells, 2, 0)
    far_sums = (flags, plan + far_plan, blocks)
    plan, far_plan = [], []
    for g in range(2):
        plan += [(0, g, 0, cells, cells, g, None), (1, g, 0, NEAR, near_at_a, g, None)]
        plan += [(2, g, 0, NEAR, near_at_b, g, (0, 1)), (None, g, 0, NEAR, near_at_b, g, (2,))]
        far_plan += [(3, g, 0, NEAR, far_at_a, g, None)]
        far_plan += [(4, g, 0, NEAR, far_at_b, g, (0, 1)), (None, g, 0, NEAR, far_at_b, g, (2,))]
    image = summed(flags, (far_own, near_a, near_b), plan, (NEAR_BAND,), befores, cells, 2, 1)
    image, far_over = lax.optimization_barrier((image, far_over))
    befores = summed(flags, far_sums[2] + (first_far_b, far_over), far_sums[1], (FAR_BAND,), None, cells, 2, 0)
    blocks = (far_own, near_a, near_b, far_a, far_b)
    return summed(flags, blocks, plan + far_plan, (FAR_BAND,), befores, cells, 2, 2, image)


def solution(mesh):
    in_specs = (P(None, "freq", "slab", None, None), P(None, "freq", "slab", None, None))
    out_specs = P("freq", None, "slab", None)
    return jax.shard_map(body, mesh=mesh, in_specs=in_specs, out_specs=out_specs, check_vma=False)
```

```python
import functools

import jax
import jax.numpy as jnp
from jax import lax
from jax.experimental import pallas as pl
from jax.experimental.pallas import tpu as pltpu
from jax.sharding import PartitionSpec as P

HMAX = 32
OFFSETS = 2 * HMAX + 1
GROUPS = 4
ROWS = 16
LANES = 128
TX = 8
TH = 4
SLOTS = 4
CHUNKS = 4
NEAR = HMAX // 2


def regroup_kernel(group_ref, source_ref, receiver_ref, *refs):
    out_refs, (held, sems) = refs[:GROUPS], refs[GROUPS:]
    freqs, cells = source_ref.shape[1], source_ref.shape[2]
    share = cells // CHUNKS

    def fetch(field, chunk):
        ref = (source_ref, receiver_ref)[field]
        part = pl.ds(chunk * share, share)
        return pltpu.make_async_copy(ref.at[:, :, part], held.at[field, :, :, part], sems.at[field, chunk])

    for chunk in range(CHUNKS):
        for field in range(2):
            fetch(field, chunk).start()

    def regroup(order):
        low = lax.broadcasted_iota(jnp.int32, (8, LANES), 0) < 4
        for chunk in range(CHUNKS):
            for field in range(2):
                fetch(field, chunk).wait()

                def one_cell(x, _):
                    for f in range(freqs):
                        parts = [[None, None] for _ in range(GROUPS)]
                        for c in range(2):
                            near = held[field, c, f, x, :, :LANES].astype(jnp.float32)
                            far = held[field, c, f, x, :, LANES:].astype(jnp.float32)
                            for pair in range(2):
                                a = near[8 * pair : 8 * pair + 8]
                                b = far[8 * pair : 8 * pair + 8]
                                parts[2 * pair][c] = jnp.where(low, a, pltpu.roll(b, 4, 0))
                                parts[2 * pair + 1][c] = jnp.where(low, pltpu.roll(a, 4, 0), b)
                        for d in range(GROUPS):
                            out_refs[d][field, f, x] = jnp.concatenate(parts[order ^ d], axis=0).astype(jnp.bfloat16)
                    return 0

                lax.fori_loop(chunk * share, (chunk + 1) * share, one_cell, 0, unroll=2)

    for order in range(GROUPS):
        pl.when(group_ref[0] == order)(functools.partial(regroup, order))


def regrouped(group, source_field, receiver_field):
    two, freqs, cells, _, _ = source_field.shape
    return pl.pallas_call(
        regroup_kernel,
        in_specs=[pl.BlockSpec(memory_space=pltpu.SMEM)] + [pl.BlockSpec(memory_space=pl.ANY)] * 2,
        out_specs=[pl.BlockSpec(memory_space=pltpu.VMEM)] * GROUPS,
        out_shape=[pltpu.VMEM((2, freqs, cells, ROWS, LANES), jnp.bfloat16)] * GROUPS,
        scratch_shapes=[pltpu.VMEM((2, 2, freqs, cells, 16, 2 * LANES), jnp.bfloat16), pltpu.SemaphoreType.DMA((2, CHUNKS))],
        compiler_params=pltpu.CompilerParams(vmem_limit_bytes=12 << 20),
        cost_estimate=pl.CostEstimate(flops=0, bytes_accessed=4 << 20, transcendentals=0),
        name="regroup",
    )(group, *(pltpu.with_memory_space_constraint(x, pltpu.HBM) for x in (source_field, receiver_field)))


def by_parity(flags_ref, choice):
    if isinstance(choice, int):
        return choice
    return jnp.where(flags_ref[0] == 0, choice[0], choice[1])


def pack_kernel(copies, refs_in, *refs):
    flags_ref, ins, outs = refs[0], refs[1 : 1 + refs_in], refs[1 + refs_in :]
    for crosses, source, part, at, out, slot in copies:

        def copy(source=source, part=part, at=at, out=out, slot=slot):
            start = by_parity(flags_ref, at)

            def one_cell(x, _):
                for field in range(2):
                    for f in range(outs[out].shape[2]):
                        where = (field, f, start + x) if part is None else (part, field, f, start + x)
                        outs[out][slot, field, f, x] = ins[source][where]
                return 0

            lax.fori_loop(0, outs[out].shape[3], one_cell, 0, unroll=4)

        if crosses is None:
            copy()
        else:
            pl.when((flags_ref[1] == 1) == crosses)(copy)


def pack(flags, arrays, copies, shapes):
    vmem = pl.BlockSpec(memory_space=pltpu.VMEM)
    return pl.pallas_call(
        functools.partial(pack_kernel, copies, len(arrays)),
        in_specs=[pl.BlockSpec(memory_space=pltpu.SMEM)] + [vmem] * len(arrays),
        out_specs=[vmem] * len(shapes),
        out_shape=[jax.ShapeDtypeStruct(shape, jnp.bfloat16) for shape in shapes],
        compiler_params=pltpu.CompilerParams(vmem_limit_bytes=12 << 20),
        cost_estimate=pl.CostEstimate(flops=0, bytes_accessed=2 << 20, transcendentals=0),
        name="pack",
    )(flags, *arrays)


def sum_kernel(plan, bands, first, last, flags_ref, *refs):
    count = 1 + max(entry[0] for entry in plan if entry[0] is not None)
    blocks, refs = refs[:count], refs[count:]
    befores = ()
    if not first:
        befores, refs = refs[: len(bands)], refs[len(bands) :]
    if last == 2:
        refs = refs[1:]
    outs = refs[: 1 if last else len(bands)]
    fields = refs[len(outs)]
    if last:
        turn, stage, sems = refs[len(outs) + 1 :]
        out_ref = outs[0]
    cells = stage.shape[4 - 1] if last else outs[0].shape[1]
    total_freqs = fields.shape[2]

    def fill(index, part, at, length, to, group):
        start, to = by_parity(flags_ref, at), by_parity(flags_ref, to)

        def one_cell(x, _):
            for field in range(2):
                for f in range(2):
                    if index is None:
                        value = jnp.zeros((ROWS, LANES), jnp.float32)
                    elif part is None:
                        value = blocks[index][field, f, start + x].astype(jnp.float32)
                    else:
                        value = blocks[index][part, field, f, start + x].astype(jnp.float32)
                    fields[field, to + x, 2 * group + f] = value
            return 0

        lax.fori_loop(0, length, one_cell, 0, unroll=4)

    for index, part, at, length, to, group, values in plan:
        place = functools.partial(fill, index, part, at, length, to, group)
        if values is None:
            place()
        else:
            pl.when(functools.reduce(jnp.logical_or, [flags_ref[1] == value for value in values]))(place)

    def tile(before, out, k0, row0, rows, x0, slot):
        s0 = x0 + 2 * HMAX - k0 - (rows - 1)
        r0 = x0 + k0
        if first:
            total = [[None] * TX for _ in range(rows)]
        else:
            total = [[before[row0 + j, x0 + i] for i in range(TX)] for j in range(rows)]
        for f in range(total_freqs):
            for c in range(2):
                s = [fields[0, s0 + i, f, 8 * c : 8 * c + 8] for i in range(TX + rows - 1)]
                r = [fields[1, r0 + i, f, 8 * c : 8 * c + 8] for i in range(TX + rows - 1)]
                for j in range(rows):
                    for i in range(TX):
                        product = s[i + rows - 1 - j] * r[i + j]
                        total[j][i] = product if total[j][i] is None else total[j][i] + product
        for j in range(rows):
            if not last:
                for i in range(TX):
                    out[row0 + j, x0 + i] = total[j][i]
                continue
            for i in range(TX):
                turn[j, pl.ds(i, 8, stride=TX)] = 0.25 * total[j][i]
            for zh in range(2):
                for y in range(4):
                    row = zh * 4 + y
                    stage[slot, y, j, pl.ds(pl.multiple_of(x0, TX), TX), zh * LANES : (zh + 1) * LANES] = turn[
                        j, row * TX : (row + 1) * TX
                    ]

    def out_copy(k0, rows, slot):
        return pltpu.make_async_copy(stage.at[slot, :, pl.ds(0, rows)], out_ref.at[:, pl.ds(k0, rows)], sems.at[slot])

    for band, (k_first, steps, jump_at, jump, rest) in enumerate(bands):
        before = befores[band] if befores else None
        out = None if last else outs[band]

        def first_row(step):
            k0 = k_first + TH * step
            return k0 if not jump else k0 + jnp.where(step >= jump_at, jump, 0)

        def rows_of(k0, row0, rows, slot):
            def x_step(xt, _):
                tile(before, out, k0, row0, rows, xt * TX, slot)
                return 0

            lax.fori_loop(0, cells // TX, x_step, 0)

        def h_step(step, _):
            slot = lax.rem(step, SLOTS)
            if last:

                @pl.when(step >= SLOTS)
                def _():
                    out_copy(first_row(step - SLOTS), TH, slot).wait()

            rows_of(first_row(step), TH * step, TH, slot)
            if last:
                out_copy(first_row(step), TH, slot).start()
            return 0

        lax.fori_loop(0, steps, h_step, 0)
        if rest:
            slot = steps % SLOTS
            k0 = k_first + TH * steps
            if last:
                out_copy(first_row(steps - SLOTS), TH, slot).wait()
            rows_of(k0, TH * steps, rest, slot)
            if last:
                out_copy(k0, rest, slot).start()
        if last:
            for step in range(steps - SLOTS + (1 if rest else 0), steps):
                out_copy(first_row(step), TH, step % SLOTS).wait()
            if rest:
                out_copy(k_first + TH * steps, rest, steps % SLOTS).wait()


NEAR_BAND = (HMAX - NEAR, 2 * NEAR // TH, 0, 0, 1)
FAR_BAND = (0, 2 * NEAR // TH, NEAR // TH, 2 * NEAR + 1, 0)


def summed(flags, blocks, plan, bands, befores, cells, groups, last, image=None):
    first = befores is None
    heights = [TH * band[1] + band[4] for band in bands]
    scratch = [pltpu.VMEM((2, 3 * cells, 2 * groups, ROWS, LANES), jnp.float32)]
    vmem = pl.BlockSpec(memory_space=pltpu.VMEM)
    hbm = pl.BlockSpec(memory_space=pl.ANY)
    operands = list(blocks) + ([] if first else list(befores))
    in_specs = [pl.BlockSpec(memory_space=pltpu.SMEM)] + [vmem] * len(operands)
    aliases = {}
    if last:
        scratch += [
            pltpu.VMEM((TH, 8 * TX, LANES), jnp.float32),
            pltpu.VMEM((SLOTS, 4, TH, cells, 2 * LANES), jnp.float32),
            pltpu.SemaphoreType.DMA((SLOTS,)),
        ]
        out_shape = jax.ShapeDtypeStruct((4, OFFSETS, cells, 2 * LANES), jnp.float32)
        out_specs = hbm
        if last == 2:
            operands.append(image)
            in_specs.append(hbm)
            aliases = {len(operands): 0}
    else:
        out_shape = [pltpu.VMEM((height, cells, 8, LANES), jnp.float32) for height in heights]
        out_specs = [vmem] * len(heights)
    return pl.pallas_call(
        functools.partial(sum_kernel, plan, bands, first, last),
        in_specs=in_specs,
        out_specs=out_specs,
        out_shape=out_shape,
        scratch_shapes=scratch,
        input_output_aliases=aliases,
        compiler_params=pltpu.CompilerParams(vmem_limit_bytes=24 << 20),
        cost_estimate=pl.CostEstimate(
            flops=260_000 * groups * sum(heights), bytes_accessed=130_000 * sum(heights), transcendentals=0
        ),
        name="image" if last else "partial",
    )(flags, *operands)


def body(source_field, receiver_field):
    slabs = lax.axis_size("slab")
    middle = slabs // 2
    cells, freqs = source_field.shape[2], source_field.shape[1]
    group = lax.axis_index("freq").astype(jnp.int32)
    slab = lax.axis_index("slab")
    beyond = jnp.where((slab == 0) | (slab == slabs - 1), 2, 0)
    beyond = jnp.where((slab == middle) | (slab == middle - 1), 1, beyond)
    flags = jnp.stack([slab % 2, beyond]).astype(jnp.int32)
    parts = regrouped(group[None], source_field, receiver_field)

    def swap(part, d):
        return lax.ppermute(part, "freq", [(g, g ^ d) for g in range(GROUPS)])

    def trade(value, partner, turned=()):
        pairs = []
        for s in range(slabs):
            for g in range(GROUPS):
                pairs.append((s * GROUPS + g, partner(s) * GROUPS + (g ^ 2 if s in turned else g)))
        return lax.ppermute(value, ("slab", "freq"), pairs)

    def side_a(s):
        return s ^ 1

    def side_b(s):
        return min(max(s + 1 if s % 2 else s - 1, 0), slabs - 1)

    def side_b_of_half(s):
        return s // middle * middle + (s + 1 if s % 2 else s - 1) % middle

    one, other = swap(parts[1], 1), swap(parts[3], 1)

    whole, half = [(2, 2, freqs, length, ROWS, LANES) for length in (cells, NEAR)]
    rest = cells - NEAR
    copies = []
    for slot in range(2):
        copies += [(None, slot, None, 0, 0, slot), (None, 2 + slot, None, 0, 1, slot)]
        copies += [(None, slot, None, (0, rest), 2, slot), (None, slot, None, (rest, 0), 3, slot)]
    own, turned_own, near_b, far_b = pack(flags, (parts[0], one, parts[2], other), copies, (whole,) * 2 + (half,) * 2)
    far_own = swap(turned_own, 2)
    whole_a = trade(own, side_a)
    first_near_b, first_far_b = trade(near_b, side_b_of_half), trade(far_b, side_b_of_half)
    over_middle = [(0, middle), (slabs - 1, middle - 1)]
    near_over, far_over = [lax.ppermute(value, "slab", over_middle) for value in (first_near_b, first_far_b)]

    copies = []
    for slot in range(2):
        for out, at in ((0, (rest, 0)), (2, (0, rest))):
            copies.append((None, 0, slot, at, out, slot))
        for out, at in ((1, (0, rest)), (3, (rest, 0))):
            copies += [(False, 0, slot, at, out, slot), (True, 1, slot, at, out, slot)]
    near_a, near_b, far_a, far_b = pack(flags, (far_own, turned_own), copies, (half,) * 4)
    turned = (middle - 1, middle)
    near_a, near_b = trade(near_a, side_a), trade(near_b, side_b, turned)
    whole_a, first_near_b, first_far_b, far_a, far_b = lax.optimization_barrier(
        (whole_a, first_near_b, first_far_b, far_a, far_b)
    )
    far_a, far_b = trade(far_a, side_a), trade(far_b, side_b, turned)

    near_at_a, near_at_b = (2 * cells, rest), (rest, 2 * cells)
    far_at_a, far_at_b = (2 * cells + NEAR, 0), (0, 2 * cells + NEAR)
    plan, far_plan = [], []
    for g in range(2):
        plan += [(0, g, 0, cells, cells, g, None), (1, g, (0, rest), NEAR, near_at_a, g, None)]
        plan += [(2, g, 0, NEAR, near_at_b, g, (0,)), (3, g, 0, NEAR, near_at_b, g, (1,))]
        plan += [(None, g, 0, NEAR, near_at_b, g, (2,))]
        far_plan += [(1, g, (rest, 0), NEAR, far_at_a, g, None)]
        far_plan += [(4, g, 0, NEAR, far_at_b, g, (0,)), (5, g, 0, NEAR, far_at_b, g, (1,))]
        far_plan += [(None, g, 0, NEAR, far_at_b, g, (2,))]
    blocks = (own, whole_a, first_near_b, near_over)
    befores = summed(flags, blocks, plan, (NEAR_BAND,), None, cells, 2, 0)
    far_over, *befores = lax.optimization_barrier((far_over, *befores))
    far_sums = (flags, plan + far_plan, blocks)
    plan, far_plan = [], []
    for g in range(2):
        plan += [(0, g, 0, cells, cells, g, None), (1, g, 0, NEAR, near_at_a, g, None)]
        plan += [(2, g, 0, NEAR, near_at_b, g, (0, 1)), (None, g, 0, NEAR, near_at_b, g, (2,))]
        far_plan += [(3, g, 0, NEAR, far_at_a, g, None)]
        far_plan += [(4, g, 0, NEAR, far_at_b, g, (0, 1)), (None, g, 0, NEAR, far_at_b, g, (2,))]
    far_befores = summed(flags, far_sums[2] + (first_far_b, far_over), far_sums[1], (FAR_BAND,), None, cells, 2, 0)
    image = summed(flags, (far_own, near_a, near_b), plan, (NEAR_BAND,), befores, cells, 2, 1)
    blocks = (far_own, near_a, near_b, far_a, far_b)
    return summed(flags, blocks, plan + far_plan, (FAR_BAND,), far_befores, cells, 2, 2, image)


def solution(mesh):
    in_specs = (P(None, "freq", "slab", None, None), P(None, "freq", "slab", None, None))
    out_specs = P("freq", None, "slab", None)
    return jax.shard_map(body, mesh=mesh, in_specs=in_specs, out_specs=out_specs, check_vma=False)
```

```python
import functools

import jax
import jax.numpy as jnp
from jax import lax
from jax.experimental import pallas as pl
from jax.experimental.pallas import tpu as pltpu
from jax.sharding import PartitionSpec as P

HMAX = 32
OFFSETS = 2 * HMAX + 1
GROUPS = 4
ROWS = 16
LANES = 128
TX = 8
TH = 4
SLOTS = 4
ORDER = (0, 2, 1, 3)
CHUNKS = 4


def regroup_kernel(group_ref, source_ref, receiver_ref, *refs):
    out_refs, (held, sems) = refs[:GROUPS], refs[GROUPS:]
    freqs, cells = source_ref.shape[1], source_ref.shape[2]
    share = cells // CHUNKS

    def fetch(field, chunk):
        ref = (source_ref, receiver_ref)[field]
        part = pl.ds(chunk * share, share)
        return pltpu.make_async_copy(ref.at[:, :, part], held.at[field, :, :, part], sems.at[field, chunk])

    for chunk in range(CHUNKS):
        for field in range(2):
            fetch(field, chunk).start()

    def regroup(order):
        low = lax.broadcasted_iota(jnp.int32, (8, LANES), 0) < 4
        for chunk in range(CHUNKS):
            for field in range(2):
                fetch(field, chunk).wait()

                def one_cell(x, _):
                    for f in range(freqs):
                        parts = [[None, None] for _ in range(GROUPS)]
                        for c in range(2):
                            near = held[field, c, f, x, :, :LANES].astype(jnp.float32)
                            far = held[field, c, f, x, :, LANES:].astype(jnp.float32)
                            for pair in range(2):
                                a = near[8 * pair : 8 * pair + 8]
                                b = far[8 * pair : 8 * pair + 8]
                                parts[2 * pair][c] = jnp.where(low, a, pltpu.roll(b, 4, 0))
                                parts[2 * pair + 1][c] = jnp.where(low, pltpu.roll(a, 4, 0), b)
                        for d in range(GROUPS):
                            out_refs[d][field, f, x] = jnp.concatenate(parts[order ^ d], axis=0).astype(jnp.bfloat16)
                    return 0

                lax.fori_loop(chunk * share, (chunk + 1) * share, one_cell, 0, unroll=2)

    for order in range(GROUPS):
        pl.when(group_ref[0] == order)(functools.partial(regroup, order))


def regrouped(group, source_field, receiver_field):
    two, freqs, cells, _, _ = source_field.shape
    return pl.pallas_call(
        regroup_kernel,
        in_specs=[pl.BlockSpec(memory_space=pltpu.SMEM)] + [pl.BlockSpec(memory_space=pl.ANY)] * 2,
        out_specs=[pl.BlockSpec(memory_space=pltpu.VMEM)] * GROUPS,
        out_shape=[pltpu.VMEM((2, freqs, cells, ROWS, LANES), jnp.bfloat16)] * GROUPS,
        scratch_shapes=[pltpu.VMEM((2, 2, freqs, cells, 16, 2 * LANES), jnp.bfloat16), pltpu.SemaphoreType.DMA((2, CHUNKS))],
        compiler_params=pltpu.CompilerParams(vmem_limit_bytes=12 << 20),
        cost_estimate=pl.CostEstimate(flops=0, bytes_accessed=4 << 20, transcendentals=0),
        name="regroup",
    )(group, *(pltpu.with_memory_space_constraint(x, pltpu.HBM) for x in (source_field, receiver_field)))


def by_parity(flags_ref, choice):
    if isinstance(choice, int):
        return choice
    return jnp.where(flags_ref[0] == 0, choice[0], choice[1])


def choose_kernel(flags_ref, usual_ref, crossing_ref, out_ref):
    cells = out_ref.shape[2]

    def copy(ref):
        def one_cell(x, _):
            for field in range(2):
                for f in range(out_ref.shape[1]):
                    out_ref[field, f, x] = ref[field, f, x]
            return 0

        lax.fori_loop(0, cells, one_cell, 0, unroll=4)

    pl.when(flags_ref[1] != 1)(functools.partial(copy, usual_ref))
    pl.when(flags_ref[1] == 1)(functools.partial(copy, crossing_ref))


def choose(flags, usual, crossing):
    vmem = pl.BlockSpec(memory_space=pltpu.VMEM)
    return pl.pallas_call(
        choose_kernel,
        in_specs=[pl.BlockSpec(memory_space=pltpu.SMEM), vmem, vmem],
        out_specs=vmem,
        out_shape=jax.ShapeDtypeStruct(usual.shape, jnp.bfloat16),
        compiler_params=pltpu.CompilerParams(vmem_limit_bytes=12 << 20),
        cost_estimate=pl.CostEstimate(flops=0, bytes_accessed=1 << 20, transcendentals=0),
        name="choose",
    )(flags, usual, crossing)


def sum_kernel(plan, bands, first, last, flags_ref, *refs):
    count = 1 + max(entry[0] for entry in plan if entry[0] is not None)
    blocks, refs = refs[:count], refs[count:]
    befores = ()
    if not first:
        befores, refs = refs[: len(bands)], refs[len(bands) :]
    outs = refs[: 1 if last else len(bands)]
    fields = refs[len(outs)]
    if last:
        turn, stage, sems = refs[len(outs) + 1 :]
        out_ref = outs[0]
    cells = stage.shape[4 - 1] if last else outs[0].shape[1]
    total_freqs = fields.shape[2]

    def fill(index, part, at, length, to, group):
        start, to = by_parity(flags_ref, at), by_parity(flags_ref, to)

        def one_cell(x, _):
            for field in range(2):
                for f in range(2):
                    if index is None:
                        value = jnp.zeros((ROWS, LANES), jnp.float32)
                    elif part is None:
                        value = blocks[index][field, f, start + x].astype(jnp.float32)
                    else:
                        value = blocks[index][part, field, f, start + x].astype(jnp.float32)
                    fields[field, to + x, 2 * group + f] = value
            return 0

        lax.fori_loop(0, length, one_cell, 0, unroll=4)

    for index, part, at, length, to, group, values in plan:
        place = functools.partial(fill, index, part, at, length, to, group)
        if values is None:
            place()
        else:
            pl.when(functools.reduce(jnp.logical_or, [flags_ref[1] == value for value in values]))(place)

    def tile(before, out, k0, row0, rows, x0, slot):
        s0 = x0 + 2 * HMAX - k0 - (rows - 1)
        r0 = x0 + k0
        if first:
            total = [[None] * TX for _ in range(rows)]
        else:
            total = [[before[row0 + j, x0 + i] for i in range(TX)] for j in range(rows)]
        for f in range(total_freqs):
            for c in range(2):
                s = [fields[0, s0 + i, f, 8 * c : 8 * c + 8] for i in range(TX + rows - 1)]
                r = [fields[1, r0 + i, f, 8 * c : 8 * c + 8] for i in range(TX + rows - 1)]
                for j in range(rows):
                    for i in range(TX):
                        product = s[i + rows - 1 - j] * r[i + j]
                        total[j][i] = product if total[j][i] is None else total[j][i] + product
        for j in range(rows):
            if not last:
                for i in range(TX):
                    out[row0 + j, x0 + i] = total[j][i]
                continue
            for i in range(TX):
                turn[j, pl.ds(i, 8, stride=TX)] = 0.25 * total[j][i]
            for zh in range(2):
                for y in range(4):
                    row = zh * 4 + y
                    stage[slot, y, j, pl.ds(pl.multiple_of(x0, TX), TX), zh * LANES : (zh + 1) * LANES] = turn[
                        j, row * TX : (row + 1) * TX
                    ]

    def out_copy(k0, rows, slot):
        return pltpu.make_async_copy(stage.at[slot, :, pl.ds(0, rows)], out_ref.at[:, pl.ds(k0, rows)], sems.at[slot])

    for band, (k_first, steps, jump_at, jump, rest) in enumerate(bands):
        before = befores[band] if befores else None
        out = None if last else outs[band]

        def first_row(step):
            k0 = k_first + TH * step
            return k0 if not jump else k0 + jnp.where(step >= jump_at, jump, 0)

        def rows_of(k0, row0, rows, slot):
            def x_step(xt, _):
                tile(before, out, k0, row0, rows, xt * TX, slot)
                return 0

            lax.fori_loop(0, cells // TX, x_step, 0)

        def h_step(step, _):
            slot = lax.rem(step, SLOTS)
            if last:

                @pl.when(step >= SLOTS)
                def _():
                    out_copy(first_row(step - SLOTS), TH, slot).wait()

            rows_of(first_row(step), TH * step, TH, slot)
            if last:
                out_copy(first_row(step), TH, slot).start()
            return 0

        lax.fori_loop(0, steps, h_step, 0)
        if rest:
            slot = steps % SLOTS
            k0 = k_first + TH * steps
            if last:
                out_copy(first_row(steps - SLOTS), TH, slot).wait()
            rows_of(k0, TH * steps, rest, slot)
            if last:
                out_copy(k0, rest, slot).start()
        if last:
            for step in range(steps - SLOTS + (1 if rest else 0), steps):
                out_copy(first_row(step), TH, step % SLOTS).wait()
            if rest:
                out_copy(k_first + TH * steps, rest, steps % SLOTS).wait()


ALL_ROWS = (0, OFFSETS // TH, 0, 0, OFFSETS % TH)


def summed(flags, blocks, plan, before, cells, groups, last):
    first = before is None
    bands, befores = (ALL_ROWS,), None if first else (before,)
    heights = [TH * band[1] + band[4] for band in bands]
    scratch = [pltpu.VMEM((2, 3 * cells, 2 * groups, ROWS, LANES), jnp.float32)]
    vmem = pl.BlockSpec(memory_space=pltpu.VMEM)
    hbm = pl.BlockSpec(memory_space=pl.ANY)
    operands = list(blocks) + ([] if first else list(befores))
    in_specs = [pl.BlockSpec(memory_space=pltpu.SMEM)] + [vmem] * len(operands)
    aliases = {}
    if last:
        scratch += [
            pltpu.VMEM((TH, 8 * TX, LANES), jnp.float32),
            pltpu.VMEM((SLOTS, 4, TH, cells, 2 * LANES), jnp.float32),
            pltpu.SemaphoreType.DMA((SLOTS,)),
        ]
        out_shape = jax.ShapeDtypeStruct((4, OFFSETS, cells, 2 * LANES), jnp.float32)
        out_specs = hbm
    else:
        out_shape = [pltpu.VMEM((height, cells, 8, LANES), jnp.float32) for height in heights]
        out_specs = [vmem] * len(heights)
        aliases = {} if first else {len(operands): 0}
    result = pl.pallas_call(
        functools.partial(sum_kernel, plan, bands, first, last),
        in_specs=in_specs,
        out_specs=out_specs,
        out_shape=out_shape,
        scratch_shapes=scratch,
        input_output_aliases=aliases,
        compiler_params=pltpu.CompilerParams(vmem_limit_bytes=24 << 20),
        cost_estimate=pl.CostEstimate(
            flops=260_000 * groups * sum(heights), bytes_accessed=130_000 * sum(heights), transcendentals=0
        ),
        name="image" if last else "partial",
    )(flags, *operands)
    return result if last else result[0]


def body(source_field, receiver_field):
    slabs = lax.axis_size("slab")
    middle = slabs // 2
    cells = source_field.shape[2]
    group = lax.axis_index("freq").astype(jnp.int32)
    slab = lax.axis_index("slab")
    beyond = jnp.where((slab == 0) | (slab == slabs - 1), 2, 0)
    beyond = jnp.where((slab == middle) | (slab == middle - 1), 1, beyond)
    flags = jnp.stack([slab % 2, beyond]).astype(jnp.int32)
    parts = regrouped(group[None], source_field, receiver_field)

    def swap(part, d):
        return lax.ppermute(part, "freq", [(g, g ^ d) for g in range(GROUPS)])

    def trade(value, partner, turn=0):
        pairs = []
        for s in range(slabs):
            for g in range(GROUPS):
                to = g ^ turn if s in (middle - 1, middle) else g
                pairs.append((s * GROUPS + g, partner(s) * GROUPS + to))
        return lax.ppermute(value, ("slab", "freq"), pairs)

    def side_a(s):
        return s ^ 1

    def side_b(s):
        return min(max(s + 1 if s % 2 else s - 1, 0), slabs - 1)

    def side_b_of_half(s):
        return s // middle * middle + (s + 1 if s % 2 else s - 1) % middle

    owned = [parts[0]] + [swap(parts[d], d) for d in range(1, GROUPS)]
    over_middle = [(0, middle), (slabs - 1, middle - 1)]
    at_a, at_b = (2 * cells, 0), (0, 2 * cells)
    traded = []
    for d in range(GROUPS):
        if d >= 2:
            sent_b = choose(flags, owned[d], parts[d])
            traded.append([trade(owned[d], side_a), trade(sent_b, side_b, d)])
        else:
            traded.append([trade(owned[d], side_a), trade(owned[d], side_b_of_half)])
            traded[d].append(lax.ppermute(traded[d][1], "slab", over_middle))
    total = None
    for d in ORDER:
        plan = [(0, None, 0, cells, cells, 0, None), (1, None, 0, cells, at_a, 0, None)]
        if d >= 2:
            plan += [(2, None, 0, cells, at_b, 0, (0, 1))]
        else:
            plan += [(2, None, 0, cells, at_b, 0, (0,)), (3, None, 0, cells, at_b, 0, (1,))]
        plan += [(None, None, 0, cells, at_b, 0, (2,))]
        total = summed(flags, (owned[d], *traded[d]), plan, total, cells, 1, d == ORDER[-1])
    return total


def solution(mesh):
    in_specs = (P(None, "freq", "slab", None, None), P(None, "freq", "slab", None, None))
    out_specs = P("freq", None, "slab", None)
    return jax.shard_map(body, mesh=mesh, in_specs=in_specs, out_specs=out_specs, check_vma=False)
```

```python
import functools

import jax
import jax.numpy as jnp
from jax import lax
from jax.experimental import pallas as pl
from jax.experimental.pallas import tpu as pltpu
from jax.sharding import PartitionSpec as P

HMAX = 32
OFFSETS = 2 * HMAX + 1
GROUPS = 4
ROWS = 16
LANES = 128
TX = 8
TH = 4
SLOTS = 4
ORDER = (2, 0, 1, 3)
CHUNKS = 4


def regroup_kernel(group_ref, source_ref, receiver_ref, *refs):
    out_refs, (held, sems) = refs[:GROUPS], refs[GROUPS:]
    freqs, cells = source_ref.shape[1], source_ref.shape[2]
    share = cells // CHUNKS

    def fetch(field, chunk):
        ref = (source_ref, receiver_ref)[field]
        part = pl.ds(chunk * share, share)
        return pltpu.make_async_copy(ref.at[:, :, part], held.at[field, :, :, part], sems.at[field, chunk])

    for chunk in range(CHUNKS):
        for field in range(2):
            fetch(field, chunk).start()

    def regroup(order):
        low = lax.broadcasted_iota(jnp.int32, (8, LANES), 0) < 4
        for chunk in range(CHUNKS):
            for field in range(2):
                fetch(field, chunk).wait()

                def one_cell(x, _):
                    for f in range(freqs):
                        parts = [[None, None] for _ in range(GROUPS)]
                        for c in range(2):
                            near = held[field, c, f, x, :, :LANES].astype(jnp.float32)
                            far = held[field, c, f, x, :, LANES:].astype(jnp.float32)
                            for pair in range(2):
                                a = near[8 * pair : 8 * pair + 8]
                                b = far[8 * pair : 8 * pair + 8]
                                parts[2 * pair][c] = jnp.where(low, a, pltpu.roll(b, 4, 0))
                                parts[2 * pair + 1][c] = jnp.where(low, pltpu.roll(a, 4, 0), b)
                        for d in range(GROUPS):
                            out_refs[d][field, f, x] = jnp.concatenate(parts[order ^ d], axis=0).astype(jnp.bfloat16)
                    return 0

                lax.fori_loop(chunk * share, (chunk + 1) * share, one_cell, 0, unroll=2)

    for order in range(GROUPS):
        pl.when(group_ref[0] == order)(functools.partial(regroup, order))


def regrouped(group, source_field, receiver_field):
    two, freqs, cells, _, _ = source_field.shape
    return pl.pallas_call(
        regroup_kernel,
        in_specs=[pl.BlockSpec(memory_space=pltpu.SMEM)] + [pl.BlockSpec(memory_space=pl.ANY)] * 2,
        out_specs=[pl.BlockSpec(memory_space=pltpu.VMEM)] * GROUPS,
        out_shape=[pltpu.VMEM((2, freqs, cells, ROWS, LANES), jnp.bfloat16)] * GROUPS,
        scratch_shapes=[pltpu.VMEM((2, 2, freqs, cells, 16, 2 * LANES), jnp.bfloat16), pltpu.SemaphoreType.DMA((2, CHUNKS))],
        compiler_params=pltpu.CompilerParams(vmem_limit_bytes=12 << 20),
        cost_estimate=pl.CostEstimate(flops=0, bytes_accessed=4 << 20, transcendentals=0),
        name="regroup",
    )(group, *(pltpu.with_memory_space_constraint(x, pltpu.HBM) for x in (source_field, receiver_field)))


def by_parity(flags_ref, choice):
    if isinstance(choice, int):
        return choice
    return jnp.where(flags_ref[0] == 0, choice[0], choice[1])


def choose_kernel(flags_ref, usual_ref, crossing_ref, out_ref):
    cells = out_ref.shape[2]

    def copy(ref):
        def one_cell(x, _):
            for field in range(2):
                for f in range(out_ref.shape[1]):
                    out_ref[field, f, x] = ref[field, f, x]
            return 0

        lax.fori_loop(0, cells, one_cell, 0, unroll=4)

    pl.when(flags_ref[1] != 1)(functools.partial(copy, usual_ref))
    pl.when(flags_ref[1] == 1)(functools.partial(copy, crossing_ref))


def choose(flags, usual, crossing):
    vmem = pl.BlockSpec(memory_space=pltpu.VMEM)
    return pl.pallas_call(
        choose_kernel,
        in_specs=[pl.BlockSpec(memory_space=pltpu.SMEM), vmem, vmem],
        out_specs=vmem,
        out_shape=jax.ShapeDtypeStruct(usual.shape, jnp.bfloat16),
        compiler_params=pltpu.CompilerParams(vmem_limit_bytes=12 << 20),
        cost_estimate=pl.CostEstimate(flops=0, bytes_accessed=1 << 20, transcendentals=0),
        name="choose",
    )(flags, usual, crossing)


def sum_kernel(plan, bands, first, last, flags_ref, *refs):
    count = 1 + max(entry[0] for entry in plan if entry[0] is not None)
    blocks, refs = refs[:count], refs[count:]
    befores = ()
    if not first:
        befores, refs = refs[: len(bands)], refs[len(bands) :]
    outs = refs[: 1 if last else len(bands)]
    fields = refs[len(outs)]
    if last:
        turn, stage, sems = refs[len(outs) + 1 :]
        out_ref = outs[0]
    cells = stage.shape[4 - 1] if last else outs[0].shape[1]
    total_freqs = fields.shape[2]

    def fill(index, part, at, length, to, group):
        start, to = by_parity(flags_ref, at), by_parity(flags_ref, to)

        def one_cell(x, _):
            for field in range(2):
                for f in range(2):
                    if index is None:
                        value = jnp.zeros((ROWS, LANES), jnp.float32)
                    elif part is None:
                        value = blocks[index][field, f, start + x].astype(jnp.float32)
                    else:
                        value = blocks[index][part, field, f, start + x].astype(jnp.float32)
                    fields[field, to + x, 2 * group + f] = value
            return 0

        lax.fori_loop(0, length, one_cell, 0, unroll=4)

    for index, part, at, length, to, group, values in plan:
        place = functools.partial(fill, index, part, at, length, to, group)
        if values is None:
            place()
        else:
            pl.when(functools.reduce(jnp.logical_or, [flags_ref[1] == value for value in values]))(place)

    def tile(before, out, k0, row0, rows, x0, slot):
        s0 = x0 + 2 * HMAX - k0 - (rows - 1)
        r0 = x0 + k0
        if first:
            total = [[None] * TX for _ in range(rows)]
        else:
            total = [[before[row0 + j, x0 + i] for i in range(TX)] for j in range(rows)]
        for f in range(total_freqs):
            for c in range(2):
                s = [fields[0, s0 + i, f, 8 * c : 8 * c + 8] for i in range(TX + rows - 1)]
                r = [fields[1, r0 + i, f, 8 * c : 8 * c + 8] for i in range(TX + rows - 1)]
                for j in range(rows):
                    for i in range(TX):
                        product = s[i + rows - 1 - j] * r[i + j]
                        total[j][i] = product if total[j][i] is None else total[j][i] + product
        for j in range(rows):
            if not last:
                for i in range(TX):
                    out[row0 + j, x0 + i] = total[j][i]
                continue
            for i in range(TX):
                turn[j, pl.ds(i, 8, stride=TX)] = 0.25 * total[j][i]
            for zh in range(2):
                for y in range(4):
                    row = zh * 4 + y
                    stage[slot, y, j, pl.ds(pl.multiple_of(x0, TX), TX), zh * LANES : (zh + 1) * LANES] = turn[
                        j, row * TX : (row + 1) * TX
                    ]

    def out_copy(k0, rows, slot):
        return pltpu.make_async_copy(stage.at[slot, :, pl.ds(0, rows)], out_ref.at[:, pl.ds(k0, rows)], sems.at[slot])

    for band, (k_first, steps, jump_at, jump, rest) in enumerate(bands):
        before = befores[band] if befores else None
        out = None if last else outs[band]

        def first_row(step):
            k0 = k_first + TH * step
            return k0 if not jump else k0 + jnp.where(step >= jump_at, jump, 0)

        def rows_of(k0, row0, rows, slot):
            def x_step(xt, _):
                tile(before, out, k0, row0, rows, xt * TX, slot)
                return 0

            lax.fori_loop(0, cells // TX, x_step, 0)

        def h_step(step, _):
            slot = lax.rem(step, SLOTS)
            if last:

                @pl.when(step >= SLOTS)
                def _():
                    out_copy(first_row(step - SLOTS), TH, slot).wait()

            rows_of(first_row(step), TH * step, TH, slot)
            if last:
                out_copy(first_row(step), TH, slot).start()
            return 0

        lax.fori_loop(0, steps, h_step, 0)
        if rest:
            slot = steps % SLOTS
            k0 = k_first + TH * steps
            if last:
                out_copy(first_row(steps - SLOTS), TH, slot).wait()
            rows_of(k0, TH * steps, rest, slot)
            if last:
                out_copy(k0, rest, slot).start()
        if last:
            for step in range(steps - SLOTS + (1 if rest else 0), steps):
                out_copy(first_row(step), TH, step % SLOTS).wait()
            if rest:
                out_copy(k_first + TH * steps, rest, steps % SLOTS).wait()


ALL_ROWS = (0, OFFSETS // TH, 0, 0, OFFSETS % TH)


def summed(flags, blocks, plan, before, cells, groups, last):
    first = before is None
    bands, befores = (ALL_ROWS,), None if first else (before,)
    heights = [TH * band[1] + band[4] for band in bands]
    scratch = [pltpu.VMEM((2, 3 * cells, 2 * groups, ROWS, LANES), jnp.float32)]
    vmem = pl.BlockSpec(memory_space=pltpu.VMEM)
    hbm = pl.BlockSpec(memory_space=pl.ANY)
    operands = list(blocks) + ([] if first else list(befores))
    in_specs = [pl.BlockSpec(memory_space=pltpu.SMEM)] + [vmem] * len(operands)
    aliases = {}
    if last:
        scratch += [
            pltpu.VMEM((TH, 8 * TX, LANES), jnp.float32),
            pltpu.VMEM((SLOTS, 4, TH, cells, 2 * LANES), jnp.float32),
            pltpu.SemaphoreType.DMA((SLOTS,)),
        ]
        out_shape = jax.ShapeDtypeStruct((4, OFFSETS, cells, 2 * LANES), jnp.float32)
        out_specs = hbm
    else:
        out_shape = [pltpu.VMEM((height, cells, 8, LANES), jnp.float32) for height in heights]
        out_specs = [vmem] * len(heights)
        aliases = {} if first else {len(operands): 0}
    result = pl.pallas_call(
        functools.partial(sum_kernel, plan, bands, first, last),
        in_specs=in_specs,
        out_specs=out_specs,
        out_shape=out_shape,
        scratch_shapes=scratch,
        input_output_aliases=aliases,
        compiler_params=pltpu.CompilerParams(vmem_limit_bytes=24 << 20),
        cost_estimate=pl.CostEstimate(
            flops=260_000 * groups * sum(heights), bytes_accessed=130_000 * sum(heights), transcendentals=0
        ),
        name="image" if last else "partial",
    )(flags, *operands)
    return result if last else result[0]


def body(source_field, receiver_field):
    slabs = lax.axis_size("slab")
    middle = slabs // 2
    cells = source_field.shape[2]
    group = lax.axis_index("freq").astype(jnp.int32)
    slab = lax.axis_index("slab")
    beyond = jnp.where((slab == 0) | (slab == slabs - 1), 2, 0)
    beyond = jnp.where((slab == middle) | (slab == middle - 1), 1, beyond)
    flags = jnp.stack([slab % 2, beyond]).astype(jnp.int32)
    parts = regrouped(group[None], source_field, receiver_field)

    def swap(part, d):
        return lax.ppermute(part, "freq", [(g, g ^ d) for g in range(GROUPS)])

    def trade(value, partner, turn=0):
        pairs = []
        for s in range(slabs):
            for g in range(GROUPS):
                to = g ^ turn if s in (middle - 1, middle) else g
                pairs.append((s * GROUPS + g, partner(s) * GROUPS + to))
        return lax.ppermute(value, ("slab", "freq"), pairs)

    def side_a(s):
        return s ^ 1

    def side_b(s):
        return min(max(s + 1 if s % 2 else s - 1, 0), slabs - 1)

    def side_b_of_half(s):
        return s // middle * middle + (s + 1 if s % 2 else s - 1) % middle

    owned = [parts[0]] + [swap(parts[d], d) for d in range(1, GROUPS)]
    over_middle = [(0, middle), (slabs - 1, middle - 1)]
    at_a, at_b = (2 * cells, 0), (0, 2 * cells)
    traded = []
    for d in range(GROUPS):
        if d < 2:
            traded.append([trade(owned[d], side_a), trade(owned[d], side_b_of_half)])
            continue
        sent_a, sent_b = owned[d], choose(flags, owned[d], parts[d])
        sent_a, traded[d - 2][0] = lax.optimization_barrier((sent_a, traded[d - 2][0]))
        sent_b, traded[d - 2][1] = lax.optimization_barrier((sent_b, traded[d - 2][1]))
        traded.append([trade(sent_a, side_a), trade(sent_b, side_b, d)])
    over_0, owned[3], *traded[1] = lax.optimization_barrier((traded[0][1], owned[3], *traded[1]))
    over_1, *traded[2] = lax.optimization_barrier((traded[1][1], *traded[2]))
    for d, value in enumerate((over_0, over_1)):
        traded[d].append(lax.ppermute(value, "slab", over_middle))
    total = None
    for d in ORDER:
        plan = [(0, None, 0, cells, cells, 0, None), (1, None, 0, cells, at_a, 0, None)]
        if d >= 2:
            plan += [(2, None, 0, cells, at_b, 0, (0, 1))]
        else:
            plan += [(2, None, 0, cells, at_b, 0, (0,)), (3, None, 0, cells, at_b, 0, (1,))]
        plan += [(None, None, 0, cells, at_b, 0, (2,))]
        total = summed(flags, (owned[d], *traded[d]), plan, total, cells, 1, d == ORDER[-1])
    return total


def solution(mesh):
    in_specs = (P(None, "freq", "slab", None, None), P(None, "freq", "slab", None, None))
    out_specs = P("freq", None, "slab", None)
    return jax.shard_map(body, mesh=mesh, in_specs=in_specs, out_specs=out_specs, check_vma=False)
```

```python
import functools

import jax
import jax.numpy as jnp
from jax import lax
from jax.experimental import pallas as pl
from jax.experimental.pallas import tpu as pltpu
from jax.sharding import PartitionSpec as P

HMAX = 32
OFFSETS = 2 * HMAX + 1
GROUPS = 4
ROWS = 16
LANES = 128
TX = 8
TH = 4
SLOTS = 4
CHUNKS = 4
NEAR = HMAX // 2


def regroup_kernel(group_ref, source_ref, receiver_ref, *refs):
    out_refs, (held, sems) = refs[:GROUPS], refs[GROUPS:]
    freqs, cells = source_ref.shape[1], source_ref.shape[2]
    share = cells // CHUNKS

    def fetch(field, chunk):
        ref = (source_ref, receiver_ref)[field]
        part = pl.ds(chunk * share, share)
        return pltpu.make_async_copy(ref.at[:, :, part], held.at[field, :, :, part], sems.at[field, chunk])

    for chunk in range(CHUNKS):
        for field in range(2):
            fetch(field, chunk).start()

    def regroup(order):
        low = lax.broadcasted_iota(jnp.int32, (8, LANES), 0) < 4
        for chunk in range(CHUNKS):
            for field in range(2):
                fetch(field, chunk).wait()

                def one_cell(x, _):
                    for f in range(freqs):
                        parts = [[None, None] for _ in range(GROUPS)]
                        for c in range(2):
                            near = held[field, c, f, x, :, :LANES].astype(jnp.float32)
                            far = held[field, c, f, x, :, LANES:].astype(jnp.float32)
                            for pair in range(2):
                                a = near[8 * pair : 8 * pair + 8]
                                b = far[8 * pair : 8 * pair + 8]
                                parts[2 * pair][c] = jnp.where(low, a, pltpu.roll(b, 4, 0))
                                parts[2 * pair + 1][c] = jnp.where(low, pltpu.roll(a, 4, 0), b)
                        for d in range(GROUPS):
                            out_refs[d][field, f, x] = jnp.concatenate(parts[order ^ d], axis=0).astype(jnp.bfloat16)
                    return 0

                lax.fori_loop(chunk * share, (chunk + 1) * share, one_cell, 0, unroll=2)

    for order in range(GROUPS):
        pl.when(group_ref[0] == order)(functools.partial(regroup, order))


def regrouped(group, source_field, receiver_field):
    two, freqs, cells, _, _ = source_field.shape
    return pl.pallas_call(
        regroup_kernel,
        in_specs=[pl.BlockSpec(memory_space=pltpu.SMEM)] + [pl.BlockSpec(memory_space=pl.ANY)] * 2,
        out_specs=[pl.BlockSpec(memory_space=pltpu.VMEM)] * GROUPS,
        out_shape=[pltpu.VMEM((2, freqs, cells, ROWS, LANES), jnp.bfloat16)] * GROUPS,
        scratch_shapes=[pltpu.VMEM((2, 2, freqs, cells, 16, 2 * LANES), jnp.bfloat16), pltpu.SemaphoreType.DMA((2, CHUNKS))],
        compiler_params=pltpu.CompilerParams(vmem_limit_bytes=12 << 20),
        cost_estimate=pl.CostEstimate(flops=0, bytes_accessed=4 << 20, transcendentals=0),
        name="regroup",
    )(group, *(pltpu.with_memory_space_constraint(x, pltpu.HBM) for x in (source_field, receiver_field)))


def by_parity(flags_ref, choice):
    if isinstance(choice, int):
        return choice
    return jnp.where(flags_ref[0] == 0, choice[0], choice[1])


def pack_kernel(copies, refs_in, *refs):
    flags_ref, ins, outs = refs[0], refs[1 : 1 + refs_in], refs[1 + refs_in :]
    for crosses, source, part, at, out, slot in copies:

        def copy(source=source, part=part, at=at, out=out, slot=slot):
            start = by_parity(flags_ref, at)

            def one_cell(x, _):
                for field in range(2):
                    for f in range(outs[out].shape[2]):
                        where = (field, f, start + x) if part is None else (part, field, f, start + x)
                        outs[out][slot, field, f, x] = ins[source][where]
                return 0

            lax.fori_loop(0, outs[out].shape[3], one_cell, 0, unroll=4)

        if crosses is None:
            copy()
        else:
            pl.when((flags_ref[1] == 1) == crosses)(copy)


def pack(flags, arrays, copies, shapes):
    vmem = pl.BlockSpec(memory_space=pltpu.VMEM)
    return pl.pallas_call(
        functools.partial(pack_kernel, copies, len(arrays)),
        in_specs=[pl.BlockSpec(memory_space=pltpu.SMEM)] + [vmem] * len(arrays),
        out_specs=[vmem] * len(shapes),
        out_shape=[jax.ShapeDtypeStruct(shape, jnp.bfloat16) for shape in shapes],
        compiler_params=pltpu.CompilerParams(vmem_limit_bytes=12 << 20),
        cost_estimate=pl.CostEstimate(flops=0, bytes_accessed=2 << 20, transcendentals=0),
        name="pack",
    )(flags, *arrays)


def sum_kernel(plan, bands, first, last, crosses, flags_ref, *refs):
    if crosses is None:
        sum_body(plan, bands, first, last, flags_ref, *refs)
    else:
        pl.when((flags_ref[1] == 1) == crosses)(functools.partial(sum_body, plan, bands, first, last, flags_ref, *refs))


def sum_body(plan, bands, first, last, flags_ref, *refs):
    count = 1 + max(entry[0] for entry in plan if entry[0] is not None)
    blocks, refs = refs[:count], refs[count:]
    befores = ()
    if not first:
        befores, refs = refs[: len(bands)], refs[len(bands) :]
    if last in (2, 3):
        refs = refs[1:]
    last = 0 if last == 3 else last
    outs = refs[: 1 if last else len(bands)]
    fields = refs[len(outs)]
    if last:
        turn, stage, sems = refs[len(outs) + 1 :]
        out_ref = outs[0]
    cells = stage.shape[4 - 1] if last else outs[0].shape[1]
    total_freqs = fields.shape[2]

    def fill(index, part, at, length, to, group):
        start, to = by_parity(flags_ref, at), by_parity(flags_ref, to)

        def one_cell(x, _):
            for field in range(2):
                for f in range(2):
                    if index is None:
                        value = jnp.zeros((ROWS, LANES), jnp.float32)
                    elif part is None:
                        value = blocks[index][field, f, start + x].astype(jnp.float32)
                    else:
                        value = blocks[index][part, field, f, start + x].astype(jnp.float32)
                    fields[field, to + x, 2 * group + f] = value
            return 0

        lax.fori_loop(0, length, one_cell, 0, unroll=4)

    for index, part, at, length, to, group, values in plan:
        place = functools.partial(fill, index, part, at, length, to, group)
        if values is None:
            place()
        else:
            pl.when(functools.reduce(jnp.logical_or, [flags_ref[1] == value for value in values]))(place)

    def tile(before, out, k0, row0, rows, x0, slot):
        s0 = x0 + 2 * HMAX - k0 - (rows - 1)
        r0 = x0 + k0
        if first:
            total = [[None] * TX for _ in range(rows)]
        else:
            total = [[before[row0 + j, x0 + i] for i in range(TX)] for j in range(rows)]
        for f in range(total_freqs):
            for c in range(2):
                s = [fields[0, s0 + i, f, 8 * c : 8 * c + 8] for i in range(TX + rows - 1)]
                r = [fields[1, r0 + i, f, 8 * c : 8 * c + 8] for i in range(TX + rows - 1)]
                for j in range(rows):
                    for i in range(TX):
                        product = s[i + rows - 1 - j] * r[i + j]
                        total[j][i] = product if total[j][i] is None else total[j][i] + product
        for j in range(rows):
            if not last:
                for i in range(TX):
                    out[row0 + j, x0 + i] = total[j][i]
                continue
            for i in range(TX):
                turn[j, pl.ds(i, 8, stride=TX)] = 0.25 * total[j][i]
            for zh in range(2):
                for y in range(4):
                    row = zh * 4 + y
                    stage[slot, y, j, pl.ds(pl.multiple_of(x0, TX), TX), zh * LANES : (zh + 1) * LANES] = turn[
                        j, row * TX : (row + 1) * TX
                    ]

    def out_copy(k0, rows, slot):
        return pltpu.make_async_copy(stage.at[slot, :, pl.ds(0, rows)], out_ref.at[:, pl.ds(k0, rows)], sems.at[slot])

    for band, (k_first, steps, jump_at, jump, rest) in enumerate(bands):
        before = befores[band] if befores else None
        out = None if last else outs[band]

        def first_row(step):
            k0 = k_first + TH * step
            return k0 if not jump else k0 + jnp.where(step >= jump_at, jump, 0)

        def rows_of(k0, row0, rows, slot):
            def x_step(xt, _):
                tile(before, out, k0, row0, rows, xt * TX, slot)
                return 0

            lax.fori_loop(0, cells // TX, x_step, 0)

        def h_step(step, _):
            slot = lax.rem(step, SLOTS)
            if last:

                @pl.when(step >= SLOTS)
                def _():
                    out_copy(first_row(step - SLOTS), TH, slot).wait()

            rows_of(first_row(step), TH * step, TH, slot)
            if last:
                out_copy(first_row(step), TH, slot).start()
            return 0

        lax.fori_loop(0, steps, h_step, 0)
        if rest:
            slot = steps % SLOTS
            k0 = k_first + TH * steps
            if last:
                out_copy(first_row(steps - SLOTS), TH, slot).wait()
            rows_of(k0, TH * steps, rest, slot)
            if last:
                out_copy(k0, rest, slot).start()
        if last:
            for step in range(steps - SLOTS + (1 if rest else 0), steps):
                out_copy(first_row(step), TH, step % SLOTS).wait()
            if rest:
                out_copy(k_first + TH * steps, rest, steps % SLOTS).wait()


NEAR_BAND = (HMAX - NEAR, 2 * NEAR // TH, 0, 0, 1)
FAR_BAND = (0, 2 * NEAR // TH, NEAR // TH, 2 * NEAR + 1, 0)


def summed(flags, blocks, plan, bands, befores, cells, groups, last, image=None, crosses=None):
    first = befores is None
    heights = [TH * band[1] + band[4] for band in bands]
    scratch = [pltpu.VMEM((2, 3 * cells, 2 * groups, ROWS, LANES), jnp.float32)]
    vmem = pl.BlockSpec(memory_space=pltpu.VMEM)
    hbm = pl.BlockSpec(memory_space=pl.ANY)
    operands = list(blocks) + ([] if first else list(befores))
    in_specs = [pl.BlockSpec(memory_space=pltpu.SMEM)] + [vmem] * len(operands)
    aliases = {}
    if last:
        scratch += [
            pltpu.VMEM((TH, 8 * TX, LANES), jnp.float32),
            pltpu.VMEM((SLOTS, 4, TH, cells, 2 * LANES), jnp.float32),
            pltpu.SemaphoreType.DMA((SLOTS,)),
        ]
        out_shape = jax.ShapeDtypeStruct((4, OFFSETS, cells, 2 * LANES), jnp.float32)
        out_specs = hbm
        if last == 2:
            operands.append(image)
            in_specs.append(hbm)
            aliases = {len(operands): 0}
    else:
        out_shape = [pltpu.VMEM((height, cells, 8, LANES), jnp.float32) for height in heights]
        out_specs = [vmem] * len(heights)
        if image is not None:
            operands.append(image)
            in_specs.append(vmem)
            aliases = {len(operands): 0}
    return pl.pallas_call(
        functools.partial(sum_kernel, plan, bands, first, last or (0 if image is None else 3), crosses),
        in_specs=in_specs,
        out_specs=out_specs,
        out_shape=out_shape,
        scratch_shapes=scratch,
        input_output_aliases=aliases,
        compiler_params=pltpu.CompilerParams(vmem_limit_bytes=24 << 20),
        cost_estimate=pl.CostEstimate(
            flops=260_000 * groups * sum(heights), bytes_accessed=130_000 * sum(heights), transcendentals=0
        ),
        name="image" if last else "partial",
    )(flags, *operands)


def body(source_field, receiver_field):
    slabs = lax.axis_size("slab")
    middle = slabs // 2
    cells, freqs = source_field.shape[2], source_field.shape[1]
    group = lax.axis_index("freq").astype(jnp.int32)
    slab = lax.axis_index("slab")
    beyond = jnp.where((slab == 0) | (slab == slabs - 1), 2, 0)
    beyond = jnp.where((slab == middle) | (slab == middle - 1), 1, beyond)
    flags = jnp.stack([slab % 2, beyond]).astype(jnp.int32)
    parts = regrouped(group[None], source_field, receiver_field)

    def swap(part, d):
        return lax.ppermute(part, "freq", [(g, g ^ d) for g in range(GROUPS)])

    def trade(value, partner, turned=()):
        pairs = []
        for s in range(slabs):
            for g in range(GROUPS):
                pairs.append((s * GROUPS + g, partner(s) * GROUPS + (g ^ 2 if s in turned else g)))
        return lax.ppermute(value, ("slab", "freq"), pairs)

    def side_a(s):
        return s ^ 1

    def side_b(s):
        return min(max(s + 1 if s % 2 else s - 1, 0), slabs - 1)

    def side_b_of_half(s):
        return s // middle * middle + (s + 1 if s % 2 else s - 1) % middle

    one, other = swap(parts[1], 1), swap(parts[3], 1)

    whole, half = [(2, 2, freqs, length, ROWS, LANES) for length in (cells, NEAR)]
    rest = cells - NEAR
    copies = []
    for slot in range(2):
        copies += [(None, slot, None, 0, 0, slot), (None, 2 + slot, None, 0, 1, slot)]
        copies += [(None, slot, None, (0, rest), 2, slot), (None, slot, None, (rest, 0), 3, slot)]
    own, turned_own, near_b, far_b = pack(flags, (parts[0], one, parts[2], other), copies, (whole,) * 2 + (half,) * 2)
    far_own = swap(turned_own, 2)
    whole_a = trade(own, side_a)
    first_near_b, first_far_b = trade(near_b, side_b_of_half), trade(far_b, side_b_of_half)
    over_middle = [(0, middle), (slabs - 1, middle - 1)]
    near_over, far_over = [lax.ppermute(value, "slab", over_middle) for value in (first_near_b, first_far_b)]

    copies = []
    for slot in range(2):
        for out, at in ((0, (rest, 0)), (2, (0, rest))):
            copies.append((None, 0, slot, at, out, slot))
        for out, at in ((1, (0, rest)), (3, (rest, 0))):
            copies += [(False, 0, slot, at, out, slot), (True, 1, slot, at, out, slot)]
    near_a, near_b, far_a, far_b = pack(flags, (far_own, turned_own), copies, (half,) * 4)
    turned = (middle - 1, middle)
    near_a, near_b = trade(near_a, side_a), trade(near_b, side_b, turned)
    whole_a, first_near_b, first_far_b, far_a, far_b = lax.optimization_barrier(
        (whole_a, first_near_b, first_far_b, far_a, far_b)
    )

    near_at_a, near_at_b = (2 * cells, rest), (rest, 2 * cells)
    far_at_a, far_at_b = (2 * cells + NEAR, 0), (0, 2 * cells + NEAR)
    plan, far_plan = [], []
    for g in range(2):
        plan += [(0, g, 0, cells, cells, g, None), (1, g, (0, rest), NEAR, near_at_a, g, None)]
        plan += [(2, g, 0, NEAR, near_at_b, g, (0,)), (3, g, 0, NEAR, near_at_b, g, (1,))]
        plan += [(None, g, 0, NEAR, near_at_b, g, (2,))]
        far_plan += [(1, g, (rest, 0), NEAR, far_at_a, g, None)]
        far_plan += [(4, g, 0, NEAR, far_at_b, g, (0,)), (5, g, 0, NEAR, far_at_b, g, (1,))]
        far_plan += [(None, g, 0, NEAR, far_at_b, g, (2,))]
    blocks = (own, whole_a, first_near_b, near_over)
    befores = summed(flags, blocks, plan, (NEAR_BAND,), None, cells, 2, 0)
    far_b, *befores = lax.optimization_barrier((far_b, *befores))
    far_a, far_b = trade(far_a, side_a), trade(far_b, side_b, turned)
    usual = [entry for entry in plan + far_plan if entry[-1] != (1,) and entry[0] != 3]
    usual = [(3 if entry[0] == 4 else entry[0], *entry[1:]) for entry in usual]
    far_blocks, far_plan = blocks + (first_far_b, far_over), plan + far_plan
    far_befores = summed(flags, blocks[:3] + (first_far_b,), usual, (FAR_BAND,), None, cells, 2, 0, None, False)
    crossing = (far_blocks, far_plan)
    plan, far_plan = [], []
    for g in range(2):
        plan += [(0, g, 0, cells, cells, g, None), (1, g, 0, NEAR, near_at_a, g, None)]
        plan += [(2, g, 0, NEAR, near_at_b, g, (0, 1)), (None, g, 0, NEAR, near_at_b, g, (2,))]
        far_plan += [(3, g, 0, NEAR, far_at_a, g, None)]
        far_plan += [(4, g, 0, NEAR, far_at_b, g, (0, 1)), (None, g, 0, NEAR, far_at_b, g, (2,))]
    image = summed(flags, (far_own, near_a, near_b), plan, (NEAR_BAND,), befores, cells, 2, 1)
    image, far_over = lax.optimization_barrier((image, far_over))
    far_blocks = crossing[0][:-1] + (far_over,)
    befores = summed(flags, far_blocks, crossing[1], (FAR_BAND,), None, cells, 2, 0, far_befores[0], True)
    blocks = (far_own, near_a, near_b, far_a, far_b)
    return summed(flags, blocks, plan + far_plan, (FAR_BAND,), befores, cells, 2, 2, image)


def solution(mesh):
    in_specs = (P(None, "freq", "slab", None, None), P(None, "freq", "slab", None, None))
    out_specs = P("freq", None, "slab", None)
    return jax.shard_map(body, mesh=mesh, in_specs=in_specs, out_specs=out_specs, check_vma=False)
```

```python
import functools

import jax
import jax.numpy as jnp
from jax import lax
from jax.experimental import pallas as pl
from jax.experimental.pallas import tpu as pltpu
from jax.sharding import PartitionSpec as P

HMAX = 32
OFFSETS = 2 * HMAX + 1
GROUPS = 4
ROWS = 16
LANES = 128
TX = 8
TH = 4
SLOTS = 4
CHUNKS = 4
NEAR = HMAX // 2


def regroup_kernel(group_ref, source_ref, receiver_ref, *refs):
    out_refs, (held, sems) = refs[:GROUPS], refs[GROUPS:]
    freqs, cells = source_ref.shape[1], source_ref.shape[2]
    share = cells // CHUNKS

    def fetch(field, chunk):
        ref = (source_ref, receiver_ref)[field]
        part = pl.ds(chunk * share, share)
        return pltpu.make_async_copy(ref.at[:, :, part], held.at[field, :, :, part], sems.at[field, chunk])

    for chunk in range(CHUNKS):
        for field in range(2):
            fetch(field, chunk).start()

    def regroup(order):
        low = lax.broadcasted_iota(jnp.int32, (8, LANES), 0) < 4
        for chunk in range(CHUNKS):
            for field in range(2):
                fetch(field, chunk).wait()

                def one_cell(x, _):
                    for f in range(freqs):
                        parts = [[None, None] for _ in range(GROUPS)]
                        for c in range(2):
                            near = held[field, c, f, x, :, :LANES].astype(jnp.float32)
                            far = held[field, c, f, x, :, LANES:].astype(jnp.float32)
                            for pair in range(2):
                                a = near[8 * pair : 8 * pair + 8]
                                b = far[8 * pair : 8 * pair + 8]
                                parts[2 * pair][c] = jnp.where(low, a, pltpu.roll(b, 4, 0))
                                parts[2 * pair + 1][c] = jnp.where(low, pltpu.roll(a, 4, 0), b)
                        for d in range(GROUPS):
                            out_refs[d][field, f, x] = jnp.concatenate(parts[order ^ d], axis=0).astype(jnp.bfloat16)
                    return 0

                lax.fori_loop(chunk * share, (chunk + 1) * share, one_cell, 0, unroll=2)

    for order in range(GROUPS):
        pl.when(group_ref[0] == order)(functools.partial(regroup, order))


def regrouped(group, source_field, receiver_field):
    two, freqs, cells, _, _ = source_field.shape
    return pl.pallas_call(
        regroup_kernel,
        in_specs=[pl.BlockSpec(memory_space=pltpu.SMEM)] + [pl.BlockSpec(memory_space=pl.ANY)] * 2,
        out_specs=[pl.BlockSpec(memory_space=pltpu.VMEM)] * GROUPS,
        out_shape=[pltpu.VMEM((2, freqs, cells, ROWS, LANES), jnp.bfloat16)] * GROUPS,
        scratch_shapes=[pltpu.VMEM((2, 2, freqs, cells, 16, 2 * LANES), jnp.bfloat16), pltpu.SemaphoreType.DMA((2, CHUNKS))],
        compiler_params=pltpu.CompilerParams(vmem_limit_bytes=12 << 20),
        cost_estimate=pl.CostEstimate(flops=0, bytes_accessed=4 << 20, transcendentals=0),
        name="regroup",
    )(group, *(pltpu.with_memory_space_constraint(x, pltpu.HBM) for x in (source_field, receiver_field)))


def by_parity(flags_ref, choice):
    if isinstance(choice, int):
        return choice
    return jnp.where(flags_ref[0] == 0, choice[0], choice[1])


def pack_kernel(copies, refs_in, *refs):
    flags_ref, ins, outs = refs[0], refs[1 : 1 + refs_in], refs[1 + refs_in :]
    for crosses, source, part, at, out, slot in copies:

        def copy(source=source, part=part, at=at, out=out, slot=slot):
            start = by_parity(flags_ref, at)

            def one_cell(x, _):
                for field in range(2):
                    for f in range(outs[out].shape[2]):
                        where = (field, f, start + x) if part is None else (part, field, f, start + x)
                        outs[out][slot, field, f, x] = ins[source][where]
                return 0

            lax.fori_loop(0, outs[out].shape[3], one_cell, 0, unroll=4)

        if crosses is None:
            copy()
        else:
            pl.when((flags_ref[1] == 1) == crosses)(copy)


def pack(flags, arrays, copies, shapes):
    vmem = pl.BlockSpec(memory_space=pltpu.VMEM)
    return pl.pallas_call(
        functools.partial(pack_kernel, copies, len(arrays)),
        in_specs=[pl.BlockSpec(memory_space=pltpu.SMEM)] + [vmem] * len(arrays),
        out_specs=[vmem] * len(shapes),
        out_shape=[jax.ShapeDtypeStruct(shape, jnp.bfloat16) for shape in shapes],
        compiler_params=pltpu.CompilerParams(vmem_limit_bytes=12 << 20),
        cost_estimate=pl.CostEstimate(flops=0, bytes_accessed=2 << 20, transcendentals=0),
        name="pack",
    )(flags, *arrays)


def sum_kernel(plan, bands, first, last, flags_ref, *refs):
    count = 1 + max(entry[0] for entry in plan if entry[0] is not None)
    blocks, refs = refs[:count], refs[count:]
    befores = ()
    if not first:
        befores, refs = refs[: len(bands)], refs[len(bands) :]
    if last == 2:
        refs = refs[1:]
    outs = refs[: 1 if last else len(bands)]
    fields = refs[len(outs)]
    if last:
        turn, stage, sems = refs[len(outs) + 1 :]
        out_ref = outs[0]
    cells = stage.shape[4 - 1] if last else outs[0].shape[1]
    total_freqs = fields.shape[2]

    def fill(index, part, at, length, to, group):
        start, to = by_parity(flags_ref, at), by_parity(flags_ref, to)

        def one_cell(x, _):
            for field in range(2):
                for f in range(2):
                    if index is None:
                        value = jnp.zeros((ROWS, LANES), jnp.float32)
                    elif part is None:
                        value = blocks[index][field, f, start + x].astype(jnp.float32)
                    else:
                        value = blocks[index][part, field, f, start + x].astype(jnp.float32)
                    fields[field, to + x, 2 * group + f] = value
            return 0

        lax.fori_loop(0, length, one_cell, 0, unroll=4)

    for index, part, at, length, to, group, values in plan:
        place = functools.partial(fill, index, part, at, length, to, group)
        if values is None:
            place()
        else:
            pl.when(functools.reduce(jnp.logical_or, [flags_ref[1] == value for value in values]))(place)

    def tile(before, out, k0, row0, rows, x0, slot):
        s0 = x0 + 2 * HMAX - k0 - (rows - 1)
        r0 = x0 + k0
        if first:
            total = [[None] * TX for _ in range(rows)]
        else:
            total = [[before[row0 + j, x0 + i] for i in range(TX)] for j in range(rows)]
        for f in range(total_freqs):
            for c in range(2):
                s = [fields[0, s0 + i, f, 8 * c : 8 * c + 8] for i in range(TX + rows - 1)]
                r = [fields[1, r0 + i, f, 8 * c : 8 * c + 8] for i in range(TX + rows - 1)]
                for j in range(rows):
                    for i in range(TX):
                        product = s[i + rows - 1 - j] * r[i + j]
                        total[j][i] = product if total[j][i] is None else total[j][i] + product
        for j in range(rows):
            if not last:
                for i in range(TX):
                    out[row0 + j, x0 + i] = total[j][i]
                continue
            for i in range(TX):
                turn[j, pl.ds(i, 8, stride=TX)] = 0.25 * total[j][i]
            for zh in range(2):
                for y in range(4):
                    row = zh * 4 + y
                    stage[slot, y, j, pl.ds(pl.multiple_of(x0, TX), TX), zh * LANES : (zh + 1) * LANES] = turn[
                        j, row * TX : (row + 1) * TX
                    ]

    def out_copy(k0, rows, slot):
        return pltpu.make_async_copy(stage.at[slot, :, pl.ds(0, rows)], out_ref.at[:, pl.ds(k0, rows)], sems.at[slot])

    for band, (k_first, steps, jump_at, jump, rest) in enumerate(bands):
        before = befores[band] if befores else None
        out = None if last else outs[band]

        def first_row(step):
            k0 = k_first + TH * step
            return k0 if not jump else k0 + jnp.where(step >= jump_at, jump, 0)

        def rows_of(k0, row0, rows, slot):
            def x_step(xt, _):
                tile(before, out, k0, row0, rows, xt * TX, slot)
                return 0

            lax.fori_loop(0, cells // TX, x_step, 0)

        def h_step(step, _):
            slot = lax.rem(step, SLOTS)
            if last:

                @pl.when(step >= SLOTS)
                def _():
                    out_copy(first_row(step - SLOTS), TH, slot).wait()

            rows_of(first_row(step), TH * step, TH, slot)
            if last:
                out_copy(first_row(step), TH, slot).start()
            return 0

        lax.fori_loop(0, steps, h_step, 0)
        if rest:
            slot = steps % SLOTS
            k0 = k_first + TH * steps
            if last:
                out_copy(first_row(steps - SLOTS), TH, slot).wait()
            rows_of(k0, TH * steps, rest, slot)
            if last:
                out_copy(k0, rest, slot).start()
        if last:
            for step in range(steps - SLOTS + (1 if rest else 0), steps):
                out_copy(first_row(step), TH, step % SLOTS).wait()
            if rest:
                out_copy(k_first + TH * steps, rest, steps % SLOTS).wait()


NEAR_BAND = (HMAX - NEAR, 2 * NEAR // TH, 0, 0, 1)
FAR_BAND = (0, 2 * NEAR // TH, NEAR // TH, 2 * NEAR + 1, 0)


def summed(flags, blocks, plan, bands, befores, cells, groups, last, image=None):
    first = befores is None
    heights = [TH * band[1] + band[4] for band in bands]
    scratch = [pltpu.VMEM((2, 3 * cells, 2 * groups, ROWS, LANES), jnp.float32)]
    vmem = pl.BlockSpec(memory_space=pltpu.VMEM)
    hbm = pl.BlockSpec(memory_space=pl.ANY)
    operands = list(blocks) + ([] if first else list(befores))
    in_specs = [pl.BlockSpec(memory_space=pltpu.SMEM)] + [vmem] * len(operands)
    aliases = {}
    if last:
        scratch += [
            pltpu.VMEM((TH, 8 * TX, LANES), jnp.float32),
            pltpu.VMEM((SLOTS, 4, TH, cells, 2 * LANES), jnp.float32),
            pltpu.SemaphoreType.DMA((SLOTS,)),
        ]
        out_shape = jax.ShapeDtypeStruct((4, OFFSETS, cells, 2 * LANES), jnp.float32)
        out_specs = hbm
        if last == 2:
            operands.append(image)
            in_specs.append(hbm)
            aliases = {len(operands): 0}
    else:
        out_shape = [pltpu.VMEM((height, cells, 8, LANES), jnp.float32) for height in heights]
        out_specs = [vmem] * len(heights)
    return pl.pallas_call(
        functools.partial(sum_kernel, plan, bands, first, last),
        in_specs=in_specs,
        out_specs=out_specs,
        out_shape=out_shape,
        scratch_shapes=scratch,
        input_output_aliases=aliases,
        compiler_params=pltpu.CompilerParams(vmem_limit_bytes=24 << 20),
        cost_estimate=pl.CostEstimate(
            flops=260_000 * groups * sum(heights), bytes_accessed=130_000 * sum(heights), transcendentals=0
        ),
        name="image" if last else "partial",
    )(flags, *operands)


def body(source_field, receiver_field):
    slabs = lax.axis_size("slab")
    middle = slabs // 2
    cells, freqs = source_field.shape[2], source_field.shape[1]
    group = lax.axis_index("freq").astype(jnp.int32)
    slab = lax.axis_index("slab")
    beyond = jnp.where((slab == 0) | (slab == slabs - 1), 2, 0)
    beyond = jnp.where((slab == middle) | (slab == middle - 1), 1, beyond)
    flags = jnp.stack([slab % 2, beyond]).astype(jnp.int32)
    parts = regrouped(group[None], source_field, receiver_field)

    def swap(part, d):
        return lax.ppermute(part, "freq", [(g, g ^ d) for g in range(GROUPS)])

    def trade(value, partner, turned=()):
        pairs = []
        for s in range(slabs):
            for g in range(GROUPS):
                pairs.append((s * GROUPS + g, partner(s) * GROUPS + (g ^ 2 if s in turned else g)))
        return lax.ppermute(value, ("slab", "freq"), pairs)

    def side_a(s):
        return s ^ 1

    def side_b(s):
        return min(max(s + 1 if s % 2 else s - 1, 0), slabs - 1)

    def side_b_of_half(s):
        return s // middle * middle + (s + 1 if s % 2 else s - 1) % middle

    one, other = swap(parts[1], 1), swap(parts[3], 1)

    whole, half = [(2, 2, freqs, length, ROWS, LANES) for length in (cells, NEAR)]
    rest = cells - NEAR
    copies = []
    for slot in range(2):
        copies += [(None, slot, None, 0, 0, slot), (None, 2 + slot, None, 0, 1, slot)]
        copies += [(None, slot, None, (0, rest), 2, slot), (None, slot, None, (rest, 0), 3, slot)]
    own, turned_own, near_b, far_b = pack(flags, (parts[0], one, parts[2], other), copies, (whole,) * 2 + (half,) * 2)
    far_own = swap(turned_own, 2)
    whole_a = trade(own, side_a)
    first_near_b, first_far_b = trade(near_b, side_b_of_half), trade(far_b, side_b)
    near_over = lax.ppermute(first_near_b, "slab", [(0, middle), (slabs - 1, middle - 1)])

    copies = []
    for slot in range(2):
        for out, at in ((0, (rest, 0)), (2, (0, rest))):
            copies.append((None, 0, slot, at, out, slot))
        for out, at in ((1, (0, rest)), (3, (rest, 0))):
            copies += [(False, 0, slot, at, out, slot), (True, 1, slot, at, out, slot)]
    near_a, near_b, far_a, far_b = pack(flags, (far_own, turned_own), copies, (half,) * 4)
    turned = (middle - 1, middle)
    near_a, near_b = trade(near_a, side_a), trade(near_b, side_b, turned)
    whole_a, first_near_b, first_far_b, far_a, far_b = lax.optimization_barrier(
        (whole_a, first_near_b, first_far_b, far_a, far_b)
    )
    far_a, far_b = trade(far_a, side_a), trade(far_b, side_b, turned)

    near_at_a, near_at_b = (2 * cells, rest), (rest, 2 * cells)
    far_at_a, far_at_b = (2 * cells + NEAR, 0), (0, 2 * cells + NEAR)
    plan, far_plan = [], []
    for g in range(2):
        plan += [(0, g, 0, cells, cells, g, None), (1, g, (0, rest), NEAR, near_at_a, g, None)]
        plan += [(2, g, 0, NEAR, near_at_b, g, (0,)), (3, g, 0, NEAR, near_at_b, g, (1,))]
        plan += [(None, g, 0, NEAR, near_at_b, g, (2,))]
        far_plan += [(1, g, (rest, 0), NEAR, far_at_a, g, None)]
        far_plan += [(4, g, 0, NEAR, far_at_b, g, (0, 1)), (None, g, 0, NEAR, far_at_b, g, (2,))]
    blocks = (own, whole_a, first_near_b, near_over)
    befores = summed(flags, blocks, plan, (NEAR_BAND,), None, cells, 2, 0)
    far_sums = (flags, plan + far_plan, blocks)
    plan, far_plan = [], []
    for g in range(2):
        plan += [(0, g, 0, cells, cells, g, None), (1, g, 0, NEAR, near_at_a, g, None)]
        plan += [(2, g, 0, NEAR, near_at_b, g, (0, 1)), (None, g, 0, NEAR, near_at_b, g, (2,))]
        far_plan += [(3, g, 0, NEAR, far_at_a, g, None)]
        far_plan += [(4, g, 0, NEAR, far_at_b, g, (0, 1)), (None, g, 0, NEAR, far_at_b, g, (2,))]
    far_befores = summed(flags, far_sums[2] + (first_far_b,), far_sums[1], (FAR_BAND,), None, cells, 2, 0)
    image = summed(flags, (far_own, near_a, near_b), plan, (NEAR_BAND,), befores, cells, 2, 1)
    blocks = (far_own, near_a, near_b, far_a, far_b)
    return summed(flags, blocks, plan + far_plan, (FAR_BAND,), far_befores, cells, 2, 2, image)


def solution(mesh):
    in_specs = (P(None, "freq", "slab", None, None), P(None, "freq", "slab", None, None))
    out_specs = P("freq", None, "slab", None)
    return jax.shard_map(body, mesh=mesh, in_specs=in_specs, out_specs=out_specs, check_vma=False)
```

```python
import functools

import jax
import jax.numpy as jnp
from jax import lax
from jax.experimental import pallas as pl
from jax.experimental.pallas import tpu as pltpu
from jax.sharding import PartitionSpec as P

HMAX = 32
OFFSETS = 2 * HMAX + 1
GROUPS = 4
ROWS = 16
LANES = 128
TX = 8
TH = 4
SLOTS = 4
CHUNKS = 4
NEAR = HMAX // 2


def regroup_kernel(group_ref, source_ref, receiver_ref, *refs):
    out_refs, (held, sems) = refs[:GROUPS], refs[GROUPS:]
    freqs, cells = source_ref.shape[1], source_ref.shape[2]
    share = cells // CHUNKS

    def fetch(field, chunk):
        ref = (source_ref, receiver_ref)[field]
        part = pl.ds(chunk * share, share)
        return pltpu.make_async_copy(ref.at[:, :, part], held.at[field, :, :, part], sems.at[field, chunk])

    for chunk in range(CHUNKS):
        for field in range(2):
            fetch(field, chunk).start()

    def regroup(order):
        low = lax.broadcasted_iota(jnp.int32, (8, LANES), 0) < 4
        for chunk in range(CHUNKS):
            for field in range(2):
                fetch(field, chunk).wait()

                def one_cell(x, _):
                    for f in range(freqs):
                        parts = [[None, None] for _ in range(GROUPS)]
                        for c in range(2):
                            near = held[field, c, f, x, :, :LANES].astype(jnp.float32)
                            far = held[field, c, f, x, :, LANES:].astype(jnp.float32)
                            for pair in range(2):
                                a = near[8 * pair : 8 * pair + 8]
                                b = far[8 * pair : 8 * pair + 8]
                                parts[2 * pair][c] = jnp.where(low, a, pltpu.roll(b, 4, 0))
                                parts[2 * pair + 1][c] = jnp.where(low, pltpu.roll(a, 4, 0), b)
                        for d in range(GROUPS):
                            out_refs[d][field, f, x] = jnp.concatenate(parts[order ^ d], axis=0).astype(jnp.bfloat16)
                    return 0

                lax.fori_loop(chunk * share, (chunk + 1) * share, one_cell, 0, unroll=2)

    for order in range(GROUPS):
        pl.when(group_ref[0] == order)(functools.partial(regroup, order))


def regrouped(group, source_field, receiver_field):
    two, freqs, cells, _, _ = source_field.shape
    return pl.pallas_call(
        regroup_kernel,
        in_specs=[pl.BlockSpec(memory_space=pltpu.SMEM)] + [pl.BlockSpec(memory_space=pl.ANY)] * 2,
        out_specs=[pl.BlockSpec(memory_space=pltpu.VMEM)] * GROUPS,
        out_shape=[pltpu.VMEM((2, freqs, cells, ROWS, LANES), jnp.bfloat16)] * GROUPS,
        scratch_shapes=[pltpu.VMEM((2, 2, freqs, cells, 16, 2 * LANES), jnp.bfloat16), pltpu.SemaphoreType.DMA((2, CHUNKS))],
        compiler_params=pltpu.CompilerParams(vmem_limit_bytes=12 << 20),
        cost_estimate=pl.CostEstimate(flops=0, bytes_accessed=4 << 20, transcendentals=0),
        name="regroup",
    )(group, *(pltpu.with_memory_space_constraint(x, pltpu.HBM) for x in (source_field, receiver_field)))


def by_parity(flags_ref, choice):
    if isinstance(choice, int):
        return choice
    return jnp.where(flags_ref[0] == 0, choice[0], choice[1])


def pack_kernel(copies, refs_in, *refs):
    flags_ref, ins, outs = refs[0], refs[1 : 1 + refs_in], refs[1 + refs_in :]
    for crosses, source, part, at, out, slot in copies:

        def copy(source=source, part=part, at=at, out=out, slot=slot):
            start = by_parity(flags_ref, at)

            def one_cell(x, _):
                for field in range(2):
                    for f in range(outs[out].shape[2]):
                        where = (field, f, start + x) if part is None else (part, field, f, start + x)
                        outs[out][slot, field, f, x] = ins[source][where]
                return 0

            lax.fori_loop(0, outs[out].shape[3], one_cell, 0, unroll=4)

        if crosses is None:
            copy()
        else:
            pl.when((flags_ref[1] == 1) == crosses)(copy)


def pack(flags, arrays, copies, shapes):
    vmem = pl.BlockSpec(memory_space=pltpu.VMEM)
    return pl.pallas_call(
        functools.partial(pack_kernel, copies, len(arrays)),
        in_specs=[pl.BlockSpec(memory_space=pltpu.SMEM)] + [vmem] * len(arrays),
        out_specs=[vmem] * len(shapes),
        out_shape=[jax.ShapeDtypeStruct(shape, jnp.bfloat16) for shape in shapes],
        compiler_params=pltpu.CompilerParams(vmem_limit_bytes=12 << 20),
        cost_estimate=pl.CostEstimate(flops=0, bytes_accessed=2 << 20, transcendentals=0),
        name="pack",
    )(flags, *arrays)


def sum_kernel(variants, count, bands, last, flags_ref, *refs):
    for crosses, plan, first, groups in variants:
        run = functools.partial(sum_body, plan, count, groups, bands, first, last, flags_ref, *refs)
        if crosses is None:
            run()
        else:
            pl.when((flags_ref[1] == 1) == crosses)(run)


def sum_body(plan, count, groups, bands, first, last, flags_ref, *refs):
    blocks, refs = refs[:count], refs[count:]
    befores = ()
    if last:
        befores, refs = refs[: len(bands)], refs[len(bands) :]
    if last == 2:
        refs = refs[1:]
    outs = refs[: 1 if last else len(bands)]
    fields = refs[len(outs)]
    if last:
        turn, stage, sems = refs[len(outs) + 1 :]
        out_ref = outs[0]
    cells = stage.shape[4 - 1] if last else outs[0].shape[1]
    total_freqs = 2 * groups

    def fill(index, part, at, length, to, group):
        start, to = by_parity(flags_ref, at), by_parity(flags_ref, to)

        def one_cell(x, _):
            for field in range(2):
                for f in range(2):
                    if index is None:
                        value = jnp.zeros((ROWS, LANES), jnp.float32)
                    elif part is None:
                        value = blocks[index][field, f, start + x].astype(jnp.float32)
                    else:
                        value = blocks[index][part, field, f, start + x].astype(jnp.float32)
                    fields[field, to + x, 2 * group + f] = value
            return 0

        lax.fori_loop(0, length, one_cell, 0, unroll=4)

    for index, part, at, length, to, group, values in plan:
        place = functools.partial(fill, index, part, at, length, to, group)
        if values is None:
            place()
        else:
            pl.when(functools.reduce(jnp.logical_or, [flags_ref[1] == value for value in values]))(place)

    def tile(before, out, k0, row0, rows, x0, slot):
        s0 = x0 + 2 * HMAX - k0 - (rows - 1)
        r0 = x0 + k0
        if first:
            total = [[None] * TX for _ in range(rows)]
        else:
            total = [[before[row0 + j, x0 + i] for i in range(TX)] for j in range(rows)]
        for f in range(total_freqs):
            for c in range(2):
                s = [fields[0, s0 + i, f, 8 * c : 8 * c + 8] for i in range(TX + rows - 1)]
                r = [fields[1, r0 + i, f, 8 * c : 8 * c + 8] for i in range(TX + rows - 1)]
                for j in range(rows):
                    for i in range(TX):
                        product = s[i + rows - 1 - j] * r[i + j]
                        total[j][i] = product if total[j][i] is None else total[j][i] + product
        for j in range(rows):
            if not last:
                for i in range(TX):
                    out[row0 + j, x0 + i] = total[j][i]
                continue
            for i in range(TX):
                turn[j, pl.ds(i, 8, stride=TX)] = 0.25 * total[j][i]
            for zh in range(2):
                for y in range(4):
                    row = zh * 4 + y
                    stage[slot, y, j, pl.ds(pl.multiple_of(x0, TX), TX), zh * LANES : (zh + 1) * LANES] = turn[
                        j, row * TX : (row + 1) * TX
                    ]

    def out_copy(k0, rows, slot):
        return pltpu.make_async_copy(stage.at[slot, :, pl.ds(0, rows)], out_ref.at[:, pl.ds(k0, rows)], sems.at[slot])

    for band, (k_first, steps, jump_at, jump, rest) in enumerate(bands):
        before = befores[band] if befores else None
        out = None if last else outs[band]

        def first_row(step):
            k0 = k_first + TH * step
            return k0 if not jump else k0 + jnp.where(step >= jump_at, jump, 0)

        def rows_of(k0, row0, rows, slot):
            def x_step(xt, _):
                tile(before, out, k0, row0, rows, xt * TX, slot)
                return 0

            lax.fori_loop(0, cells // TX, x_step, 0)

        def h_step(step, _):
            slot = lax.rem(step, SLOTS)
            if last:

                @pl.when(step >= SLOTS)
                def _():
                    out_copy(first_row(step - SLOTS), TH, slot).wait()

            rows_of(first_row(step), TH * step, TH, slot)
            if last:
                out_copy(first_row(step), TH, slot).start()
            return 0

        lax.fori_loop(0, steps, h_step, 0)
        if rest:
            slot = steps % SLOTS
            k0 = k_first + TH * steps
            if last:
                out_copy(first_row(steps - SLOTS), TH, slot).wait()
            rows_of(k0, TH * steps, rest, slot)
            if last:
                out_copy(k0, rest, slot).start()
        if last:
            for step in range(steps - SLOTS + (1 if rest else 0), steps):
                out_copy(first_row(step), TH, step % SLOTS).wait()
            if rest:
                out_copy(k_first + TH * steps, rest, steps % SLOTS).wait()


NEAR_BAND = (HMAX - NEAR, 2 * NEAR // TH, 0, 0, 1)
FAR_BAND = (0, 2 * NEAR // TH, NEAR // TH, 2 * NEAR + 1, 0)


def summed(flags, blocks, variants, bands, befores, cells, last, image=None):
    heights = [TH * band[1] + band[4] for band in bands]
    groups = max(variant[-1] for variant in variants)
    scratch = [pltpu.VMEM((2, 3 * cells, 2 * groups, ROWS, LANES), jnp.float32)]
    vmem = pl.BlockSpec(memory_space=pltpu.VMEM)
    hbm = pl.BlockSpec(memory_space=pl.ANY)
    operands = list(blocks) + list(befores)
    in_specs = [pl.BlockSpec(memory_space=pltpu.SMEM)] + [vmem] * len(operands)
    aliases = {}
    if last:
        scratch += [
            pltpu.VMEM((TH, 8 * TX, LANES), jnp.float32),
            pltpu.VMEM((SLOTS, 4, TH, cells, 2 * LANES), jnp.float32),
            pltpu.SemaphoreType.DMA((SLOTS,)),
        ]
        out_shape = jax.ShapeDtypeStruct((4, OFFSETS, cells, 2 * LANES), jnp.float32)
        out_specs = hbm
        if last == 2:
            operands.append(image)
            in_specs.append(hbm)
            aliases = {len(operands): 0}
    else:
        out_shape = [pltpu.VMEM((height, cells, 8, LANES), jnp.float32) for height in heights]
        out_specs = [vmem] * len(heights)
    return pl.pallas_call(
        functools.partial(sum_kernel, variants, len(blocks), bands, last),
        in_specs=in_specs,
        out_specs=out_specs,
        out_shape=out_shape,
        scratch_shapes=scratch,
        input_output_aliases=aliases,
        compiler_params=pltpu.CompilerParams(vmem_limit_bytes=32 << 20),
        cost_estimate=pl.CostEstimate(
            flops=520_000 * sum(heights), bytes_accessed=130_000 * sum(heights), transcendentals=0
        ),
        name="image" if last else "partial",
    )(flags, *operands)


def body(source_field, receiver_field):
    slabs = lax.axis_size("slab")
    middle = slabs // 2
    cells, freqs = source_field.shape[2], source_field.shape[1]
    group = lax.axis_index("freq").astype(jnp.int32)
    slab = lax.axis_index("slab")
    beyond = jnp.where((slab == 0) | (slab == slabs - 1), 2, 0)
    beyond = jnp.where((slab == middle) | (slab == middle - 1), 1, beyond)
    flags = jnp.stack([slab % 2, beyond]).astype(jnp.int32)
    parts = regrouped(group[None], source_field, receiver_field)

    def swap(part, d):
        return lax.ppermute(part, "freq", [(g, g ^ d) for g in range(GROUPS)])

    def trade(value, partner, turned=()):
        pairs = []
        for s in range(slabs):
            for g in range(GROUPS):
                pairs.append((s * GROUPS + g, partner(s) * GROUPS + (g ^ 2 if s in turned else g)))
        return lax.ppermute(value, ("slab", "freq"), pairs)

    def side_a(s):
        return s ^ 1

    def side_b(s):
        return min(max(s + 1 if s % 2 else s - 1, 0), slabs - 1)

    def side_b_of_half(s):
        return s // middle * middle + (s + 1 if s % 2 else s - 1) % middle

    one, other = swap(parts[1], 1), swap(parts[3], 1)

    whole, half = [(2, 2, freqs, length, ROWS, LANES) for length in (cells, NEAR)]
    rest = cells - NEAR
    copies = [(None, slot, None, 0, 0, slot) for slot in range(2)]
    (turned_own,) = pack(flags, (parts[2], other), copies, (whole,))
    far_own = swap(turned_own, 2)
    copies = []
    for slot in range(2):
        for out, at in ((0, 0), (1, (0, rest)), (2, (rest, 0))):
            copies.append((None, slot, None, at, out, slot))
    own, near_b, far_b = pack(flags, (parts[0], one), copies, (whole,) + (half,) * 2)
    whole_a = trade(own, side_a)
    first_near_b, first_far_b = trade(near_b, side_b_of_half), trade(far_b, side_b_of_half)
    over_middle = [(0, middle), (slabs - 1, middle - 1)]
    near_over = lax.ppermute(first_near_b, "slab", over_middle)

    copies = []
    for slot in range(2):
        for out, at in ((0, (rest, 0)), (2, (0, rest))):
            copies.append((None, 0, slot, at, out, slot))
        for out, at in ((1, (0, rest)), (3, (rest, 0))):
            copies += [(False, 0, slot, at, out, slot), (True, 1, slot, at, out, slot)]
    near_a, near_b, far_a, far_b = pack(flags, (far_own, turned_own), copies, (half,) * 4)
    turned = (middle - 1, middle)
    near_a, near_b = trade(near_a, side_a), trade(near_b, side_b, turned)
    far_a, far_b = trade(far_a, side_a), trade(far_b, side_b, turned)

    near_at_a, near_at_b = (2 * cells, rest), (rest, 2 * cells)
    far_at_a, far_at_b = (2 * cells + NEAR, 0), (0, 2 * cells + NEAR)
    zero = (None, 0, 0, NEAR)

    def first_groups(own, whole_a, near_b, far_b, near_over, far_over, to, far):
        plan = []
        for g in range(2):
            plan += [(own, g, 0, cells, cells, to + g, None), (whole_a, g, (0, rest), NEAR, near_at_a, to + g, None)]
            plan += [(near_b, g, 0, NEAR, near_at_b, to + g, (0,)), (*zero, near_at_b, to + g, (2,))]
            if near_over is not None:
                plan += [(near_over, g, 0, NEAR, near_at_b, to + g, (1,))]
            if far:
                plan += [(whole_a, g, (rest, 0), NEAR, far_at_a, to + g, None)]
                plan += [(far_b, g, 0, NEAR, far_at_b, to + g, (0,)), (*zero, far_at_b, to + g, (2,))]
                if far_over is not None:
                    plan += [(far_over, g, 0, NEAR, far_at_b, to + g, (1,))]
        return plan

    def last_groups(own, near_a, near_b, far_a, far_b, far):
        plan = []
        for g in range(2):
            plan += [(own, g, 0, cells, cells, g, None), (near_a, g, 0, NEAR, near_at_a, g, None)]
            plan += [(near_b, g, 0, NEAR, near_at_b, g, (0, 1)), (*zero, near_at_b, g, (2,))]
            if far:
                plan += [(far_a, g, 0, NEAR, far_at_a, g, None)]
                plan += [(far_b, g, 0, NEAR, far_at_b, g, (0, 1)), (*zero, far_at_b, g, (2,))]
        return plan

    plan = first_groups(0, 1, 2, None, 3, None, 0, False)
    near_sums = summed(flags, (own, whole_a, first_near_b, near_over), ((None, plan, True, 2),), (NEAR_BAND,), (), cells, 0)
    plan = first_groups(0, 1, 2, 3, None, None, 0, True)
    blocks = (own, whole_a, first_near_b, first_far_b)
    far_sums = summed(flags, blocks, ((False, plan, True, 2),), (FAR_BAND,), (), cells, 0)
    far_over, *far_sums = lax.optimization_barrier((first_far_b, *far_sums))
    far_over = lax.ppermute(far_over, "slab", over_middle)
    plan = last_groups(0, 1, 2, None, None, False)
    image = summed(flags, (far_own, near_a, near_b), ((None, plan, False, 2),), (NEAR_BAND,), near_sums, cells, 1)
    plan = last_groups(0, 1, 2, 3, 4, True)
    crossing = plan + first_groups(5, 6, None, None, 7, 8, 2, True)
    crossing = [entry for entry in crossing if entry[0] is not None or entry[5] < 2]
    crossing = [entry for entry in crossing if entry[-1] != (0,)]
    blocks = (far_own, near_a, near_b, far_a, far_b, own, whole_a, near_over, far_over)
    variants = ((False, plan, False, 2), (True, crossing, True, 4))
    return summed(flags, blocks, variants, (FAR_BAND,), far_sums, cells, 2, image)


def solution(mesh):
    in_specs = (P(None, "freq", "slab", None, None), P(None, "freq", "slab", None, None))
    out_specs = P("freq", None, "slab", None)
    return jax.shard_map(body, mesh=mesh, in_specs=in_specs, out_specs=out_specs, check_vma=False)
```

```python
import functools

import jax
import jax.numpy as jnp
from jax import lax
from jax.experimental import pallas as pl
from jax.experimental.pallas import tpu as pltpu
from jax.sharding import PartitionSpec as P

HMAX = 32
OFFSETS = 2 * HMAX + 1
GROUPS = 4
ROWS = 16
LANES = 128
TX = 8
TH = 4
SLOTS = 4
CHUNKS = 4
NEAR = HMAX // 2


def regroup_kernel(group_ref, source_ref, receiver_ref, *refs):
    out_refs, (held, sems) = refs[:GROUPS], refs[GROUPS:]
    freqs, cells = source_ref.shape[1], source_ref.shape[2]
    share = cells // CHUNKS

    def fetch(field, chunk):
        ref = (source_ref, receiver_ref)[field]
        part = pl.ds(chunk * share, share)
        return pltpu.make_async_copy(ref.at[:, :, part], held.at[field, :, :, part], sems.at[field, chunk])

    for chunk in range(CHUNKS):
        for field in range(2):
            fetch(field, chunk).start()

    def regroup(order):
        low = lax.broadcasted_iota(jnp.int32, (8, LANES), 0) < 4
        for chunk in range(CHUNKS):
            for field in range(2):
                fetch(field, chunk).wait()

                def one_cell(x, _):
                    for f in range(freqs):
                        parts = [[None, None] for _ in range(GROUPS)]
                        for c in range(2):
                            near = held[field, c, f, x, :, :LANES].astype(jnp.float32)
                            far = held[field, c, f, x, :, LANES:].astype(jnp.float32)
                            for pair in range(2):
                                a = near[8 * pair : 8 * pair + 8]
                                b = far[8 * pair : 8 * pair + 8]
                                parts[2 * pair][c] = jnp.where(low, a, pltpu.roll(b, 4, 0))
                                parts[2 * pair + 1][c] = jnp.where(low, pltpu.roll(a, 4, 0), b)
                        for d in range(GROUPS):
                            out_refs[d][field, f, x] = jnp.concatenate(parts[order ^ d], axis=0).astype(jnp.bfloat16)
                    return 0

                lax.fori_loop(chunk * share, (chunk + 1) * share, one_cell, 0, unroll=2)

    for order in range(GROUPS):
        pl.when(group_ref[0] == order)(functools.partial(regroup, order))


def regrouped(group, source_field, receiver_field):
    two, freqs, cells, _, _ = source_field.shape
    return pl.pallas_call(
        regroup_kernel,
        in_specs=[pl.BlockSpec(memory_space=pltpu.SMEM)] + [pl.BlockSpec(memory_space=pl.ANY)] * 2,
        out_specs=[pl.BlockSpec(memory_space=pltpu.VMEM)] * GROUPS,
        out_shape=[pltpu.VMEM((2, freqs, cells, ROWS, LANES), jnp.bfloat16)] * GROUPS,
        scratch_shapes=[pltpu.VMEM((2, 2, freqs, cells, 16, 2 * LANES), jnp.bfloat16), pltpu.SemaphoreType.DMA((2, CHUNKS))],
        compiler_params=pltpu.CompilerParams(vmem_limit_bytes=12 << 20),
        cost_estimate=pl.CostEstimate(flops=0, bytes_accessed=4 << 20, transcendentals=0),
        name="regroup",
    )(group, *(pltpu.with_memory_space_constraint(x, pltpu.HBM) for x in (source_field, receiver_field)))


def by_parity(flags_ref, choice):
    if isinstance(choice, int):
        return choice
    return jnp.where(flags_ref[0] == 0, choice[0], choice[1])


def pack_kernel(copies, refs_in, *refs):
    flags_ref, ins, outs = refs[0], refs[1 : 1 + refs_in], refs[1 + refs_in :]
    for crosses, source, part, at, out, slot in copies:

        def copy(source=source, part=part, at=at, out=out, slot=slot):
            start = by_parity(flags_ref, at)

            def one_cell(x, _):
                for field in range(2):
                    for f in range(outs[out].shape[2]):
                        where = (field, f, start + x) if part is None else (part, field, f, start + x)
                        outs[out][slot, field, f, x] = ins[source][where]
                return 0

            lax.fori_loop(0, outs[out].shape[3], one_cell, 0, unroll=4)

        if crosses is None:
            copy()
        else:
            pl.when((flags_ref[1] == 1) == crosses)(copy)


def pack(flags, arrays, copies, shapes):
    vmem = pl.BlockSpec(memory_space=pltpu.VMEM)
    return pl.pallas_call(
        functools.partial(pack_kernel, copies, len(arrays)),
        in_specs=[pl.BlockSpec(memory_space=pltpu.SMEM)] + [vmem] * len(arrays),
        out_specs=[vmem] * len(shapes),
        out_shape=[jax.ShapeDtypeStruct(shape, jnp.bfloat16) for shape in shapes],
        compiler_params=pltpu.CompilerParams(vmem_limit_bytes=12 << 20),
        cost_estimate=pl.CostEstimate(flops=0, bytes_accessed=2 << 20, transcendentals=0),
        name="pack",
    )(flags, *arrays)


def sum_kernel(variants, count, bands, last, flags_ref, *refs):
    for crosses, plan, first, groups in variants:
        run = functools.partial(sum_body, plan, count, groups, bands, first, last, flags_ref, *refs)
        if crosses is None:
            run()
        else:
            pl.when((flags_ref[1] == 1) == crosses)(run)


def sum_body(plan, count, groups, bands, first, last, flags_ref, *refs):
    blocks, refs = refs[:count], refs[count:]
    befores = ()
    if last in (1, 2):
        befores, refs = refs[: len(bands)], refs[len(bands) :]
    if last >= 2:
        refs = refs[1:]
    last = last % 3
    outs = refs[: 1 if last else len(bands)]
    fields = refs[len(outs)]
    if last:
        turn, stage, sems = refs[len(outs) + 1 :]
        out_ref = outs[0]
    cells = stage.shape[4 - 1] if last else outs[0].shape[1]

    def fill(index, part, at, length, to, group):
        start, to = by_parity(flags_ref, at), by_parity(flags_ref, to)

        def one_cell(x, _):
            for field in range(2):
                for f in range(2):
                    if index is None:
                        value = jnp.zeros((ROWS, LANES), jnp.float32)
                    elif part is None:
                        value = blocks[index][field, f, start + x].astype(jnp.float32)
                    else:
                        value = blocks[index][part, field, f, start + x].astype(jnp.float32)
                    fields[field, to + x, 2 * group + f] = value
            return 0

        lax.fori_loop(0, length, one_cell, 0, unroll=4)

    for index, part, at, length, to, group, values in plan:
        place = functools.partial(fill, index, part, at, length, to, group)
        if values is None:
            place()
        else:
            pl.when(functools.reduce(jnp.logical_or, [flags_ref[1] == value for value in values]))(place)

    def tile(before, out, k0, row0, rows, x0, slot, fresh, freqs):
        s0 = x0 + 2 * HMAX - k0 - (rows - 1)
        r0 = x0 + k0
        if fresh:
            total = [[None] * TX for _ in range(rows)]
        else:
            total = [[before[row0 + j, x0 + i] for i in range(TX)] for j in range(rows)]
        for f in range(freqs):
            for c in range(2):
                s = [fields[0, s0 + i, f, 8 * c : 8 * c + 8] for i in range(TX + rows - 1)]
                r = [fields[1, r0 + i, f, 8 * c : 8 * c + 8] for i in range(TX + rows - 1)]
                for j in range(rows):
                    for i in range(TX):
                        product = s[i + rows - 1 - j] * r[i + j]
                        total[j][i] = product if total[j][i] is None else total[j][i] + product
        for j in range(rows):
            if not last:
                for i in range(TX):
                    out[row0 + j, x0 + i] = total[j][i]
                continue
            for i in range(TX):
                turn[j, pl.ds(i, 8, stride=TX)] = 0.25 * total[j][i]
            for zh in range(2):
                for y in range(4):
                    row = zh * 4 + y
                    stage[slot, y, j, pl.ds(pl.multiple_of(x0, TX), TX), zh * LANES : (zh + 1) * LANES] = turn[
                        j, row * TX : (row + 1) * TX
                    ]

    def out_copy(k0, rows, slot):
        return pltpu.make_async_copy(stage.at[slot, :, pl.ds(0, rows)], out_ref.at[:, pl.ds(k0, rows)], sems.at[slot])

    for band, (k_first, steps, jump_at, jump, rest) in enumerate(bands):
        before = befores[band] if befores else None
        out = None if last else outs[band]

        def first_row(step):
            k0 = k_first + TH * step
            return k0 if not jump else k0 + jnp.where(step >= jump_at, jump, 0)

        def rows_of(k0, row0, rows, slot):
            def x_step(start, fresh, freqs, xt, _):
                tile(before, out, k0, row0, rows, (start + xt) * TX, slot, fresh, freqs)
                return 0

            if first == "half":
                middle = cells // TX // 2
                beside = functools.partial(x_step, by_parity(flags_ref, (0, middle)), True, 2 * groups)
                lax.fori_loop(0, middle, beside, 0)
                other = functools.partial(x_step, by_parity(flags_ref, (middle, 0)), False, 4)
                lax.fori_loop(0, middle, other, 0)
            else:
                lax.fori_loop(0, cells // TX, functools.partial(x_step, 0, first, 2 * groups), 0)

        def h_step(step, _):
            slot = lax.rem(step, SLOTS)
            if last:

                @pl.when(step >= SLOTS)
                def _():
                    out_copy(first_row(step - SLOTS), TH, slot).wait()

            rows_of(first_row(step), TH * step, TH, slot)
            if last:
                out_copy(first_row(step), TH, slot).start()
            return 0

        lax.fori_loop(0, steps, h_step, 0)
        if rest:
            slot = steps % SLOTS
            k0 = k_first + TH * steps
            if last:
                out_copy(first_row(steps - SLOTS), TH, slot).wait()
            rows_of(k0, TH * steps, rest, slot)
            if last:
                out_copy(k0, rest, slot).start()
        if last:
            for step in range(steps - SLOTS + (1 if rest else 0), steps):
                out_copy(first_row(step), TH, step % SLOTS).wait()
            if rest:
                out_copy(k_first + TH * steps, rest, steps % SLOTS).wait()


NEAR_BAND = (HMAX - NEAR, 2 * NEAR // TH, 0, 0, 1)
FAR_BAND = (0, 2 * NEAR // TH, NEAR // TH, 2 * NEAR + 1, 0)


def summed(flags, blocks, variants, bands, befores, cells, last, image=None):
    heights = [TH * band[1] + band[4] for band in bands]
    groups = max(variant[-1] for variant in variants)
    scratch = [pltpu.VMEM((2, 3 * cells, 2 * groups, ROWS, LANES), jnp.float32)]
    vmem = pl.BlockSpec(memory_space=pltpu.VMEM)
    hbm = pl.BlockSpec(memory_space=pl.ANY)
    operands = list(blocks) + list(befores)
    in_specs = [pl.BlockSpec(memory_space=pltpu.SMEM)] + [vmem] * len(operands)
    aliases = {}
    if last:
        scratch += [
            pltpu.VMEM((TH, 8 * TX, LANES), jnp.float32),
            pltpu.VMEM((SLOTS, 4, TH, cells, 2 * LANES), jnp.float32),
            pltpu.SemaphoreType.DMA((SLOTS,)),
        ]
        out_shape = jax.ShapeDtypeStruct((4, OFFSETS, cells, 2 * LANES), jnp.float32)
        out_specs = hbm
        if last == 2:
            operands.append(image)
            in_specs.append(hbm)
            aliases = {len(operands): 0}
    else:
        out_shape = [pltpu.VMEM((height, cells, 8, LANES), jnp.float32) for height in heights]
        out_specs = [vmem] * len(heights)
        if image is not None:
            operands.append(image)
            in_specs.append(vmem)
            aliases = {len(operands): 0}
    return pl.pallas_call(
        functools.partial(sum_kernel, variants, len(blocks), bands, last if image is None or last else 3),
        in_specs=in_specs,
        out_specs=out_specs,
        out_shape=out_shape,
        scratch_shapes=scratch,
        input_output_aliases=aliases,
        compiler_params=pltpu.CompilerParams(vmem_limit_bytes=32 << 20),
        cost_estimate=pl.CostEstimate(
            flops=520_000 * sum(heights), bytes_accessed=130_000 * sum(heights), transcendentals=0
        ),
        name="image" if last else "partial",
    )(flags, *operands)


def body(source_field, receiver_field):
    slabs = lax.axis_size("slab")
    middle = slabs // 2
    cells, freqs = source_field.shape[2], source_field.shape[1]
    group = lax.axis_index("freq").astype(jnp.int32)
    slab = lax.axis_index("slab")
    beyond = jnp.where((slab == 0) | (slab == slabs - 1), 2, 0)
    beyond = jnp.where((slab == middle) | (slab == middle - 1), 1, beyond)
    flags = jnp.stack([slab % 2, beyond]).astype(jnp.int32)
    parts = regrouped(group[None], source_field, receiver_field)

    def swap(part, d):
        return lax.ppermute(part, "freq", [(g, g ^ d) for g in range(GROUPS)])

    def trade(value, partner, turned=()):
        pairs = []
        for s in range(slabs):
            for g in range(GROUPS):
                pairs.append((s * GROUPS + g, partner(s) * GROUPS + (g ^ 2 if s in turned else g)))
        return lax.ppermute(value, ("slab", "freq"), pairs)

    def side_a(s):
        return s ^ 1

    def side_b(s):
        return min(max(s + 1 if s % 2 else s - 1, 0), slabs - 1)

    def side_b_of_half(s):
        return s // middle * middle + (s + 1 if s % 2 else s - 1) % middle

    one, other = swap(parts[1], 1), swap(parts[3], 1)

    whole, half = [(2, 2, freqs, length, ROWS, LANES) for length in (cells, NEAR)]
    rest = cells - NEAR
    copies = [(None, slot, None, 0, 0, slot) for slot in range(2)]
    (turned_own,) = pack(flags, (parts[2], other), copies, (whole,))
    far_own = swap(turned_own, 2)
    copies = []
    for slot in range(2):
        for out, at in ((0, 0), (1, (0, rest)), (2, (rest, 0))):
            copies.append((None, slot, None, at, out, slot))
    own, near_b, far_b = pack(flags, (parts[0], one), copies, (whole,) + (half,) * 2)
    whole_a = trade(own, side_a)
    first_near_b, first_far_b = trade(near_b, side_b_of_half), trade(far_b, side_b_of_half)
    over_middle = [(0, middle), (slabs - 1, middle - 1)]
    near_over = lax.ppermute(first_near_b, "slab", over_middle)

    copies = []
    for slot in range(2):
        for out, at in ((0, (rest, 0)), (2, (0, rest))):
            copies.append((None, 0, slot, at, out, slot))
        for out, at in ((1, (0, rest)), (3, (rest, 0))):
            copies += [(False, 0, slot, at, out, slot), (True, 1, slot, at, out, slot)]
    near_a, near_b, far_a, far_b = pack(flags, (far_own, turned_own), copies, (half,) * 4)
    turned = (middle - 1, middle)
    near_a, near_b = trade(near_a, side_a), trade(near_b, side_b, turned)
    far_a, far_b = trade(far_a, side_a), trade(far_b, side_b, turned)

    near_at_a, near_at_b = (2 * cells, rest), (rest, 2 * cells)
    far_at_a, far_at_b = (2 * cells + NEAR, 0), (0, 2 * cells + NEAR)
    zero = (None, 0, 0, NEAR)

    def first_groups(own, whole_a, near_b, far_b, near_over, far_over, to, far):
        plan = []
        for g in range(2):
            plan += [(own, g, 0, cells, cells, to + g, None), (whole_a, g, (0, rest), NEAR, near_at_a, to + g, None)]
            plan += [(near_b, g, 0, NEAR, near_at_b, to + g, (0,)), (*zero, near_at_b, to + g, (2,))]
            if near_over is not None:
                plan += [(near_over, g, 0, NEAR, near_at_b, to + g, (1,))]
            if far:
                plan += [(whole_a, g, (rest, 0), NEAR, far_at_a, to + g, None)]
                plan += [(far_b, g, 0, NEAR, far_at_b, to + g, (0,)), (*zero, far_at_b, to + g, (2,))]
                if far_over is not None:
                    plan += [(far_over, g, 0, NEAR, far_at_b, to + g, (1,))]
        return plan

    def last_groups(own, near_a, near_b, far_a, far_b, far):
        plan = []
        for g in range(2):
            plan += [(own, g, 0, cells, cells, g, None), (near_a, g, 0, NEAR, near_at_a, g, None)]
            plan += [(near_b, g, 0, NEAR, near_at_b, g, (0, 1)), (*zero, near_at_b, g, (2,))]
            if far:
                plan += [(far_a, g, 0, NEAR, far_at_a, g, None)]
                plan += [(far_b, g, 0, NEAR, far_at_b, g, (0, 1)), (*zero, far_at_b, g, (2,))]
        return plan

    plan = first_groups(0, 1, 2, None, 3, None, 0, False)
    near_sums = summed(flags, (own, whole_a, first_near_b, near_over), ((None, plan, True, 2),), (NEAR_BAND,), (), cells, 0)
    plan = first_groups(0, 1, 2, 3, None, None, 0, True)
    blocks = (own, whole_a, first_near_b, first_far_b)
    far_sums = summed(flags, blocks, ((False, plan, True, 2),), (FAR_BAND,), (), cells, 0)
    far_over, *far_sums = lax.optimization_barrier((first_far_b, *far_sums))
    far_over = lax.ppermute(far_over, "slab", over_middle)
    plan = first_groups(0, 1, None, None, 2, None, 0, True)
    plan = [entry for entry in plan if entry[-1] != (0,)] + [(*zero, far_at_b, g, (1,)) for g in range(2)]
    far_sums = summed(
        flags, (own, whole_a, near_over), ((True, plan, True, 2),), (FAR_BAND,), (), cells, 0, far_sums[0]
    )
    plan = last_groups(0, 1, 2, None, None, False)
    image = summed(flags, (far_own, near_a, near_b), ((None, plan, False, 2),), (NEAR_BAND,), near_sums, cells, 1)
    plan = last_groups(0, 1, 2, 3, 4, True)
    crossing = plan + first_groups(5, 6, None, None, 7, 8, 2, True)
    crossing = [entry for entry in crossing if entry[0] is not None or entry[5] < 2]
    crossing = [entry for entry in crossing if entry[-1] != (0,)]
    blocks = (far_own, near_a, near_b, far_a, far_b, own, whole_a, near_over, far_over)
    variants = ((False, plan, False, 2), (True, crossing, "half", 4))
    return summed(flags, blocks, variants, (FAR_BAND,), far_sums, cells, 2, image)


def solution(mesh):
    in_specs = (P(None, "freq", "slab", None, None), P(None, "freq", "slab", None, None))
    out_specs = P("freq", None, "slab", None)
    return jax.shard_map(body, mesh=mesh, in_specs=in_specs, out_specs=out_specs, check_vma=False)
```

```python
import functools

import jax
import jax.numpy as jnp
from jax import lax
from jax.experimental import pallas as pl
from jax.experimental.pallas import tpu as pltpu
from jax.sharding import PartitionSpec as P

HMAX = 32
OFFSETS = 2 * HMAX + 1
GROUPS = 4
ROWS = 16
LANES = 128
TX = 8
TH = 4
SLOTS = 4
CHUNKS = 4
NEAR = HMAX // 2


def regroup_kernel(group_ref, source_ref, receiver_ref, *refs):
    out_refs, (held, sems) = refs[:GROUPS], refs[GROUPS:]
    freqs, cells = source_ref.shape[1], source_ref.shape[2]
    share = cells // CHUNKS

    def fetch(field, chunk):
        ref = (source_ref, receiver_ref)[field]
        part = pl.ds(chunk * share, share)
        return pltpu.make_async_copy(ref.at[:, :, part], held.at[field, :, :, part], sems.at[field, chunk])

    for chunk in range(CHUNKS):
        for field in range(2):
            fetch(field, chunk).start()

    def regroup(order):
        low = lax.broadcasted_iota(jnp.int32, (8, LANES), 0) < 4
        for chunk in range(CHUNKS):
            for field in range(2):
                fetch(field, chunk).wait()

                def one_cell(x, _):
                    for f in range(freqs):
                        parts = [[None, None] for _ in range(GROUPS)]
                        for c in range(2):
                            near = held[field, c, f, x, :, :LANES].astype(jnp.float32)
                            far = held[field, c, f, x, :, LANES:].astype(jnp.float32)
                            for pair in range(2):
                                a = near[8 * pair : 8 * pair + 8]
                                b = far[8 * pair : 8 * pair + 8]
                                parts[2 * pair][c] = jnp.where(low, a, pltpu.roll(b, 4, 0))
                                parts[2 * pair + 1][c] = jnp.where(low, pltpu.roll(a, 4, 0), b)
                        for d in range(GROUPS):
                            out_refs[d][field, f, x] = jnp.concatenate(parts[order ^ d], axis=0).astype(jnp.bfloat16)
                    return 0

                lax.fori_loop(chunk * share, (chunk + 1) * share, one_cell, 0, unroll=2)

    for order in range(GROUPS):
        pl.when(group_ref[0] == order)(functools.partial(regroup, order))


def regrouped(group, source_field, receiver_field):
    two, freqs, cells, _, _ = source_field.shape
    return pl.pallas_call(
        regroup_kernel,
        in_specs=[pl.BlockSpec(memory_space=pltpu.SMEM)] + [pl.BlockSpec(memory_space=pl.ANY)] * 2,
        out_specs=[pl.BlockSpec(memory_space=pltpu.VMEM)] * GROUPS,
        out_shape=[pltpu.VMEM((2, freqs, cells, ROWS, LANES), jnp.bfloat16)] * GROUPS,
        scratch_shapes=[pltpu.VMEM((2, 2, freqs, cells, 16, 2 * LANES), jnp.bfloat16), pltpu.SemaphoreType.DMA((2, CHUNKS))],
        compiler_params=pltpu.CompilerParams(vmem_limit_bytes=12 << 20),
        cost_estimate=pl.CostEstimate(flops=0, bytes_accessed=4 << 20, transcendentals=0),
        name="regroup",
    )(group, *(pltpu.with_memory_space_constraint(x, pltpu.HBM) for x in (source_field, receiver_field)))


def by_parity(flags_ref, choice):
    if isinstance(choice, int):
        return choice
    return jnp.where(flags_ref[0] == 0, choice[0], choice[1])


def pack_kernel(copies, refs_in, *refs):
    flags_ref, ins, outs = refs[0], refs[1 : 1 + refs_in], refs[1 + refs_in :]
    for crosses, source, part, at, out, slot in copies:

        def copy(source=source, part=part, at=at, out=out, slot=slot):
            start = by_parity(flags_ref, at)

            def one_cell(x, _):
                for field in range(2):
                    for f in range(outs[out].shape[2]):
                        where = (field, f, start + x) if part is None else (part, field, f, start + x)
                        outs[out][slot, field, f, x] = ins[source][where]
                return 0

            lax.fori_loop(0, outs[out].shape[3], one_cell, 0, unroll=4)

        if crosses is None:
            copy()
        else:
            pl.when((flags_ref[1] == 1) == crosses)(copy)


def pack(flags, arrays, copies, shapes):
    vmem = pl.BlockSpec(memory_space=pltpu.VMEM)
    return pl.pallas_call(
        functools.partial(pack_kernel, copies, len(arrays)),
        in_specs=[pl.BlockSpec(memory_space=pltpu.SMEM)] + [vmem] * len(arrays),
        out_specs=[vmem] * len(shapes),
        out_shape=[jax.ShapeDtypeStruct(shape, jnp.bfloat16) for shape in shapes],
        compiler_params=pltpu.CompilerParams(vmem_limit_bytes=12 << 20),
        cost_estimate=pl.CostEstimate(flops=0, bytes_accessed=2 << 20, transcendentals=0),
        name="pack",
    )(flags, *arrays)


def sum_kernel(variants, count, bands, last, flags_ref, *refs):
    for crosses, plan, first, groups in variants:
        run = functools.partial(sum_body, plan, count, groups, bands, first, last, flags_ref, *refs)
        if crosses is None:
            run()
        else:
            pl.when((flags_ref[1] == 1) == crosses)(run)


def sum_body(plan, count, groups, bands, first, last, flags_ref, *refs):
    blocks, refs = refs[:count], refs[count:]
    befores = ()
    if last in (1, 2):
        befores, refs = refs[: len(bands)], refs[len(bands) :]
    if last >= 2:
        refs = refs[1:]
    last = last % 3
    outs = refs[: 1 if last else len(bands)]
    fields = refs[len(outs)]
    if last:
        turn, stage, sems = refs[len(outs) + 1 :]
        out_ref = outs[0]
    cells = stage.shape[4 - 1] if last else outs[0].shape[1]

    def fill(index, part, at, length, to, group):
        start, to = by_parity(flags_ref, at), by_parity(flags_ref, to)

        def one_cell(x, _):
            for field in range(2):
                for f in range(2):
                    if index is None:
                        value = jnp.zeros((ROWS, LANES), jnp.float32)
                    elif part is None:
                        value = blocks[index][field, f, start + x].astype(jnp.float32)
                    else:
                        value = blocks[index][part, field, f, start + x].astype(jnp.float32)
                    fields[field, to + x, 2 * group + f] = value
            return 0

        lax.fori_loop(0, length, one_cell, 0, unroll=4)

    for index, part, at, length, to, group, values in plan:
        place = functools.partial(fill, index, part, at, length, to, group)
        if values is None:
            place()
        else:
            pl.when(functools.reduce(jnp.logical_or, [flags_ref[1] == value for value in values]))(place)

    def tile(before, out, k0, row0, rows, x0, slot, fresh, freqs):
        s0 = x0 + 2 * HMAX - k0 - (rows - 1)
        r0 = x0 + k0
        if fresh:
            total = [[None] * TX for _ in range(rows)]
        else:
            total = [[before[row0 + j, x0 + i] for i in range(TX)] for j in range(rows)]
        for f in range(freqs):
            for c in range(2):
                s = [fields[0, s0 + i, f, 8 * c : 8 * c + 8] for i in range(TX + rows - 1)]
                r = [fields[1, r0 + i, f, 8 * c : 8 * c + 8] for i in range(TX + rows - 1)]
                for j in range(rows):
                    for i in range(TX):
                        product = s[i + rows - 1 - j] * r[i + j]
                        total[j][i] = product if total[j][i] is None else total[j][i] + product
        for j in range(rows):
            if not last:
                for i in range(TX):
                    out[row0 + j, x0 + i] = total[j][i]
                continue
            for i in range(TX):
                turn[j, pl.ds(i, 8, stride=TX)] = 0.25 * total[j][i]
            for zh in range(2):
                for y in range(4):
                    row = zh * 4 + y
                    stage[slot, y, j, pl.ds(pl.multiple_of(x0, TX), TX), zh * LANES : (zh + 1) * LANES] = turn[
                        j, row * TX : (row + 1) * TX
                    ]

    def out_copy(k0, rows, slot):
        return pltpu.make_async_copy(stage.at[slot, :, pl.ds(0, rows)], out_ref.at[:, pl.ds(k0, rows)], sems.at[slot])

    for band, (k_first, steps, jump_at, jump, rest) in enumerate(bands):
        before = befores[band] if befores else None
        out = None if last else outs[band]

        def first_row(step):
            k0 = k_first + TH * step
            return k0 if not jump else k0 + jnp.where(step >= jump_at, jump, 0)

        def rows_of(k0, row0, rows, slot):
            def x_step(start, fresh, freqs, xt, _):
                tile(before, out, k0, row0, rows, (start + xt) * TX, slot, fresh, freqs)
                return 0

            if first == "half":
                middle = cells // TX // 2
                beside = functools.partial(x_step, by_parity(flags_ref, (0, middle)), True, 2 * groups)
                lax.fori_loop(0, middle, beside, 0)
                other = functools.partial(x_step, by_parity(flags_ref, (middle, 0)), False, 4)
                lax.fori_loop(0, middle, other, 0)
            else:
                lax.fori_loop(0, cells // TX, functools.partial(x_step, 0, first, 2 * groups), 0)

        def h_step(step, _):
            slot = lax.rem(step, SLOTS)
            if last:

                @pl.when(step >= SLOTS)
                def _():
                    out_copy(first_row(step - SLOTS), TH, slot).wait()

            rows_of(first_row(step), TH * step, TH, slot)
            if last:
                out_copy(first_row(step), TH, slot).start()
            return 0

        lax.fori_loop(0, steps, h_step, 0)
        if rest:
            slot = steps % SLOTS
            k0 = k_first + TH * steps
            if last:
                out_copy(first_row(steps - SLOTS), TH, slot).wait()
            rows_of(k0, TH * steps, rest, slot)
            if last:
                out_copy(k0, rest, slot).start()
        if last:
            for step in range(steps - SLOTS + (1 if rest else 0), steps):
                out_copy(first_row(step), TH, step % SLOTS).wait()
            if rest:
                out_copy(k_first + TH * steps, rest, steps % SLOTS).wait()


NEAR_BAND = (HMAX - NEAR, 2 * NEAR // TH, 0, 0, 1)
FAR_BAND = (0, 2 * NEAR // TH, NEAR // TH, 2 * NEAR + 1, 0)


def summed(flags, blocks, variants, bands, befores, cells, last, image=None):
    heights = [TH * band[1] + band[4] for band in bands]
    groups = max(variant[-1] for variant in variants)
    scratch = [pltpu.VMEM((2, 3 * cells, 2 * groups, ROWS, LANES), jnp.float32)]
    vmem = pl.BlockSpec(memory_space=pltpu.VMEM)
    hbm = pl.BlockSpec(memory_space=pl.ANY)
    operands = list(blocks) + list(befores)
    in_specs = [pl.BlockSpec(memory_space=pltpu.SMEM)] + [vmem] * len(operands)
    aliases = {}
    if last:
        scratch += [
            pltpu.VMEM((TH, 8 * TX, LANES), jnp.float32),
            pltpu.VMEM((SLOTS, 4, TH, cells, 2 * LANES), jnp.float32),
            pltpu.SemaphoreType.DMA((SLOTS,)),
        ]
        out_shape = jax.ShapeDtypeStruct((4, OFFSETS, cells, 2 * LANES), jnp.float32)
        out_specs = hbm
        if last == 2:
            operands.append(image)
            in_specs.append(hbm)
            aliases = {len(operands): 0}
    else:
        out_shape = [pltpu.VMEM((height, cells, 8, LANES), jnp.float32) for height in heights]
        out_specs = [vmem] * len(heights)
        if image is not None:
            operands.append(image)
            in_specs.append(vmem)
            aliases = {len(operands): 0}
    return pl.pallas_call(
        functools.partial(sum_kernel, variants, len(blocks), bands, last if image is None or last else 3),
        in_specs=in_specs,
        out_specs=out_specs,
        out_shape=out_shape,
        scratch_shapes=scratch,
        input_output_aliases=aliases,
        compiler_params=pltpu.CompilerParams(vmem_limit_bytes=32 << 20),
        cost_estimate=pl.CostEstimate(
            flops=520_000 * sum(heights), bytes_accessed=130_000 * sum(heights), transcendentals=0
        ),
        name="image" if last else "partial",
    )(flags, *operands)


def body(source_field, receiver_field):
    slabs = lax.axis_size("slab")
    middle = slabs // 2
    cells, freqs = source_field.shape[2], source_field.shape[1]
    group = lax.axis_index("freq").astype(jnp.int32)
    slab = lax.axis_index("slab")
    beyond = jnp.where((slab == 0) | (slab == slabs - 1), 2, 0)
    beyond = jnp.where((slab == middle) | (slab == middle - 1), 1, beyond)
    flags = jnp.stack([slab % 2, beyond]).astype(jnp.int32)
    parts = regrouped(group[None], source_field, receiver_field)

    def swap(part, d):
        return lax.ppermute(part, "freq", [(g, g ^ d) for g in range(GROUPS)])

    def trade(value, partner, turned=()):
        pairs = []
        for s in range(slabs):
            for g in range(GROUPS):
                pairs.append((s * GROUPS + g, partner(s) * GROUPS + (g ^ 2 if s in turned else g)))
        return lax.ppermute(value, ("slab", "freq"), pairs)

    def side_a(s):
        return s ^ 1

    def side_b(s):
        return min(max(s + 1 if s % 2 else s - 1, 0), slabs - 1)

    def side_b_of_half(s):
        return s // middle * middle + (s + 1 if s % 2 else s - 1) % middle

    one, other = swap(parts[1], 1), swap(parts[3], 1)

    whole, half = [(2, 2, freqs, length, ROWS, LANES) for length in (cells, NEAR)]
    rest = cells - NEAR
    copies = [(None, slot, None, 0, 0, slot) for slot in range(2)]
    (turned_own,) = pack(flags, (parts[2], other), copies, (whole,))
    far_own = swap(turned_own, 2)
    copies = []
    for slot in range(2):
        for out, at in ((0, 0), (1, (0, rest)), (2, (rest, 0))):
            copies.append((None, slot, None, at, out, slot))
    own, near_b, far_b = pack(flags, (parts[0], one), copies, (whole,) + (half,) * 2)
    whole_a = trade(own, side_a)
    first_near_b, first_far_b = trade(near_b, side_b_of_half), trade(far_b, side_b_of_half)
    over_middle = [(0, middle), (slabs - 1, middle - 1)]
    near_over = lax.ppermute(first_near_b, "slab", over_middle)

    copies = []
    for slot in range(2):
        for out, at in ((0, (rest, 0)), (2, (0, rest))):
            copies.append((None, 0, slot, at, out, slot))
        for out, at in ((1, (0, rest)), (3, (rest, 0))):
            copies += [(False, 0, slot, at, out, slot), (True, 1, slot, at, out, slot)]
    near_a, near_b, far_a, far_b = pack(flags, (far_own, turned_own), copies, (half,) * 4)
    turned = (middle - 1, middle)
    near_b = trade(near_b, side_b, turned)
    near_a = trade(near_a, side_a)
    far_b = trade(far_b, side_b, turned)
    far_a = trade(far_a, side_a)

    near_at_a, near_at_b = (2 * cells, rest), (rest, 2 * cells)
    far_at_a, far_at_b = (2 * cells + NEAR, 0), (0, 2 * cells + NEAR)
    zero = (None, 0, 0, NEAR)

    def first_groups(own, whole_a, near_b, far_b, near_over, far_over, to, far):
        plan = []
        for g in range(2):
            plan += [(own, g, 0, cells, cells, to + g, None), (whole_a, g, (0, rest), NEAR, near_at_a, to + g, None)]
            plan += [(near_b, g, 0, NEAR, near_at_b, to + g, (0,)), (*zero, near_at_b, to + g, (2,))]
            if near_over is not None:
                plan += [(near_over, g, 0, NEAR, near_at_b, to + g, (1,))]
            if far:
                plan += [(whole_a, g, (rest, 0), NEAR, far_at_a, to + g, None)]
                plan += [(far_b, g, 0, NEAR, far_at_b, to + g, (0,)), (*zero, far_at_b, to + g, (2,))]
                if far_over is not None:
                    plan += [(far_over, g, 0, NEAR, far_at_b, to + g, (1,))]
        return plan

    def last_groups(own, near_a, near_b, far_a, far_b, far):
        plan = []
        for g in range(2):
            plan += [(own, g, 0, cells, cells, g, None), (near_a, g, 0, NEAR, near_at_a, g, None)]
            plan += [(near_b, g, 0, NEAR, near_at_b, g, (0, 1)), (*zero, near_at_b, g, (2,))]
            if far:
                plan += [(far_a, g, 0, NEAR, far_at_a, g, None)]
                plan += [(far_b, g, 0, NEAR, far_at_b, g, (0, 1)), (*zero, far_at_b, g, (2,))]
        return plan

    plan = first_groups(0, 1, 2, None, 3, None, 0, False)
    near_sums = summed(flags, (own, whole_a, first_near_b, near_over), ((None, plan, True, 2),), (NEAR_BAND,), (), cells, 0)
    plan = first_groups(0, 1, 2, 3, None, None, 0, True)
    blocks = (own, whole_a, first_near_b, first_far_b)
    far_sums = summed(flags, blocks, ((False, plan, True, 2),), (FAR_BAND,), (), cells, 0)
    far_over, *far_sums = lax.optimization_barrier((first_far_b, *far_sums))
    far_over = lax.ppermute(far_over, "slab", over_middle)
    plan = first_groups(0, 1, None, None, 2, None, 0, True)
    plan = [entry for entry in plan if entry[-1] != (0,)] + [(*zero, far_at_b, g, (1,)) for g in range(2)]
    far_sums = summed(
        flags, (own, whole_a, near_over), ((True, plan, True, 2),), (FAR_BAND,), (), cells, 0, far_sums[0]
    )
    plan = last_groups(0, 2, 1, None, None, False)
    image = summed(flags, (far_own, near_b, near_a), ((None, plan, False, 2),), (NEAR_BAND,), near_sums, cells, 1)
    plan = last_groups(0, 2, 1, 4, 3, True)
    crossing = plan + first_groups(5, 6, None, None, 7, 8, 2, True)
    crossing = [entry for entry in crossing if entry[0] is not None or entry[5] < 2]
    crossing = [entry for entry in crossing if entry[-1] != (0,)]
    blocks = (far_own, near_b, near_a, far_b, far_a, own, whole_a, near_over, far_over)
    variants = ((False, plan, False, 2), (True, crossing, "half", 4))
    return summed(flags, blocks, variants, (FAR_BAND,), far_sums, cells, 2, image)


def solution(mesh):
    in_specs = (P(None, "freq", "slab", None, None), P(None, "freq", "slab", None, None))
    out_specs = P("freq", None, "slab", None)
    return jax.shard_map(body, mesh=mesh, in_specs=in_specs, out_specs=out_specs, check_vma=False)
```

```python
import functools

import jax
import jax.numpy as jnp
from jax import lax
from jax.experimental import pallas as pl
from jax.experimental.pallas import tpu as pltpu
from jax.sharding import PartitionSpec as P

HMAX = 32
OFFSETS = 2 * HMAX + 1
GROUPS = 4
ROWS = 16
LANES = 128
TX = 8
TH = 4
SLOTS = 4
CHUNKS = 4
NEAR = HMAX // 2


def regroup_kernel(group_ref, source_ref, receiver_ref, *refs):
    out_refs, (held, sems) = refs[:GROUPS], refs[GROUPS:]
    freqs, cells = source_ref.shape[1], source_ref.shape[2]
    share = cells // CHUNKS

    def fetch(field, chunk):
        ref = (source_ref, receiver_ref)[field]
        part = pl.ds(chunk * share, share)
        return pltpu.make_async_copy(ref.at[:, :, part], held.at[field, :, :, part], sems.at[field, chunk])

    for chunk in range(CHUNKS):
        for field in range(2):
            fetch(field, chunk).start()

    def regroup(order):
        low = lax.broadcasted_iota(jnp.int32, (8, LANES), 0) < 4
        for chunk in range(CHUNKS):
            for field in range(2):
                fetch(field, chunk).wait()

                def one_cell(x, _):
                    for f in range(freqs):
                        parts = [[None, None] for _ in range(GROUPS)]
                        for c in range(2):
                            near = held[field, c, f, x, :, :LANES].astype(jnp.float32)
                            far = held[field, c, f, x, :, LANES:].astype(jnp.float32)
                            for pair in range(2):
                                a = near[8 * pair : 8 * pair + 8]
                                b = far[8 * pair : 8 * pair + 8]
                                parts[2 * pair][c] = jnp.where(low, a, pltpu.roll(b, 4, 0))
                                parts[2 * pair + 1][c] = jnp.where(low, pltpu.roll(a, 4, 0), b)
                        for d in range(GROUPS):
                            out_refs[d][field, f, x] = jnp.concatenate(parts[order ^ d], axis=0).astype(jnp.bfloat16)
                    return 0

                lax.fori_loop(chunk * share, (chunk + 1) * share, one_cell, 0, unroll=2)

    for order in range(GROUPS):
        pl.when(group_ref[0] == order)(functools.partial(regroup, order))


def regrouped(group, source_field, receiver_field):
    two, freqs, cells, _, _ = source_field.shape
    return pl.pallas_call(
        regroup_kernel,
        in_specs=[pl.BlockSpec(memory_space=pltpu.SMEM)] + [pl.BlockSpec(memory_space=pl.ANY)] * 2,
        out_specs=[pl.BlockSpec(memory_space=pltpu.VMEM)] * GROUPS,
        out_shape=[pltpu.VMEM((2, freqs, cells, ROWS, LANES), jnp.bfloat16)] * GROUPS,
        scratch_shapes=[pltpu.VMEM((2, 2, freqs, cells, 16, 2 * LANES), jnp.bfloat16), pltpu.SemaphoreType.DMA((2, CHUNKS))],
        compiler_params=pltpu.CompilerParams(vmem_limit_bytes=12 << 20),
        cost_estimate=pl.CostEstimate(flops=0, bytes_accessed=4 << 20, transcendentals=0),
        name="regroup",
    )(group, *(pltpu.with_memory_space_constraint(x, pltpu.HBM) for x in (source_field, receiver_field)))


def by_parity(flags_ref, choice):
    if isinstance(choice, int):
        return choice
    return jnp.where(flags_ref[0] == 0, choice[0], choice[1])


def pack_kernel(copies, refs_in, *refs):
    flags_ref, ins, outs = refs[0], refs[1 : 1 + refs_in], refs[1 + refs_in :]
    for crosses, source, part, at, out, slot in copies:

        def copy(source=source, part=part, at=at, out=out, slot=slot):
            start = by_parity(flags_ref, at)

            def one_cell(x, _):
                for field in range(2):
                    for f in range(outs[out].shape[2]):
                        where = (field, f, start + x) if part is None else (part, field, f, start + x)
                        outs[out][slot, field, f, x] = ins[source][where]
                return 0

            lax.fori_loop(0, outs[out].shape[3], one_cell, 0, unroll=4)

        if crosses is None:
            copy()
        else:
            pl.when((flags_ref[1] == 1) == crosses)(copy)


def pack(flags, arrays, copies, shapes):
    vmem = pl.BlockSpec(memory_space=pltpu.VMEM)
    return pl.pallas_call(
        functools.partial(pack_kernel, copies, len(arrays)),
        in_specs=[pl.BlockSpec(memory_space=pltpu.SMEM)] + [vmem] * len(arrays),
        out_specs=[vmem] * len(shapes),
        out_shape=[jax.ShapeDtypeStruct(shape, jnp.bfloat16) for shape in shapes],
        compiler_params=pltpu.CompilerParams(vmem_limit_bytes=12 << 20),
        cost_estimate=pl.CostEstimate(flops=0, bytes_accessed=2 << 20, transcendentals=0),
        name="pack",
    )(flags, *arrays)


def sum_kernel(variants, count, bands, last, flags_ref, *refs):
    for crosses, plan, first, groups in variants:
        run = functools.partial(sum_body, plan, count, groups, bands, first, last, flags_ref, *refs)
        if crosses is None:
            run()
        else:
            pl.when((flags_ref[1] == 1) == crosses)(run)


def sum_body(plan, count, groups, bands, first, last, flags_ref, *refs):
    blocks, refs = refs[:count], refs[count:]
    befores = ()
    if last in (1, 2):
        befores, refs = refs[: len(bands)], refs[len(bands) :]
    if last >= 2:
        refs = refs[1:]
    last = last % 3
    outs = refs[: 1 if last else len(bands)]
    fields = refs[len(outs)]
    if last:
        turn, stage, sems = refs[len(outs) + 1 :]
        out_ref = outs[0]
    cells = stage.shape[4 - 1] if last else outs[0].shape[1]

    def fill(index, part, at, length, to, group):
        start, to = by_parity(flags_ref, at), by_parity(flags_ref, to)

        def one_cell(x, _):
            for field in range(2):
                for f in range(2):
                    if index is None:
                        value = jnp.zeros((ROWS, LANES), jnp.float32)
                    elif part is None:
                        value = blocks[index][field, f, start + x].astype(jnp.float32)
                    else:
                        value = blocks[index][part, field, f, start + x].astype(jnp.float32)
                    fields[field, to + x, 2 * group + f] = value
            return 0

        lax.fori_loop(0, length, one_cell, 0, unroll=4)

    for index, part, at, length, to, group, values in plan:
        place = functools.partial(fill, index, part, at, length, to, group)
        if values is None:
            place()
        else:
            pl.when(functools.reduce(jnp.logical_or, [flags_ref[1] == value for value in values]))(place)

    def tile(before, out, k0, row0, rows, x0, slot, fresh, freqs):
        s0 = x0 + 2 * HMAX - k0 - (rows - 1)
        r0 = x0 + k0
        if fresh:
            total = [[None] * TX for _ in range(rows)]
        else:
            total = [[before[row0 + j, x0 + i] for i in range(TX)] for j in range(rows)]
        for f in range(freqs):
            for c in range(2):
                s = [fields[0, s0 + i, f, 8 * c : 8 * c + 8] for i in range(TX + rows - 1)]
                r = [fields[1, r0 + i, f, 8 * c : 8 * c + 8] for i in range(TX + rows - 1)]
                for j in range(rows):
                    for i in range(TX):
                        product = s[i + rows - 1 - j] * r[i + j]
                        total[j][i] = product if total[j][i] is None else total[j][i] + product
        for j in range(rows):
            if not last:
                for i in range(TX):
                    out[row0 + j, x0 + i] = total[j][i]
                continue
            for i in range(TX):
                turn[j, pl.ds(i, 8, stride=TX)] = 0.25 * total[j][i]
            for zh in range(2):
                for y in range(4):
                    row = zh * 4 + y
                    stage[slot, y, j, pl.ds(pl.multiple_of(x0, TX), TX), zh * LANES : (zh + 1) * LANES] = turn[
                        j, row * TX : (row + 1) * TX
                    ]

    def out_copy(k0, rows, slot):
        return pltpu.make_async_copy(stage.at[slot, :, pl.ds(0, rows)], out_ref.at[:, pl.ds(k0, rows)], sems.at[slot])

    for band, (k_first, steps, jump_at, jump, rest) in enumerate(bands):
        before = befores[band] if befores else None
        out = None if last else outs[band]

        def first_row(step):
            k0 = k_first + TH * step
            return k0 if not jump else k0 + jnp.where(step >= jump_at, jump, 0)

        def rows_of(k0, row0, rows, slot):
            def x_step(start, fresh, freqs, xt, _):
                tile(before, out, k0, row0, rows, (start + xt) * TX, slot, fresh, freqs)
                return 0

            if first == "half":
                middle = cells // TX // 2
                beside = functools.partial(x_step, by_parity(flags_ref, (0, middle)), True, 2 * groups)
                lax.fori_loop(0, middle, beside, 0)
                other = functools.partial(x_step, by_parity(flags_ref, (middle, 0)), False, 4)
                lax.fori_loop(0, middle, other, 0)
            else:
                lax.fori_loop(0, cells // TX, functools.partial(x_step, 0, first, 2 * groups), 0)

        def h_step(step, _):
            slot = lax.rem(step, SLOTS)
            if last:

                @pl.when(step >= SLOTS)
                def _():
                    out_copy(first_row(step - SLOTS), TH, slot).wait()

            rows_of(first_row(step), TH * step, TH, slot)
            if last:
                out_copy(first_row(step), TH, slot).start()
            return 0

        lax.fori_loop(0, steps, h_step, 0)
        if rest:
            slot = steps % SLOTS
            k0 = k_first + TH * steps
            if last:
                out_copy(first_row(steps - SLOTS), TH, slot).wait()
            rows_of(k0, TH * steps, rest, slot)
            if last:
                out_copy(k0, rest, slot).start()
        if last:
            for step in range(steps - SLOTS + (1 if rest else 0), steps):
                out_copy(first_row(step), TH, step % SLOTS).wait()
            if rest:
                out_copy(k_first + TH * steps, rest, steps % SLOTS).wait()


NEAR_BAND = (HMAX - NEAR, 2 * NEAR // TH, 0, 0, 1)
FAR_BAND = (0, 2 * NEAR // TH, NEAR // TH, 2 * NEAR + 1, 0)


def summed(flags, blocks, variants, bands, befores, cells, last, image=None):
    heights = [TH * band[1] + band[4] for band in bands]
    groups = max(variant[-1] for variant in variants)
    scratch = [pltpu.VMEM((2, 3 * cells, 2 * groups, ROWS, LANES), jnp.float32)]
    vmem = pl.BlockSpec(memory_space=pltpu.VMEM)
    hbm = pl.BlockSpec(memory_space=pl.ANY)
    operands = list(blocks) + list(befores)
    in_specs = [pl.BlockSpec(memory_space=pltpu.SMEM)] + [vmem] * len(operands)
    aliases = {}
    if last:
        scratch += [
            pltpu.VMEM((TH, 8 * TX, LANES), jnp.float32),
            pltpu.VMEM((SLOTS, 4, TH, cells, 2 * LANES), jnp.float32),
            pltpu.SemaphoreType.DMA((SLOTS,)),
        ]
        out_shape = jax.ShapeDtypeStruct((4, OFFSETS, cells, 2 * LANES), jnp.float32)
        out_specs = hbm
        if last == 2:
            operands.append(image)
            in_specs.append(hbm)
            aliases = {len(operands): 0}
    else:
        out_shape = [pltpu.VMEM((height, cells, 8, LANES), jnp.float32) for height in heights]
        out_specs = [vmem] * len(heights)
        if image is not None:
            operands.append(image)
            in_specs.append(vmem)
            aliases = {len(operands): 0}
    return pl.pallas_call(
        functools.partial(sum_kernel, variants, len(blocks), bands, last if image is None or last else 3),
        in_specs=in_specs,
        out_specs=out_specs,
        out_shape=out_shape,
        scratch_shapes=scratch,
        input_output_aliases=aliases,
        compiler_params=pltpu.CompilerParams(vmem_limit_bytes=32 << 20),
        cost_estimate=pl.CostEstimate(
            flops=520_000 * sum(heights), bytes_accessed=130_000 * sum(heights), transcendentals=0
        ),
        name="image" if last else "partial",
    )(flags, *operands)


def body(source_field, receiver_field):
    slabs = lax.axis_size("slab")
    middle = slabs // 2
    cells, freqs = source_field.shape[2], source_field.shape[1]
    group = lax.axis_index("freq").astype(jnp.int32)
    slab = lax.axis_index("slab")
    beyond = jnp.where((slab == 0) | (slab == slabs - 1), 2, 0)
    beyond = jnp.where((slab == middle) | (slab == middle - 1), 1, beyond)
    flags = jnp.stack([slab % 2, beyond]).astype(jnp.int32)
    parts = regrouped(group[None], source_field, receiver_field)

    def swap(part, d):
        return lax.ppermute(part, "freq", [(g, g ^ d) for g in range(GROUPS)])

    def trade(value, partner, turned=()):
        pairs = []
        for s in range(slabs):
            for g in range(GROUPS):
                pairs.append((s * GROUPS + g, partner(s) * GROUPS + (g ^ 2 if s in turned else g)))
        return lax.ppermute(value, ("slab", "freq"), pairs)

    def side_a(s):
        return s ^ 1

    def side_b(s):
        return min(max(s + 1 if s % 2 else s - 1, 0), slabs - 1)

    def side_b_of_half(s):
        return s // middle * middle + (s + 1 if s % 2 else s - 1) % middle

    one, other = swap(parts[1], 1), swap(parts[3], 1)

    whole, half = [(2, 2, freqs, length, ROWS, LANES) for length in (cells, NEAR)]
    rest = cells - NEAR
    copies = [(None, slot, None, 0, 0, slot) for slot in range(2)]
    (turned_own,) = pack(flags, (parts[2], other), copies, (whole,))
    far_own = swap(turned_own, 2)
    copies = []
    for slot in range(2):
        for out, at in ((0, 0), (1, (0, rest)), (2, (rest, 0))):
            copies.append((None, slot, None, at, out, slot))
    own, near_b, far_b = pack(flags, (parts[0], one), copies, (whole,) + (half,) * 2)
    whole_a = trade(own, side_a)
    first_near_b, first_far_b = trade(near_b, side_b_of_half), trade(far_b, side_b_of_half)
    over_middle = [(0, middle), (slabs - 1, middle - 1)]
    near_over = lax.ppermute(first_near_b, "slab", over_middle)

    copies = []
    for slot in range(2):
        for out, at in ((0, (rest, 0)), (2, (0, rest))):
            copies.append((None, 0, slot, at, out, slot))
        for out, at in ((1, (0, rest)), (3, (rest, 0))):
            copies += [(False, 0, slot, at, out, slot), (True, 1, slot, at, out, slot)]
    near_a, near_b, far_a, far_b = pack(flags, (far_own, turned_own), copies, (half,) * 4)
    turned = (middle - 1, middle)
    near_b = trade(near_b, side_b, turned)
    near_a, whole_a = lax.optimization_barrier((near_a, whole_a))
    near_a = trade(near_a, side_a)
    far_a, far_b = trade(far_a, side_a), trade(far_b, side_b, turned)

    near_at_a, near_at_b = (2 * cells, rest), (rest, 2 * cells)
    far_at_a, far_at_b = (2 * cells + NEAR, 0), (0, 2 * cells + NEAR)
    zero = (None, 0, 0, NEAR)

    def first_groups(own, whole_a, near_b, far_b, near_over, far_over, to, far):
        plan = []
        for g in range(2):
            plan += [(own, g, 0, cells, cells, to + g, None), (whole_a, g, (0, rest), NEAR, near_at_a, to + g, None)]
            plan += [(near_b, g, 0, NEAR, near_at_b, to + g, (0,)), (*zero, near_at_b, to + g, (2,))]
            if near_over is not None:
                plan += [(near_over, g, 0, NEAR, near_at_b, to + g, (1,))]
            if far:
                plan += [(whole_a, g, (rest, 0), NEAR, far_at_a, to + g, None)]
                plan += [(far_b, g, 0, NEAR, far_at_b, to + g, (0,)), (*zero, far_at_b, to + g, (2,))]
                if far_over is not None:
                    plan += [(far_over, g, 0, NEAR, far_at_b, to + g, (1,))]
        return plan

    def last_groups(own, near_a, near_b, far_a, far_b, far):
        plan = []
        for g in range(2):
            plan += [(own, g, 0, cells, cells, g, None), (near_a, g, 0, NEAR, near_at_a, g, None)]
            plan += [(near_b, g, 0, NEAR, near_at_b, g, (0, 1)), (*zero, near_at_b, g, (2,))]
            if far:
                plan += [(far_a, g, 0, NEAR, far_at_a, g, None)]
                plan += [(far_b, g, 0, NEAR, far_at_b, g, (0, 1)), (*zero, far_at_b, g, (2,))]
        return plan

    plan = first_groups(0, 1, 2, None, 3, None, 0, False)
    near_sums = summed(flags, (own, whole_a, first_near_b, near_over), ((None, plan, True, 2),), (NEAR_BAND,), (), cells, 0)
    plan = first_groups(0, 1, 2, 3, None, None, 0, True)
    blocks = (own, whole_a, first_near_b, first_far_b)
    far_sums = summed(flags, blocks, ((False, plan, True, 2),), (FAR_BAND,), (), cells, 0)
    far_over, *far_sums = lax.optimization_barrier((first_far_b, *far_sums))
    far_over = lax.ppermute(far_over, "slab", over_middle)
    plan = first_groups(0, 1, None, None, 2, None, 0, True)
    plan = [entry for entry in plan if entry[-1] != (0,)] + [(*zero, far_at_b, g, (1,)) for g in range(2)]
    far_sums = summed(
        flags, (own, whole_a, near_over), ((True, plan, True, 2),), (FAR_BAND,), (), cells, 0, far_sums[0]
    )
    plan = last_groups(0, 1, 2, None, None, False)
    image = summed(flags, (far_own, near_a, near_b), ((None, plan, False, 2),), (NEAR_BAND,), near_sums, cells, 1)
    plan = last_groups(0, 1, 2, 3, 4, True)
    crossing = plan + first_groups(5, 6, None, None, 7, 8, 2, True)
    crossing = [entry for entry in crossing if entry[0] is not None or entry[5] < 2]
    crossing = [entry for entry in crossing if entry[-1] != (0,)]
    blocks = (far_own, near_a, near_b, far_a, far_b, own, whole_a, near_over, far_over)
    variants = ((False, plan, False, 2), (True, crossing, "half", 4))
    return summed(flags, blocks, variants, (FAR_BAND,), far_sums, cells, 2, image)


def solution(mesh):
    in_specs = (P(None, "freq", "slab", None, None), P(None, "freq", "slab", None, None))
    out_specs = P("freq", None, "slab", None)
    return jax.shard_map(body, mesh=mesh, in_specs=in_specs, out_specs=out_specs, check_vma=False)
```
